32 devices in a mesh: grp: 2 (over y), ctx: 4 (over x, core), exp: 4 (over z).
Axes of the slice: x: 2, y: 2, z: 4, core: 2. Of those that a mesh axis runs over, the one named last changes fastest.
Arguments:
- queries: bfloat16 [2048, 8192], P(('grp', 'ctx'), 'exp'), parts along dimension 0, may hold values from -6.5 to 6.5
- keys: bfloat16 [2048, 512], P(('grp', 'ctx')), parts along dimension 0, may hold values from -4 to 4
- values: bfloat16 [2048, 512], P(('grp', 'ctx')), parts along dimension 0, may hold values from -6 to 6
- doc_lengths: int32 [48], P('grp'), parts along dimension 0, may hold values from 1 to 512, 1024 in all
- residual_in: bfloat16 [2048, 4096], P(('grp', 'ctx', 'exp')), parts along dimension 0, may hold values from -3 to 3
- out_weight: bfloat16 [8192, 4096], P('exp', 'ctx'), may hold values from -0.125 to 0.125
- norm_gain: float32 [4096], replicated, may hold values from 0.5 to 2
- routes: int32 [2048, 8], P(('grp', 'ctx', 'exp')), parts along dimension 0, may hold values from 0 to 127, as said below
- route_weights: float32 [2048, 8], P(('grp', 'ctx', 'exp')), parts along dimension 0, may hold values from 0.05 to 1
- gate_weight: bfloat16 [4, 4096, 1536], P('exp', None, 'ctx'), may hold values from -0.09375 to 0.09375
- up_weight: bfloat16 [4, 4096, 1536], P('exp', None, 'ctx'), may hold values from -0.09375 to 0.09375
- down_weight: bfloat16 [4, 1536, 4096], P('exp', None, 'ctx'), may hold values from -0.3125 to 0.3125
Outputs:
- attended: bfloat16 [2048, 4096], P(('grp', 'ctx', 'exp')), parts along dimension 0
- expert_sum: bfloat16 [2048, 4096], P(('grp', 'ctx', 'exp')), parts along dimension 0
The draws below stay inside these ranges and needn't reach their ends.
There are 2 independent parts, one for each index of `grp`. The reference program is written for one: setup_inputs(seed, part) draws one part's arguments, and reference() takes and returns one part's arrays. A program takes and returns all parts, laid end to end along the dimension named above; an argument that names none is the same for every part. Nothing has to cross between parts.
Inputs may be any that keep to these rules, and one draw needn't show every extreme that they name: `routes`: each row names 8 different experts. In each aligned block of 64 rows, each of the experts below 4 is named by at most 2 rows, and one of them by exactly 2 rows in every block.
All inputs are finite; a program needn't handle non-finite values.
Results may differ from the reference program's by a relative error of at most 0.018.
Values may be sent and summed in bfloat16 or wider, within the bound.
No kernel may reach another device: no remote copies, remote signals or barrier semaphores. Data moves between devices by JAX's collectives and lax.ppermute only.
A program may use at most 128 MiB of HBM per device.

```python
import math
import jax
import jax.numpy as jnp
import numpy as np
from jax import lax

D = 4096
QH = 64
KVH = 4
HD = 128
FF = 1536
EXPERTS = 128
TOP = 8
TC = 256
CAP = 2
DOCS = 24
TOKENS = 1024
TD = 64
HPG = 16
FLIGHT = 4
DOCMAX = 512
N_CTX = 4
N_EXP = 4


def draw_queries(key, part):
    key = jax.random.fold_in(key, 1)
    result = jnp.clip(jax.random.normal(key, (TOKENS, QH * HD), jnp.float32) * 1.4, -5.6, 5.6)
    return result.astype(jnp.bfloat16)


def draw_keys(key, part):
    key = jax.random.fold_in(key, 2)
    result = jnp.clip(jax.random.normal(key, (TOKENS, KVH * HD), jnp.float32), -4.0, 4.0)
    return result.astype(jnp.bfloat16)


def draw_routes(key, part):
    key = jax.random.fold_in(key, 5)
    parts_keys = jax.random.split(key, 5)
    blocks = TOKENS // TD
    wide = (FLIGHT * CAP + TD - 1) // TD
    hot = jax.random.randint(parts_keys[0], (), 0, FLIGHT)
    counts = jax.random.randint(parts_keys[1], (blocks, FLIGHT), 0, CAP + 1)
    counts = jnp.where(jnp.arange(FLIGHT, dtype=jnp.int32)[None, :] == hot, CAP, counts).astype(jnp.int32)
    ends = jnp.cumsum(counts, axis=1).astype(jnp.int32)
    begins = ends - counts
    cells = jnp.arange(TD * wide, dtype=jnp.int32)
    hit = (cells[None, :, None] >= begins[:, None, :]) & (cells[None, :, None] < ends[:, None, :])
    owner = jnp.sum(jnp.where(hit, jnp.arange(FLIGHT, dtype=jnp.int32)[None, None, :], 0), axis=2)
    owner = jnp.where(jnp.any(hit, axis=2), owner, -1).astype(jnp.int32)
    owner = jnp.transpose(owner.reshape(blocks, wide, TD), (0, 2, 1))
    orders = jax.vmap(lambda k: jax.random.permutation(k, TD))(jax.random.split(parts_keys[2], blocks))
    owner = jnp.take_along_axis(owner, orders[:, :, None].astype(jnp.int32), axis=1).reshape(TOKENS, wide)
    rest = EXPERTS - FLIGHT
    scores = jax.random.randint(parts_keys[3], (TOKENS, rest), 0, 1 << 20) * rest + jnp.arange(rest, dtype=jnp.int32)[None, :]
    others = (lax.top_k(scores, TOP)[1] + FLIGHT).astype(jnp.int32)
    front = jnp.where(owner >= 0, owner, others[:, :wide])
    picked = jnp.concatenate([front, others[:, wide:]], axis=1)
    shuffle = jax.random.randint(parts_keys[4], (TOKENS, TOP), 0, 1 << 20) * TOP + jnp.arange(TOP, dtype=jnp.int32)[None, :]
    order = lax.top_k(shuffle, TOP)[1]
    return jnp.take_along_axis(picked, order, axis=1).astype(jnp.int32)


def shard_levels(rng, dims, shards, smallest, high):
    gain = 1.0
    for position, parts in shards:
        heights = jax.random.uniform(jax.random.fold_in(jax.random.fold_in(rng, 6), position), (parts,), jnp.float32, smallest / len(shards), high / len(shards))
        gain = gain * jnp.repeat(jnp.exp(heights), dims[position] // parts).reshape((-1,) + (1,) * (len(dims) - 1 - position))
    return gain


def split_up(amount, total, limit, lean):
    weights = [(1 << 20) // math.isqrt(grade ** lean) + 1 for grade in range(2, amount + 1)]
    spare, given = total - limit - (amount - 1), [1] * (amount - 1)
    while spare > 0:
        candidates = [i for i in range(amount - 1) if given[i] < limit]
        mass, left = sum([weights[i] for i in candidates]), spare
        for i in candidates:
            extra = min(limit - given[i], max(1, left * weights[i] // mass), spare)
            given[i] = given[i] + extra
            spare = spare - extra
    return np.array([limit] + given)


def ragged(rng, count, total, limit, lean):
    if count == 2:
        one = jax.random.randint(rng, (), max(1, total - limit), min(limit, total - 1) + 1)
        return jnp.stack([one, total - one])
    sizes = jnp.asarray(split_up(count, total, limit, lean), jnp.int32)
    pairs = (count - 1) // 2
    source_of, sink = sizes[1:1 + 2 * pairs:2], sizes[2:2 + 2 * pairs:2]
    room = jnp.minimum(source_of - 1, limit - sink)
    passed = jax.random.randint(jax.random.fold_in(rng, 1), (pairs,), 0, 1 << 20) % (room + 1)
    sizes = sizes.at[1:1 + 2 * pairs:2].set(source_of - passed).at[2:2 + 2 * pairs:2].set(sink + passed)
    return sizes[jax.random.permutation(jax.random.fold_in(rng, 2), count)]


def noise(stream_key, extent, scale, most, cuts=(), held_as=jnp.bfloat16):
    drawn = scale * jax.random.normal(stream_key, extent, jnp.float32)
    if cuts:
        drawn = drawn * shard_levels(stream_key, extent, cuts, -0.22, 0.18)
    return jnp.clip(drawn, -most, most).astype(held_as)


def setup_inputs(seed: int = 0, part: int = 0) -> dict:
    key_list = jax.random.split(jax.random.key(seed), 13)
    part_keys = jax.random.split(jax.random.fold_in(key_list[12], part), 13)
    queries = draw_queries(jax.random.fold_in(jax.random.fold_in(key_list[12], part), 71), part)
    keys = draw_keys(jax.random.fold_in(jax.random.fold_in(key_list[12], part), 71), part)
    values = noise(part_keys[2], (TOKENS, KVH * HD), 1.0, 6.0, ((0, 4),))
    doc_lengths = ragged(part_keys[3], DOCS, TOKENS, DOCMAX, 2).astype(jnp.int32)
    residual_in = noise(part_keys[4], (TOKENS, D), 0.5, 3.0, ((0, 16),))
    out_weight = noise(key_list[5], (QH * HD, D), (QH * HD // 4) ** -0.5, 0.125, ((0, 4), (1, 4)))
    norm_gain = jnp.clip(jnp.exp(jax.random.uniform(key_list[6], (D,), jnp.float32, math.log(0.5), math.log(2.0))), 0.5, 2.0)
    routes = draw_routes(jax.random.fold_in(jax.random.fold_in(key_list[12], part), 71), part)
    route_weights = jnp.clip(jnp.exp(math.log(1.0) - 2.9957323 * jax.random.uniform(part_keys[8], (TOKENS, TOP), jnp.float32) ** shard_levels(part_keys[8], (TOKENS, TOP), ((0, 16),), -0.2, 0.2)), 0.05, 1.0)
    gate_weight = noise(key_list[9], (FLIGHT, D, FF), D ** -0.5, 0.09375, ((0, 4), (2, 4)))
    up_weight = noise(key_list[10], (FLIGHT, D, FF), D ** -0.5, 0.09375, ((0, 4), (2, 4)))
    down_weight = noise(key_list[11], (FLIGHT, FF, D), (FF // 4) ** -0.5, 0.3125, ((0, 4), (2, 4)))
    return dict(queries=queries, keys=keys, values=values, doc_lengths=doc_lengths, residual_in=residual_in, out_weight=out_weight, norm_gain=norm_gain, routes=routes, route_weights=route_weights, gate_weight=gate_weight, up_weight=up_weight, down_weight=down_weight)


def doc_starts(doc_lengths, positions):
    bounds = (jnp.cumsum(doc_lengths) - doc_lengths).astype(jnp.int32)
    picked = jnp.where(bounds[None, :] <= positions[:, None], bounds[None, :], 0)
    return lax.optimization_barrier(jnp.max(picked, axis=1)).astype(jnp.int32)

def slot_tables(route_rows, weight_rows, flight, capacity):
    count = route_rows.shape[0]
    top = route_rows.shape[1]
    flat = route_rows.reshape(-1)
    experts = jnp.arange(flight, dtype=jnp.int32)
    onehot = (flat[:, None] == experts[None, :]).astype(jnp.int32)
    earlier = (jnp.cumsum(onehot, axis=0) - onehot).astype(jnp.int32)
    rank = lax.optimization_barrier(jnp.sum(earlier * onehot, axis=1)).astype(jnp.int32)
    target = jnp.where(flat < flight, flat * capacity + rank, flight * capacity)
    slots = jnp.arange(flight * capacity, dtype=jnp.int32)
    chosen = (target[None, :] == slots[:, None]).reshape(flight * capacity, count, top)
    picks = lax.optimization_barrier(jnp.sum(chosen.astype(jnp.float32), axis=2))
    weights = lax.optimization_barrier(jnp.sum(jnp.where(chosen, weight_rows[None, :, :], jnp.float32(0.0)), axis=2))
    return (picks, weights)

def reference(queries, keys, values, doc_lengths, residual_in, out_weight, norm_gain, routes, route_weights, gate_weight, up_weight, down_weight):
    positions = jnp.arange(TOKENS, dtype=jnp.int32)
    starts = doc_starts(doc_lengths, positions)
    scale = 1.0 / HD ** 0.5
    group = QH // KVH
    reach = (DOCMAX + TC - 2) // TC
    span = (reach + 1) * TC

    def one_head(head):
        query_cols = lax.dynamic_slice_in_dim(queries, head * HD, HD, 1)
        kv_col = head // group * HD
        key_cols = jnp.pad(lax.dynamic_slice_in_dim(keys, kv_col, HD, 1), ((reach * TC, 0), (0, 0)))
        value_cols = jnp.pad(lax.dynamic_slice_in_dim(values, kv_col, HD, 1), ((reach * TC, 0), (0, 0)))

        def one_block(block):
            first = block * TC
            query_block = lax.dynamic_slice_in_dim(query_cols, first, TC, 0)
            key_block = lax.dynamic_slice_in_dim(key_cols, first, span, 0)
            value_block = lax.dynamic_slice_in_dim(value_cols, first, span, 0)
            query_pos = first + jnp.arange(TC, dtype=jnp.int32)
            key_pos = first - reach * TC + jnp.arange(span, dtype=jnp.int32)
            block_starts = lax.dynamic_slice_in_dim(starts, first, TC, 0)
            scores = jnp.dot(query_block, key_block.T, preferred_element_type=jnp.float32) * scale
            allowed = (key_pos[None, :] <= query_pos[:, None]) & (key_pos[None, :] >= block_starts[:, None])
            scores = jnp.where(allowed, scores, jnp.float32(-1e+30))
            best = lax.optimization_barrier(jnp.max(scores, axis=1, keepdims=True))
            probs = jnp.where(allowed, jnp.exp(scores - best), jnp.float32(0.0))
            total = lax.optimization_barrier(jnp.sum(probs, axis=1, keepdims=True))
            mixed = jnp.dot(probs.astype(jnp.bfloat16), value_block, preferred_element_type=jnp.float32)
            return (mixed / total).astype(jnp.bfloat16)
        blocks = lax.map(one_block, jnp.arange(N_CTX, dtype=jnp.int32))
        return blocks.reshape(TOKENS, HD)
    heads = lax.map(one_head, jnp.arange(QH, dtype=jnp.int32))
    heads_out = jnp.transpose(heads, (1, 0, 2)).reshape(TOKENS, QH * HD)
    width = HPG * HD

    def add_group(accum, index):
        cols = lax.dynamic_slice_in_dim(heads_out, index * width, width, 1)
        rows = lax.dynamic_slice_in_dim(out_weight, index * width, width, 0)
        part = jnp.dot(cols, rows, preferred_element_type=jnp.float32).astype(jnp.bfloat16)
        part = lax.optimization_barrier(part)
        return (accum + part.astype(jnp.float32), None)
    head_sum, unused = lax.scan(add_group, jnp.zeros((TOKENS, D), jnp.float32), jnp.arange(N_EXP, dtype=jnp.int32))
    stream = residual_in.astype(jnp.float32) + head_sum
    attended = stream.astype(jnp.bfloat16)
    normed = (stream * lax.rsqrt(lax.optimization_barrier(jnp.mean(stream * stream, axis=1, keepdims=True)) + 1e-06) * norm_gain[None, :]).astype(jnp.bfloat16)
    shares = route_weights / lax.optimization_barrier(jnp.sum(route_weights, axis=1, keepdims=True))
    blocks = TOKENS // TD
    picks, weights = jax.vmap(lambda r, w: slot_tables(r, w, FLIGHT, CAP))(routes.reshape(blocks, TD, TOP), shares.reshape(blocks, TD, TOP))
    sent = jnp.einsum('bst,btd->bsd', picks, normed.reshape(blocks, TD, D).astype(jnp.float32), precision=lax.Precision.HIGHEST).astype(jnp.bfloat16)
    per_expert = jnp.transpose(sent.reshape(blocks, FLIGHT, CAP, D), (1, 0, 2, 3)).reshape(FLIGHT, blocks * CAP, D)

    def run_expert(operands):
        rows, gate_mat, up_mat, down_mat = operands
        gate = jnp.dot(rows, gate_mat, preferred_element_type=jnp.float32)
        up = jnp.dot(rows, up_mat, preferred_element_type=jnp.float32)
        hidden = (jax.nn.silu(gate) * up).astype(jnp.bfloat16)
        return jnp.dot(hidden, down_mat, preferred_element_type=jnp.float32).astype(jnp.bfloat16)
    produced = lax.map(run_expert, (per_expert, gate_weight, up_weight, down_weight))
    back = jnp.transpose(produced.reshape(FLIGHT, blocks, CAP, D), (1, 0, 2, 3)).reshape(blocks, FLIGHT * CAP, D)
    combined = jnp.einsum('bst,bsd->btd', weights, back.astype(jnp.float32), precision=lax.Precision.HIGHEST)
    expert_sum = combined.reshape(TOKENS, D).astype(jnp.bfloat16)
    return (attended, expert_sum)
```

```python
import functools

import jax
import jax.numpy as jnp
from jax import lax
from jax.experimental import pallas as pl
from jax.experimental.pallas import tpu as pltpu
from jax.sharding import PartitionSpec as P

QH = 64
KVH = 4
HD = 128
CAP = 2
DOCMAX = 512
KEY_TILE = 128
MIB = 1024 * 1024
LOG2E = 1.4426950408889634


def swap(x, axis, mask):
    count = lax.axis_size(axis)
    return lax.ppermute(x, axis, [(i, i ^ mask) for i in range(count)])


def shift(x, axis, by):
    count = lax.axis_size(axis)
    return lax.ppermute(x, axis, [(i, i + by) for i in range(count - by)])


def reversed_bits(count):
    order = [0]
    step = 1
    while step < count:
        order = [2 * i for i in order]
        order = order + [i + 1 for i in order]
        step *= 2
    return order


def vmem(limit_mib):
    return pltpu.CompilerParams(vmem_limit_bytes=limit_mib * MIB)


def whole_vmem(count):
    return [pl.BlockSpec(memory_space=pltpu.VMEM)] * count


def slot_ranks(routes_t, flight):
    tokens = routes_t.shape[1]
    rows = [jnp.max((routes_t == j).astype(jnp.float32), axis=0, keepdims=True) for j in range(flight)]
    named = jnp.concatenate(rows, axis=0)
    before = lax.broadcasted_iota(jnp.int32, (tokens, tokens), 0) < lax.broadcasted_iota(
        jnp.int32, (tokens, tokens), 1
    )
    ranks = jnp.dot(
        named.astype(jnp.bfloat16), before.astype(jnp.bfloat16), preferred_element_type=jnp.float32
    )
    return named, ranks


def spread(rows, count, source_of):
    have = rows.shape[0]
    out_row = lax.broadcasted_iota(jnp.int32, (count, have), 0)
    col = lax.broadcasted_iota(jnp.int32, (count, have), 1)
    onehot = (col == source_of(out_row)).astype(jnp.bfloat16)
    return jnp.dot(onehot, rows.astype(jnp.bfloat16), preferred_element_type=jnp.float32)


def prep_kernel(routes_ref, weights_ref, residual_ref, rows_ref, combine_ref, *, flight):
    routes_t = routes_ref[...]
    named, ranks = slot_ranks(routes_t, flight)
    slots = flight * CAP
    slot_row = lax.broadcasted_iota(jnp.int32, (slots, 1), 0)
    named_s = spread(named, slots, lambda i: i // CAP)
    ranks_s = spread(ranks, slots, lambda i: i // CAP)
    want = (slot_row % CAP).astype(jnp.float32)
    hit = (named_s > 0.5) & (ranks_s == want)
    picks = jnp.where(hit, 1.0, 0.0).astype(jnp.bfloat16)
    rows_ref[...] = jnp.dot(picks, residual_ref[...], preferred_element_type=jnp.float32).astype(
        jnp.bfloat16
    )
    scores = weights_ref[...]
    shares = scores / jnp.sum(scores, axis=0, keepdims=True)
    parts = [
        jnp.sum(jnp.where(routes_t == j, shares, 0.0), axis=0, keepdims=True) for j in range(flight)
    ]
    for j in range(flight):
        for r in range(CAP):
            line = j * CAP + r
            combine_ref[line : line + 1, :] = jnp.where(hit[line : line + 1, :], parts[j], 0.0)


def prep(routes_t, weights_t, residual, flight):
    tokens = residual.shape[0]
    width = residual.shape[1]
    return pl.pallas_call(
        functools.partial(prep_kernel, flight=flight),
        out_shape=(
            jax.ShapeDtypeStruct((flight * CAP, width), jnp.bfloat16),
            jax.ShapeDtypeStruct((flight * CAP, tokens), jnp.float32),
        ),
        in_specs=whole_vmem(3),
        out_specs=whole_vmem(2),
        compiler_params=vmem(16),
        name="prep",
    )(routes_t, weights_t, residual)


def attention_kernel(
    lengths_ref,
    q_ref,
    kv_far_ref,
    kv_near_ref,
    kv_own_ref,
    routes_ref,
    *refs,
    heads,
    homes,
    halves,
    reach,
):
    out_refs = refs[:halves]
    routed_ref = refs[halves]
    k_all, v_all = refs[halves + 1 :]
    tokens = q_ref.shape[0]
    top = routes_ref.shape[1]
    block_tokens = tokens // homes
    sub = block_tokens // halves
    ctx_index = lax.axis_index("ctx")
    exp_index = lax.axis_index("exp")
    first = ctx_index * tokens
    for place, ref in enumerate((kv_far_ref, kv_near_ref, kv_own_ref)):
        k_all[place * tokens : (place + 1) * tokens, :] = ref[0]
        v_all[place * tokens : (place + 1) * tokens, :] = ref[1]
    order = reversed_bits(homes)
    window = reach + KEY_TILE
    docs = lengths_ref.shape[0]
    scale = LOG2E / HD**0.5

    for half in range(halves):

        @pl.loop(0, homes)
        def one_home(home):
            row0 = home * block_tokens + half * sub
            row0 = pl.multiple_of(row0, sub)
            key0 = pl.multiple_of(row0 // KEY_TILE * KEY_TILE, KEY_TILE)
            query_pos = first + row0 + lax.broadcasted_iota(jnp.int32, (sub, 1), 0)
            starts = jnp.zeros((sub, 1), jnp.int32)
            bound = jnp.int32(0)
            for i in range(docs):
                starts = jnp.where(query_pos >= bound, bound, starts)
                bound = bound + lengths_ref[i]
            key_pos = first + key0 - reach + lax.broadcasted_iota(jnp.int32, (sub, window), 1)
            allowed = (key_pos <= query_pos) & (key_pos >= starts)
            bias = jnp.where(allowed, 0.0, -1e30)
            queries = jnp.concatenate(
                [q_ref[pl.ds(row0, sub), h * HD : (h + 1) * HD] for h in range(heads)], axis=0
            )
            k = k_all[pl.ds(key0, window), :]
            v = v_all[pl.ds(key0, window), :]
            scores = lax.dot_general(
                queries, k, (((1,), (1,)), ((), ())), preferred_element_type=jnp.float32
            )
            scores = scores.reshape(heads, sub, window) * scale + bias[None]
            best = jnp.max(scores, axis=2, keepdims=True)
            probs = jnp.exp2(scores - best)
            total = jnp.sum(probs, axis=2, keepdims=True)
            mixed = jnp.dot(
                probs.reshape(heads * sub, window).astype(jnp.bfloat16),
                v,
                preferred_element_type=jnp.float32,
            )
            result = (mixed / total.reshape(heads * sub, 1)).astype(jnp.bfloat16)
            other = home ^ exp_index
            place = jnp.int32(0)
            for position in range(homes):
                place = jnp.where(other == order[position], position, place)
            at = pl.multiple_of(place * sub, sub)
            for h in range(heads):
                out_refs[half][pl.ds(at, sub), h * HD : (h + 1) * HD] = result[
                    h * sub : (h + 1) * sub
                ]

    flight = homes
    lines = flight * homes * CAP
    line = lax.broadcasted_iota(jnp.int32, (lines, 1), 0)
    line_home = line // CAP % homes
    line_slot = line % CAP
    line_place = line // (CAP * homes)
    line_expert = jnp.zeros((lines, 1), jnp.int32)
    for position in range(flight):
        line_expert = jnp.where(line_place == position, order[position] ^ exp_index, line_expert)
    routed = jnp.zeros((lines, heads * HD), jnp.float32)
    for position in range(homes):
        mask = order[position]
        named, ranks = slot_ranks(routes_ref[mask], flight)
        col = lax.broadcasted_iota(jnp.int32, (lines, flight), 1)
        onehot = (col == line_expert).astype(jnp.bfloat16)
        named_l = jnp.dot(onehot, named.astype(jnp.bfloat16), preferred_element_type=jnp.float32)
        ranks_l = jnp.dot(onehot, ranks.astype(jnp.bfloat16), preferred_element_type=jnp.float32)
        hit = (
            (named_l > 0.5)
            & (ranks_l == line_slot.astype(jnp.float32))
            & (line_home == (mask ^ exp_index))
        )
        picks = jnp.where(hit, 1.0, 0.0)
        for half in range(halves):
            routed = routed + jnp.dot(
                picks[:, half * sub : (half + 1) * sub].astype(jnp.bfloat16),
                out_refs[half][position * sub : (position + 1) * sub, :],
                preferred_element_type=jnp.float32,
            )
    routed_ref[...] = routed.astype(jnp.bfloat16)


def attention(lengths, queries, kv_far, kv_near, kv_own, routes_all, homes, halves, reach):
    tokens, width = queries.shape
    heads = width // HD
    rows = tokens // halves
    flops = 4 * heads * HD * tokens * (reach + KEY_TILE)
    return pl.pallas_call(
        functools.partial(
            attention_kernel, heads=heads, homes=homes, halves=halves, reach=reach
        ),
        out_shape=tuple(jax.ShapeDtypeStruct((rows, width), jnp.bfloat16) for _ in range(halves))
        + (jax.ShapeDtypeStruct((homes * homes * CAP, width), jnp.bfloat16),),
        in_specs=[pl.BlockSpec(memory_space=pltpu.SMEM)] + whole_vmem(5),
        out_specs=tuple(whole_vmem(halves + 1)),
        scratch_shapes=[pltpu.VMEM((3 * tokens, HD), jnp.bfloat16)] * 2,
        compiler_params=vmem(40),
        cost_estimate=pl.CostEstimate(
            flops=flops,
            bytes_accessed=4 * tokens * width,
            transcendentals=heads * tokens * (reach + KEY_TILE),
        ),
        name="attention",
    )(lengths, queries, kv_far, kv_near, kv_own, routes_all)


def hidden_kernel(*refs, count):
    row_refs = refs[:count]
    gain_ref, gate_ref, up_ref, out_ref = refs[count:]
    ctx_index = lax.axis_index("ctx")
    cols = row_refs[0].shape[1]
    rows = [ref[...].astype(jnp.float32) for ref in row_refs]
    square = sum(jnp.sum(row * row, axis=1, keepdims=True) for row in rows)
    inverse = lax.rsqrt(square / (cols * count) + 1e-06)
    gate = None
    up = None
    for place in range(count):
        at = pl.multiple_of((ctx_index ^ place) * cols, cols)
        normed = (rows[place] * inverse * gain_ref[:, pl.ds(at, cols)]).astype(jnp.bfloat16)
        gate_part = jnp.dot(normed, gate_ref[0, pl.ds(at, cols), :], preferred_element_type=jnp.float32)
        up_part = jnp.dot(normed, up_ref[0, pl.ds(at, cols), :], preferred_element_type=jnp.float32)
        gate = gate_part if gate is None else gate + gate_part
        up = up_part if up is None else up + up_part
    out_ref[...] = (gate / (1.0 + jnp.exp(-gate)) * up).astype(jnp.bfloat16)


def hidden_units(pieces, gain, gate_weight, up_weight):
    count = len(pieces)
    rows = pieces[0].shape[0]
    units = gate_weight.shape[2]
    return pl.pallas_call(
        functools.partial(hidden_kernel, count=count),
        out_shape=jax.ShapeDtypeStruct((rows, units), jnp.bfloat16),
        in_specs=whole_vmem(count + 3),
        out_specs=pl.BlockSpec(memory_space=pltpu.VMEM),
        compiler_params=vmem(20),
        name="hidden_units",
    )(*pieces, gain, gate_weight, up_weight)


def down_kernel(*refs, count):
    piece_refs = refs[:count]
    down_ref, out_ref = refs[count:]
    ctx_index = lax.axis_index("ctx")
    units = piece_refs[0].shape[1]
    total = None
    for place in range(count):
        at = pl.multiple_of((ctx_index ^ place) * units, units)
        part = jnp.dot(
            piece_refs[place][...], down_ref[0, pl.ds(at, units), :], preferred_element_type=jnp.float32
        )
        total = part if total is None else total + part
    out_ref[...] = total.astype(jnp.bfloat16)


def down_product(pieces, down_weight):
    count = len(pieces)
    rows = pieces[0].shape[0]
    return pl.pallas_call(
        functools.partial(down_kernel, count=count),
        out_shape=jax.ShapeDtypeStruct((rows, down_weight.shape[2]), jnp.bfloat16),
        in_specs=whole_vmem(count + 1),
        out_specs=pl.BlockSpec(memory_space=pltpu.VMEM),
        compiler_params=vmem(20),
        name="down_product",
    )(*pieces, down_weight)


def attended_kernel(*refs, count):
    piece_refs = refs[:count]
    residual_ref, out_ref = refs[count:]
    ctx_index = lax.axis_index("ctx")
    cols = piece_refs[0].shape[1]
    for place in range(count):
        at = pl.multiple_of((ctx_index ^ place) * cols, cols)
        total = residual_ref[:, pl.ds(at, cols)].astype(jnp.float32) + piece_refs[place][...].astype(
            jnp.float32
        )
        out_ref[:, pl.ds(at, cols)] = total.astype(jnp.bfloat16)


def attended_rows(pieces, residual):
    count = len(pieces)
    return pl.pallas_call(
        functools.partial(attended_kernel, count=count),
        out_shape=jax.ShapeDtypeStruct(residual.shape, jnp.bfloat16),
        in_specs=whole_vmem(count + 1),
        out_specs=pl.BlockSpec(memory_space=pltpu.VMEM),
        compiler_params=vmem(20),
        name="attended_rows",
    )(*pieces, residual)


def gather_pieces(x, axis):
    count = lax.axis_size(axis)
    found = {0: x}
    step = count // 2
    while step >= 1:
        keys = sorted(found)
        if len(keys) == 1:
            moved = [swap(found[0], axis, step)]
        else:
            packed = swap(jnp.stack([found[k] for k in keys]), axis, step)
            moved = [packed[i] for i in range(len(keys))]
        for k, piece in zip(keys, moved):
            found[k ^ step] = piece
        step //= 2
    return [found[k] for k in range(count)]


def sum_over_exp(part):
    step = 1
    total = part
    while total.shape[0] > 1:
        half = total.shape[0] // 2
        arrived = swap(total[half:].astype(jnp.bfloat16), "exp", step)
        total = total[:half].astype(jnp.float32) + arrived.astype(jnp.float32)
        step *= 2
    return total[0]


def shards(
    queries,
    keys,
    values,
    doc_lengths,
    residual_in,
    out_weight,
    norm_gain,
    routes,
    route_weights,
    gate_weight,
    up_weight,
    down_weight,
):
    tokens = queries.shape[0]
    local_heads = queries.shape[1] // HD
    n_ctx = lax.axis_size("ctx")
    homes = lax.axis_size("exp")
    flight = gate_weight.shape[0] * homes
    ctx_index = lax.axis_index("ctx")
    exp_index = lax.axis_index("exp")
    block_tokens = residual_in.shape[0]
    width = residual_in.shape[1]
    cols = out_weight.shape[1]
    halves = 2 if block_tokens % 32 == 0 else 1
    sub = block_tokens // halves
    reach = DOCMAX

    kv_head = exp_index * local_heads // (QH // KVH)
    kv_own = jnp.stack(
        [
            lax.dynamic_slice_in_dim(keys, kv_head * HD, HD, 1),
            lax.dynamic_slice_in_dim(values, kv_head * HD, HD, 1),
        ]
    )
    kv_near = shift(kv_own, "ctx", 1)
    kv_far = shift(kv_own, "ctx", 2)
    routes_t = routes.T
    routes_all = jnp.stack(gather_pieces(routes_t, "exp"))
    rows_own, combine = prep(routes_t, route_weights.T, residual_in, flight)
    residual_rows = gather_pieces(rows_own, "ctx")

    *heads_out, routed = attention(
        doc_lengths, queries, kv_far, kv_near, kv_own, routes_all, homes, halves, reach
    )

    def project(rows):
        return jnp.dot(rows, out_weight, preferred_element_type=jnp.float32).astype(jnp.bfloat16)

    routed_pieces = gather_pieces(routed, "ctx")
    order = reversed_bits(homes)
    lines = flight * homes * CAP
    line = jnp.arange(lines, dtype=jnp.int32)
    expert = jnp.asarray(order, jnp.int32)[line // (CAP * homes)] ^ exp_index
    source = jnp.where(line // CAP % homes == exp_index, expert * CAP + line % CAP, -1)
    place_rows = (source[:, None] == jnp.arange(flight * CAP, dtype=jnp.int32)[None, :]).astype(
        jnp.bfloat16
    )
    routed_all = jnp.stack(routed_pieces)
    own_cols = [
        lax.dynamic_slice_in_dim(rows, ctx_index * cols, cols, 1) for rows in residual_rows
    ]
    extra = jnp.einsum(
        "ls,csd->cld", place_rows, jnp.stack(own_cols), preferred_element_type=jnp.float32
    )
    routed_part = (
        jnp.einsum("cld,dn->cln", routed_all, out_weight, preferred_element_type=jnp.float32) + extra
    ).astype(jnp.bfloat16)
    routed_part = jnp.transpose(
        routed_part.reshape(n_ctx, flight, homes * CAP, cols), (1, 0, 2, 3)
    )
    routed_sum = sum_over_exp(routed_part).astype(jnp.bfloat16)
    absolute = jnp.stack(
        [lax.dynamic_index_in_dim(routed_sum, ctx_index ^ k, 0, keepdims=False) for k in range(n_ctx)]
    )
    stream_rows = gather_pieces(absolute.reshape(-1, cols), "ctx")
    hidden = hidden_units(stream_rows, norm_gain[None, :], gate_weight, up_weight)
    produced = down_product(gather_pieces(hidden, "ctx"), down_weight)
    back = lax.all_to_all(
        produced.reshape(n_ctx * homes, CAP, cols),
        ("ctx", "exp"),
        split_axis=0,
        concat_axis=0,
        tiled=True,
    )
    back = jnp.transpose(back.reshape(n_ctx, flight * CAP, cols), (1, 0, 2)).reshape(
        flight * CAP, width
    )
    combined = jnp.dot(combine.T, back.astype(jnp.float32), precision=lax.Precision.HIGHEST)

    near = [swap(rows, "ctx", 1) for rows in heads_out]
    far = []
    for rows in heads_out:
        found = {0: rows}
        step = n_ctx // 2
        while step >= 2:
            for k in sorted(found):
                found[k ^ step] = swap(found[k], "ctx", step)
            step //= 2
        for k in sorted(found):
            found[k ^ 1] = swap(found[k], "ctx", 1) if k else None
        far.append(found)

    def reduced(blocks):
        part = project(jnp.concatenate(blocks, axis=0))
        part = part.reshape(len(blocks), homes, sub, cols)
        return sum_over_exp(jnp.transpose(part, (1, 0, 2, 3)))

    first = reduced(heads_out + near).astype(jnp.bfloat16)
    pieces = {0: list(first[:halves]), 1: list(first[halves:])}
    for half in range(halves):
        keys_far = [k for k in sorted(far[half]) if k > 1]
        got = reduced([far[half][k] for k in keys_far]).astype(jnp.bfloat16)
        for i, k in enumerate(keys_far):
            pieces.setdefault(k, []).append(got[i])
    returned = [jnp.concatenate(pieces[0], axis=0)]
    for k in range(1, n_ctx):
        returned.append(
            jnp.concatenate([swap(piece, "ctx", k) for piece in pieces[k]], axis=0)
        )
    attended = attended_rows(returned, residual_in)
    return (attended, combined.astype(jnp.bfloat16))


def solution(mesh):
    placed = (
        P(("grp", "ctx"), "exp"),
        P(("grp", "ctx"), None),
        P(("grp", "ctx"), None),
        P("grp"),
        P(("grp", "ctx", "exp"), None),
        P("exp", "ctx"),
        P(),
        P(("grp", "ctx", "exp"), None),
        P(("grp", "ctx", "exp"), None),
        P("exp", None, "ctx"),
        P("exp", None, "ctx"),
        P("exp", None, "ctx"),
    )
    return jax.shard_map(
        shards,
        mesh=mesh,
        in_specs=placed,
        out_specs=(P(("grp", "ctx", "exp"), None), P(("grp", "ctx", "exp"), None)),
        check_vma=False,
    )
```

```python
import functools

import jax
import jax.numpy as jnp
from jax import lax
from jax.experimental import pallas as pl
from jax.experimental.pallas import tpu as pltpu
from jax.sharding import PartitionSpec as P

QH = 64
KVH = 4
HD = 128
CAP = 2
DOCMAX = 512
KEY_TILE = 128
MIB = 1024 * 1024
LOG2E = 1.4426950408889634


def swap(x, axis, mask):
    count = lax.axis_size(axis)
    return lax.ppermute(x, axis, [(i, i ^ mask) for i in range(count)])


def shift(x, axis, by):
    count = lax.axis_size(axis)
    return lax.ppermute(x, axis, [(i, i + by) for i in range(count - by)])


def reversed_bits(count):
    order = [0]
    step = 1
    while step < count:
        order = [2 * i for i in order]
        order = order + [i + 1 for i in order]
        step *= 2
    return order


def vmem(limit_mib):
    return pltpu.CompilerParams(vmem_limit_bytes=limit_mib * MIB)


def whole_vmem(count):
    return [pl.BlockSpec(memory_space=pltpu.VMEM)] * count


def anywhere(count):
    return [pl.BlockSpec(memory_space=pl.ANY)] * count


FREE = pl.CostEstimate(flops=0, bytes_accessed=0, transcendentals=0)


def slot_ranks(routes_t, flight):
    tokens = routes_t.shape[1]
    rows = [jnp.max((routes_t == j).astype(jnp.float32), axis=0, keepdims=True) for j in range(flight)]
    named = jnp.concatenate(rows, axis=0)
    before = lax.broadcasted_iota(jnp.int32, (tokens, tokens), 0) < lax.broadcasted_iota(
        jnp.int32, (tokens, tokens), 1
    )
    ranks = jnp.dot(
        named.astype(jnp.bfloat16), before.astype(jnp.bfloat16), preferred_element_type=jnp.float32
    )
    return named, ranks


def spread(rows, count, source_of):
    have = rows.shape[0]
    out_row = lax.broadcasted_iota(jnp.int32, (count, have), 0)
    col = lax.broadcasted_iota(jnp.int32, (count, have), 1)
    onehot = (col == source_of(out_row)).astype(jnp.bfloat16)
    return jnp.dot(onehot, rows.astype(jnp.bfloat16), preferred_element_type=jnp.float32)


def attention_kernel(
    lengths_ref,
    q_ref,
    kv_far_ref,
    kv_near_ref,
    kv_own_ref,
    out_ref,
    k_all,
    v_all,
    *,
    heads,
    homes,
    half,
    sub,
):
    tokens = q_ref.shape[0]
    block_tokens = tokens // homes
    first = lax.axis_index("ctx") * tokens
    exp_index = lax.axis_index("exp")
    for place, ref in enumerate((kv_far_ref, kv_near_ref, kv_own_ref)):
        k_all[place * tokens : (place + 1) * tokens, :] = ref[0]
        v_all[place * tokens : (place + 1) * tokens, :] = ref[1]
    order = reversed_bits(homes)
    reach = DOCMAX
    window = reach + KEY_TILE
    docs = lengths_ref.shape[0]
    scale = LOG2E / HD**0.5

    @pl.loop(0, homes)
    def one_home(home):
        row0 = pl.multiple_of(home * block_tokens + half * sub, sub)
        key0 = pl.multiple_of(row0 // KEY_TILE * KEY_TILE, KEY_TILE)
        query_pos = first + row0 + lax.broadcasted_iota(jnp.int32, (sub, 1), 0)
        starts = jnp.zeros((sub, 1), jnp.int32)
        bound = jnp.int32(0)
        for i in range(docs):
            starts = jnp.where(query_pos >= bound, bound, starts)
            bound = bound + lengths_ref[i]
        key_pos = first + key0 - reach + lax.broadcasted_iota(jnp.int32, (sub, window), 1)
        allowed = (key_pos <= query_pos) & (key_pos >= starts)
        bias = jnp.where(allowed, 0.0, -1e30)
        queries = jnp.concatenate(
            [q_ref[pl.ds(row0, sub), h * HD : (h + 1) * HD] for h in range(heads)], axis=0
        )
        k = k_all[pl.ds(key0, window), :]
        v = v_all[pl.ds(key0, window), :]
        scores = lax.dot_general(
            queries, k, (((1,), (1,)), ((), ())), preferred_element_type=jnp.float32
        )
        scores = scores.reshape(heads, sub, window) * scale + bias[None]
        best = jnp.max(scores, axis=2, keepdims=True)
        probs = jnp.exp2(scores - best)
        total = jnp.sum(probs, axis=2, keepdims=True)
        mixed = jnp.dot(
            probs.reshape(heads * sub, window).astype(jnp.bfloat16),
            v,
            preferred_element_type=jnp.float32,
        )
        result = (mixed / total.reshape(heads * sub, 1)).astype(jnp.bfloat16)
        other = home ^ exp_index
        place = jnp.int32(0)
        for position in range(homes):
            place = jnp.where(other == order[position], position, place)
        at = pl.multiple_of(place * sub, sub)
        for h in range(heads):
            out_ref[pl.ds(at, sub), h * HD : (h + 1) * HD] = result[h * sub : (h + 1) * sub]


def attention(lengths, queries, kv_far, kv_near, kv_own, homes, half, sub):
    tokens, width = queries.shape
    return pl.pallas_call(
        functools.partial(
            attention_kernel, heads=width // HD, homes=homes, half=half, sub=sub
        ),
        out_shape=jax.ShapeDtypeStruct((homes * sub, width), jnp.bfloat16),
        in_specs=[pl.BlockSpec(memory_space=pltpu.SMEM)] + whole_vmem(4),
        out_specs=pl.BlockSpec(memory_space=pltpu.VMEM),
        scratch_shapes=[pltpu.VMEM((3 * tokens, HD), jnp.bfloat16)] * 2,
        compiler_params=vmem(24),
        cost_estimate=FREE,
        name="attention_" + str(half),
    )(lengths, queries, kv_far, kv_near, kv_own)


def pick_kernel(residual_ref, *refs, homes, halves, sub):
    routes_refs = refs[:homes]
    heads_refs = refs[homes : homes + halves]
    out_ref = refs[-1]
    exp_index = lax.axis_index("exp")
    order = reversed_bits(homes)
    width = heads_refs[0].shape[1]
    flight = homes
    lines = flight * homes * CAP
    line = lax.broadcasted_iota(jnp.int32, (lines, 1), 0)
    line_home = line // CAP % homes
    line_slot = (line % CAP).astype(jnp.float32)
    line_place = line // (CAP * homes)
    line_expert = jnp.zeros((lines, 1), jnp.int32)
    for position in range(flight):
        line_expert = jnp.where(line_place == position, order[position] ^ exp_index, line_expert)
    col = lax.broadcasted_iota(jnp.int32, (lines, flight), 1)
    onehot = (col == line_expert).astype(jnp.bfloat16)
    routed = jnp.zeros((lines, width), jnp.float32)
    for position in range(homes):
        mask = order[position]
        named, ranks = slot_ranks(routes_refs[mask][...], flight)
        named_l = jnp.dot(onehot, named.astype(jnp.bfloat16), preferred_element_type=jnp.float32)
        ranks_l = jnp.dot(onehot, ranks.astype(jnp.bfloat16), preferred_element_type=jnp.float32)
        hit = (named_l > 0.5) & (ranks_l == line_slot) & (line_home == (mask ^ exp_index))
        picks = jnp.where(hit, 1.0, 0.0)
        for half in range(halves):
            routed = routed + jnp.dot(
                picks[:, half * sub : (half + 1) * sub].astype(jnp.bfloat16),
                heads_refs[half][position * sub : (position + 1) * sub, :],
                preferred_element_type=jnp.float32,
            )
    out_ref[:lines, :] = routed.astype(jnp.bfloat16)
    slots = flight * CAP
    named, ranks = slot_ranks(routes_refs[0][...], flight)
    slot = lax.broadcasted_iota(jnp.int32, (slots, 1), 0)
    named_s = spread(named, slots, lambda i: i // CAP)
    ranks_s = spread(ranks, slots, lambda i: i // CAP)
    hit = (named_s > 0.5) & (ranks_s == (slot % CAP).astype(jnp.float32))
    rows = jnp.dot(
        jnp.where(hit, 1.0, 0.0).astype(jnp.bfloat16),
        residual_ref[...],
        preferred_element_type=jnp.float32,
    )
    parts = residual_ref.shape[1] // width
    rows = jnp.concatenate([rows[:, i * width : (i + 1) * width] for i in range(parts)], axis=0)
    out_ref[lines:, :] = rows.astype(jnp.bfloat16)


def pick(residual, routes_pieces, heads_out, sub):
    homes = len(routes_pieces)
    width = heads_out[0].shape[1]
    rows = homes * homes * CAP + homes * CAP * (residual.shape[1] // width)
    return pl.pallas_call(
        functools.partial(pick_kernel, homes=homes, halves=len(heads_out), sub=sub),
        out_shape=jax.ShapeDtypeStruct((rows, width), jnp.bfloat16),
        in_specs=whole_vmem(1 + homes + len(heads_out)),
        out_specs=pl.BlockSpec(memory_space=pltpu.VMEM),
        compiler_params=vmem(16),
        cost_estimate=FREE,
        name="pick",
    )(residual, *routes_pieces, *heads_out)


def routed_kernel(*refs, count, homes, after):
    piece_refs = refs[:count]
    weight_ref = refs[count]
    keep_ref, send_ref = refs[count + 1 + after :]
    ctx_index = lax.axis_index("ctx")
    exp_index = lax.axis_index("exp")
    order = reversed_bits(homes)
    cols = weight_ref.shape[1]
    depth = weight_ref.shape[0]
    flight = homes
    slots = flight * CAP
    lines = flight * homes * CAP
    half = lines // 2
    line = lax.broadcasted_iota(jnp.int32, (lines, slots), 0)
    line_place = line // (CAP * homes)
    expert = jnp.zeros((lines, slots), jnp.int32)
    for position in range(flight):
        expert = jnp.where(line_place == position, order[position] ^ exp_index, expert)
    source = jnp.where(line // CAP % homes == exp_index, expert * CAP + line % CAP, -1)
    onehot = (source == lax.broadcasted_iota(jnp.int32, (lines, slots), 1)).astype(jnp.bfloat16)
    heads = jnp.concatenate([ref[:lines, :] for ref in piece_refs], axis=0)
    product = jnp.dot(heads, weight_ref[...], preferred_element_type=jnp.float32)
    first_col = ctx_index * cols
    column = pl.multiple_of(first_col % depth, HD)
    row = pl.multiple_of(lines + first_col // depth * slots, slots)
    for place in range(count):
        extra = jnp.dot(
            onehot,
            piece_refs[place][pl.ds(row, slots), pl.ds(column, cols)],
            preferred_element_type=jnp.float32,
        )
        total = product[place * lines : (place + 1) * lines] + extra
        keep_ref[ctx_index ^ place] = total[:half].astype(jnp.bfloat16)
        send_ref[ctx_index ^ place] = total[half:].astype(jnp.bfloat16)


def routed_product(pieces, out_weight, homes, after=()):
    count = len(pieces)
    cols = out_weight.shape[1]
    shape = jax.ShapeDtypeStruct((count, homes * homes * CAP // 2, cols), jnp.bfloat16)
    return pl.pallas_call(
        functools.partial(routed_kernel, count=count, homes=homes, after=len(after)),
        out_shape=(shape, shape),
        in_specs=whole_vmem(count + 1) + anywhere(len(after)),
        out_specs=tuple(whole_vmem(2)),
        compiler_params=vmem(32),
        cost_estimate=FREE,
        name="routed_product",
    )(*pieces, out_weight, *after)


def add_middle_kernel(keep_ref, arrived_ref, *refs, last):
    total = keep_ref[...].astype(jnp.float32) + arrived_ref[...].astype(jnp.float32)
    count, rows, cols = total.shape
    if last:
        refs[0][...] = total.reshape(count * rows, cols).astype(refs[0].dtype)
    else:
        refs[0][...] = total[:, : rows // 2].astype(refs[0].dtype)
        refs[1][...] = total[:, rows // 2 :].astype(refs[1].dtype)


def add_middle(keep, arrived, last):
    count, rows, cols = keep.shape
    if last:
        out = jax.ShapeDtypeStruct((count * rows, cols), jnp.bfloat16)
    else:
        out = (
            jax.ShapeDtypeStruct((count, rows // 2, cols), jnp.float32),
            jax.ShapeDtypeStruct((count, rows // 2, cols), jnp.bfloat16),
        )
    return pl.pallas_call(
        functools.partial(add_middle_kernel, last=last),
        out_shape=out,
        in_specs=whole_vmem(2),
        out_specs=whole_vmem(1)[0] if last else tuple(whole_vmem(2)),
        compiler_params=vmem(16),
        cost_estimate=FREE,
        name="routed_sum",
    )(keep, arrived)


def project_kernel(*refs, count, homes, sub, upper, after):
    piece_refs = refs[:count]
    weight_ref = refs[count]
    out_ref = refs[-1]
    half = homes // 2
    begin = half * sub if upper else 0
    weight = weight_ref[...]
    for i in range(0, count, 2):
        pair = piece_refs[i : i + 2]
        rows = jnp.concatenate([ref[begin : begin + half * sub, :] for ref in pair], axis=0)
        product = jnp.dot(rows, weight, preferred_element_type=jnp.float32).astype(jnp.bfloat16)
        for k in range(len(pair)):
            for place in range(half):
                at = (place * count + i + k) * sub
                source = (k * half + place) * sub
                out_ref[at : at + sub, :] = product[source : source + sub]


def project(pieces, out_weight, homes, sub, upper, after=()):
    count = len(pieces)
    return pl.pallas_call(
        functools.partial(
            project_kernel, count=count, homes=homes, sub=sub, upper=upper, after=len(after)
        ),
        out_shape=jax.ShapeDtypeStruct(
            (homes // 2 * count * sub, out_weight.shape[1]), jnp.bfloat16
        ),
        in_specs=whole_vmem(count + 1) + anywhere(len(after)),
        out_specs=pl.BlockSpec(memory_space=pltpu.VMEM),
        compiler_params=vmem(32),
        cost_estimate=FREE,
        name="project_leave" if upper else "project_stay",
    )(*pieces, out_weight, *after)


def add_kernel(keep_ref, arrived_ref, *refs):
    rows = keep_ref.shape[0] // len(refs)
    for i, ref in enumerate(refs):
        part = slice(i * rows, (i + 1) * rows)
        total = keep_ref[part, :].astype(jnp.float32) + arrived_ref[part, :].astype(jnp.float32)
        ref[...] = total.astype(ref.dtype)


def add(keep, arrived, dtypes):
    rows, cols = keep.shape
    count = len(dtypes)
    out = tuple(jax.ShapeDtypeStruct((rows // count, cols), dtype) for dtype in dtypes)
    return pl.pallas_call(
        add_kernel,
        out_shape=out,
        in_specs=whole_vmem(2),
        out_specs=tuple(whole_vmem(count)),
        compiler_params=vmem(16),
        cost_estimate=FREE,
        name="add",
    )(keep, arrived)


def hidden_kernel(*refs, count):
    row_refs = refs[:count]
    gain_ref, gate_ref, up_ref = refs[count : count + 3]
    out_ref = refs[-1]
    ctx_index = lax.axis_index("ctx")
    cols = row_refs[0].shape[1]
    rows = [ref[...].astype(jnp.float32) for ref in row_refs]
    square = sum(jnp.sum(row * row, axis=1, keepdims=True) for row in rows)
    inverse = lax.rsqrt(square / (cols * count) + 1e-06)
    gate = None
    up = None
    for place in range(count):
        at = pl.multiple_of((ctx_index ^ place) * cols, cols)
        normed = (rows[place] * inverse * gain_ref[:, pl.ds(at, cols)]).astype(jnp.bfloat16)
        gate_part = jnp.dot(normed, gate_ref[0, pl.ds(at, cols), :], preferred_element_type=jnp.float32)
        up_part = jnp.dot(normed, up_ref[0, pl.ds(at, cols), :], preferred_element_type=jnp.float32)
        gate = gate_part if gate is None else gate + gate_part
        up = up_part if up is None else up + up_part
    out_ref[...] = (gate / (1.0 + jnp.exp(-gate)) * up).astype(jnp.bfloat16)


def hidden_units(pieces, gain, gate_weight, up_weight, after=()):
    count = len(pieces)
    rows = pieces[0].shape[0]
    units = gate_weight.shape[2]
    return pl.pallas_call(
        functools.partial(hidden_kernel, count=count),
        out_shape=jax.ShapeDtypeStruct((rows, units), jnp.bfloat16),
        in_specs=whole_vmem(count + 3) + anywhere(len(after)),
        out_specs=pl.BlockSpec(memory_space=pltpu.VMEM),
        compiler_params=vmem(20),
        cost_estimate=FREE,
        name="hidden_units",
    )(*pieces, gain, gate_weight, up_weight, *after)


def down_kernel(*refs, count):
    piece_refs = refs[:count]
    down_ref = refs[count]
    out_ref = refs[-1]
    ctx_index = lax.axis_index("ctx")
    units = piece_refs[0].shape[1]
    total = None
    for place in range(count):
        at = pl.multiple_of((ctx_index ^ place) * units, units)
        part = jnp.dot(
            piece_refs[place][...], down_ref[0, pl.ds(at, units), :], preferred_element_type=jnp.float32
        )
        total = part if total is None else total + part
    out_ref[...] = total.astype(jnp.bfloat16)


def down_product(pieces, down_weight, after=()):
    count = len(pieces)
    rows = pieces[0].shape[0]
    return pl.pallas_call(
        functools.partial(down_kernel, count=count),
        out_shape=jax.ShapeDtypeStruct((rows, down_weight.shape[2]), jnp.bfloat16),
        in_specs=whole_vmem(count + 1) + anywhere(len(after)),
        out_specs=pl.BlockSpec(memory_space=pltpu.VMEM),
        compiler_params=vmem(20),
        cost_estimate=FREE,
        name="down_product",
    )(*pieces, down_weight, *after)


def attended_kernel(*refs, places):
    residual_ref = refs[len(places)]
    out_ref = refs[-1]
    ctx_index = lax.axis_index("ctx")
    for (place, row0), ref in zip(places, refs):
        rows, cols = ref.shape
        at = pl.multiple_of((ctx_index ^ place) * cols, cols)
        total = residual_ref[row0 : row0 + rows, pl.ds(at, cols)].astype(jnp.float32)
        total = total + ref[...].astype(jnp.float32)
        out_ref[row0 : row0 + rows, pl.ds(at, cols)] = total.astype(jnp.bfloat16)


def attended_rows(pieces, places, residual):
    return pl.pallas_call(
        functools.partial(attended_kernel, places=places),
        out_shape=jax.ShapeDtypeStruct(residual.shape, jnp.bfloat16),
        in_specs=whole_vmem(len(pieces) + 1),
        out_specs=pl.BlockSpec(memory_space=pltpu.VMEM),
        compiler_params=vmem(20),
        cost_estimate=FREE,
        name="attended_rows",
    )(*pieces, residual)


def combine_kernel(routes_ref, weights_ref, *refs, flight, count):
    back_refs = refs[:count]
    out_ref = refs[-1]
    routes_t = routes_ref[...]
    scores = weights_ref[...]
    shares = scores / jnp.sum(scores, axis=0, keepdims=True)
    named, ranks = slot_ranks(routes_t, flight)
    lines = []
    for j in range(flight):
        share = jnp.sum(jnp.where(routes_t == j, shares, 0.0), axis=0, keepdims=True)
        for r in range(CAP):
            lines.append(jnp.where(ranks[j : j + 1] == r, share, 0.0))
    lines = jnp.concatenate(lines, axis=0)
    cols = back_refs[0].shape[1]
    for place, ref in enumerate(back_refs):
        out_ref[:, place * cols : (place + 1) * cols] = lax.dot_general(
            lines,
            ref[...].astype(jnp.float32),
            (((0,), (0,)), ((), ())),
            precision=lax.Precision.HIGHEST,
            preferred_element_type=jnp.float32,
        ).astype(jnp.bfloat16)


def gather_pieces(x, axis):
    count = lax.axis_size(axis)
    found = {0: x}
    step = count // 2
    while step >= 1:
        keys = sorted(found)
        if len(keys) == 1:
            moved = [swap(found[0], axis, step)]
        else:
            packed = swap(jnp.stack([found[k] for k in keys]), axis, step)
            moved = [packed[i] for i in range(len(keys))]
        for k, piece in zip(keys, moved):
            found[k ^ step] = piece
        step //= 2
    return [found[k] for k in range(count)]


def gather_direct(x, axis):
    return [x] + [swap(x, axis, k) for k in range(1, lax.axis_size(axis))]


def sum_over_exp(keep, send, kinds):
    count = lax.axis_size("exp")
    step = 1
    while True:
        arrived = swap(send, "exp", step)
        step *= 2
        if step >= count:
            return add(keep, arrived, kinds)
        keep, send = add(keep, arrived, (jnp.float32, jnp.bfloat16))


def routed_over_exp(keep, send):
    count = lax.axis_size("exp")
    step = 1
    while True:
        arrived = swap(send, "exp", step)
        step *= 2
        if step >= count:
            return add_middle(keep, arrived, True)
        keep, send = add_middle(keep, arrived, False)


def shards(
    queries,
    keys,
    values,
    doc_lengths,
    residual_in,
    out_weight,
    norm_gain,
    routes,
    route_weights,
    gate_weight,
    up_weight,
    down_weight,
):
    tokens = queries.shape[0]
    local_heads = queries.shape[1] // HD
    n_ctx = lax.axis_size("ctx")
    homes = lax.axis_size("exp")
    flight = gate_weight.shape[0] * homes
    ctx_index = lax.axis_index("ctx")
    exp_index = lax.axis_index("exp")
    block_tokens = residual_in.shape[0]
    width = residual_in.shape[1]
    cols = out_weight.shape[1]
    halves = 2 if block_tokens % 32 == 0 else 1
    sub = block_tokens // halves
    kinds = jnp.bfloat16

    routes_t = routes.T
    routes_pieces = gather_pieces(routes_t, "exp")
    kv_head = exp_index * local_heads // (QH // KVH)
    kv_own = jnp.stack(
        [
            lax.dynamic_slice_in_dim(keys, kv_head * HD, HD, 1),
            lax.dynamic_slice_in_dim(values, kv_head * HD, HD, 1),
        ]
    )
    kv_near = shift(kv_own, "ctx", 1)
    kv_far = shift(kv_own, "ctx", 2)
    heads_out = [
        attention(doc_lengths, queries, kv_far, kv_near, kv_own, homes, half, sub)
        for half in range(halves)
    ]
    near = [swap(rows, "ctx", 1) for rows in heads_out]
    routed = pick(residual_in, routes_pieces, heads_out, sub)
    routed_pieces = gather_pieces(routed, "ctx")

    far = []
    for rows in heads_out:
        found = {0: rows}
        step = n_ctx // 2
        while step >= 2:
            for k in sorted(found):
                found[k ^ step] = swap(found[k], "ctx", step)
            step //= 2
        for k in sorted(found):
            if k:
                found[k ^ 1] = swap(found[k], "ctx", 1)
        far.append({k: found[k] for k in sorted(found) if k})

    both = heads_out + near
    send = project(both, out_weight, homes, sub, True)
    keep = project(both, out_weight, homes, sub, False)
    own_sum, near_sum = sum_over_exp(keep, send, (kinds, kinds))
    parts = [own_sum, swap(near_sum, "ctx", 1)]
    places = [(0, 0), (1, 0)]

    keep, send = routed_product(routed_pieces, out_weight, homes)
    routed_rows = routed_over_exp(keep, send)
    stream_rows = gather_direct(routed_rows, "ctx")
    hidden = hidden_units(stream_rows, norm_gain[None, :], gate_weight, up_weight)

    for half in range(halves):
        names = sorted(far[half])
        blocks = [far[half][k] for k in names]
        send = project(blocks, out_weight, homes, sub, True)
        keep = project(blocks, out_weight, homes, sub, False)
        sums = sum_over_exp(keep, send, (kinds,) * len(names))
        for k, piece in zip(names, sums):
            parts.append(swap(piece, "ctx", k))
            places.append((k, half * sub))

    produced = down_product(gather_direct(hidden, "ctx"), down_weight)
    back = lax.all_to_all(
        produced.reshape(n_ctx * homes, CAP, cols),
        ("ctx", "exp"),
        split_axis=0,
        concat_axis=0,
        tiled=True,
    ).reshape(n_ctx, flight * CAP, cols)
    combined = pl.pallas_call(
        functools.partial(combine_kernel, flight=flight, count=n_ctx),
        out_shape=jax.ShapeDtypeStruct((block_tokens, width), jnp.bfloat16),
        in_specs=whole_vmem(2 + n_ctx),
        out_specs=pl.BlockSpec(memory_space=pltpu.VMEM),
        compiler_params=vmem(20),
        cost_estimate=FREE,
        name="combine",
    )(routes_t, route_weights.T, *[back[i] for i in range(n_ctx)])
    attended = attended_rows(parts, places, residual_in)
    return (attended, combined)


def solution(mesh):
    placed = (
        P(("grp", "ctx"), "exp"),
        P(("grp", "ctx"), None),
        P(("grp", "ctx"), None),
        P("grp"),
        P(("grp", "ctx", "exp"), None),
        P("exp", "ctx"),
        P(),
        P(("grp", "ctx", "exp"), None),
        P(("grp", "ctx", "exp"), None),
        P("exp", None, "ctx"),
        P("exp", None, "ctx"),
        P("exp", None, "ctx"),
    )
    return jax.shard_map(
        shards,
        mesh=mesh,
        in_specs=placed,
        out_specs=(P(("grp", "ctx", "exp"), None), P(("grp", "ctx", "exp"), None)),
        check_vma=False,
    )
```

```python
import functools

import jax
import jax.numpy as jnp
from jax import lax
from jax.experimental import pallas as pl
from jax.experimental.pallas import tpu as pltpu
from jax.sharding import PartitionSpec as P

QH = 64
KVH = 4
HD = 128
CAP = 2
DOCMAX = 512
KEY_TILE = 128
MIB = 1024 * 1024
LOG2E = 1.4426950408889634


def swap(x, axis, mask):
    count = lax.axis_size(axis)
    return lax.ppermute(x, axis, [(i, i ^ mask) for i in range(count)])


def shift(x, axis, by):
    count = lax.axis_size(axis)
    return lax.ppermute(x, axis, [(i, (i + by) % count) for i in range(count)])


def reversed_bits(count):
    order = [0]
    step = 1
    while step < count:
        order = [2 * i for i in order]
        order = order + [i + 1 for i in order]
        step *= 2
    return order


def vmem(limit_mib):
    return pltpu.CompilerParams(vmem_limit_bytes=limit_mib * MIB)


def whole_vmem(count):
    return [pl.BlockSpec(memory_space=pltpu.VMEM)] * count


def anywhere(count):
    return [pl.BlockSpec(memory_space=pl.ANY)] * count


FREE = pl.CostEstimate(flops=0, bytes_accessed=0, transcendentals=0)


def slot_ranks(routes_t, flight):
    tokens = routes_t.shape[1]
    rows = [jnp.max((routes_t == j).astype(jnp.float32), axis=0, keepdims=True) for j in range(flight)]
    named = jnp.concatenate(rows, axis=0)
    before = lax.broadcasted_iota(jnp.int32, (tokens, tokens), 0) < lax.broadcasted_iota(
        jnp.int32, (tokens, tokens), 1
    )
    ranks = jnp.dot(
        named.astype(jnp.bfloat16), before.astype(jnp.bfloat16), preferred_element_type=jnp.float32
    )
    return named, ranks


def spread(rows, count, source_of):
    have = rows.shape[0]
    out_row = lax.broadcasted_iota(jnp.int32, (count, have), 0)
    col = lax.broadcasted_iota(jnp.int32, (count, have), 1)
    onehot = (col == source_of(out_row)).astype(jnp.bfloat16)
    return jnp.dot(onehot, rows.astype(jnp.bfloat16), preferred_element_type=jnp.float32)


def ready_kernel(
    lengths_hbm, q_hbm, q_ref, bias_ref, lengths_ref, q_sem, lengths_sem
):
    q_copy = pltpu.make_async_copy(q_hbm, q_ref, q_sem)
    lengths_copy = pltpu.make_async_copy(lengths_hbm, lengths_ref, lengths_sem)
    lengths_copy.start()
    q_copy.start()
    tokens = q_ref.shape[0]
    window = DOCMAX + KEY_TILE
    lengths_copy.wait()
    first = lax.axis_index("ctx") * tokens
    bounds = [jnp.int32(0)]
    for i in range(lengths_ref.shape[0] - 1):
        bounds.append(bounds[-1] + lengths_ref[i])
    for row0 in range(0, tokens, KEY_TILE):
        query_pos = first + row0 + lax.broadcasted_iota(jnp.int32, (KEY_TILE, 1), 0)
        starts = jnp.zeros((KEY_TILE, 1), jnp.int32)
        for bound in bounds:
            starts = jnp.where(query_pos >= bound, bound, starts)
        key_pos = first + row0 - DOCMAX + lax.broadcasted_iota(jnp.int32, (KEY_TILE, window), 1)
        allowed = (key_pos <= query_pos) & (key_pos >= starts)
        bias_ref[row0 : row0 + KEY_TILE, :] = jnp.where(allowed, 0.0, -1e30)
    q_copy.wait()


def ready(lengths, queries):
    tokens = queries.shape[0]
    return pl.pallas_call(
        ready_kernel,
        out_shape=(
            jax.ShapeDtypeStruct(queries.shape, queries.dtype),
            jax.ShapeDtypeStruct((tokens, DOCMAX + KEY_TILE), jnp.float32),
        ),
        in_specs=[pl.BlockSpec(memory_space=pltpu.HBM)] * 2,
        out_specs=tuple(whole_vmem(2)),
        scratch_shapes=[
            pltpu.SMEM(lengths.shape, jnp.int32),
            pltpu.SemaphoreType.DMA,
            pltpu.SemaphoreType.DMA,
        ],
        compiler_params=vmem(16),
        cost_estimate=FREE,
        name="ready",
    )(lengths, queries)


def attention_kernel(
    q_ref, bias_ref, kv_far_ref, kv_near_ref, kv_own_ref, out_ref, k_all, v_all, *, heads, homes, half, sub
):
    tokens = q_ref.shape[0]
    block_tokens = tokens // homes
    exp_index = lax.axis_index("exp")
    for place, ref in enumerate((kv_far_ref, kv_near_ref, kv_own_ref)):
        k_all[place * tokens : (place + 1) * tokens, :] = ref[0]
        v_all[place * tokens : (place + 1) * tokens, :] = ref[1]
    order = reversed_bits(homes)
    window = DOCMAX + KEY_TILE
    scale = LOG2E / HD**0.5
    for home in range(homes):
        row0 = home * block_tokens + half * sub
        key0 = row0 // KEY_TILE * KEY_TILE
        k = k_all[key0 : key0 + window, :]
        v = v_all[key0 : key0 + window, :]
        other = home ^ exp_index
        place = jnp.int32(0)
        for position in range(homes):
            place = jnp.where(other == order[position], position, place)
        at = pl.multiple_of(place * sub, sub)
        queries = jnp.concatenate(
            [q_ref[row0 : row0 + sub, h * HD : (h + 1) * HD] for h in range(heads)], axis=0
        )
        scores = lax.dot_general(
            queries, k, (((1,), (1,)), ((), ())), preferred_element_type=jnp.float32
        )
        scores = scores.reshape(heads, sub, window) * scale + bias_ref[row0 : row0 + sub, :][None]
        best = jnp.max(scores, axis=2, keepdims=True)
        probs = jnp.exp2(scores - best)
        total = jnp.sum(probs, axis=2, keepdims=True)
        mixed = jnp.dot(
            probs.reshape(heads * sub, window).astype(jnp.bfloat16),
            v,
            preferred_element_type=jnp.float32,
        )
        result = (mixed / total.reshape(heads * sub, 1)).astype(jnp.bfloat16)
        for h in range(heads):
            out_ref[pl.ds(at, sub), h * HD : (h + 1) * HD] = result[h * sub : (h + 1) * sub]


def attention(queries, bias, kv_far, kv_near, kv_own, homes, half, sub):
    tokens, width = queries.shape
    return pl.pallas_call(
        functools.partial(
            attention_kernel, heads=width // HD, homes=homes, half=half, sub=sub
        ),
        out_shape=jax.ShapeDtypeStruct((homes * sub, width), jnp.bfloat16),
        in_specs=whole_vmem(5),
        out_specs=pl.BlockSpec(memory_space=pltpu.VMEM),
        scratch_shapes=[pltpu.VMEM((3 * tokens, HD), jnp.bfloat16)] * 2,
        compiler_params=vmem(24),
        cost_estimate=FREE,
        name="attention_" + str(half),
    )(queries, bias, kv_far, kv_near, kv_own)


def pick_kernel(residual_ref, *refs, homes, halves, sub):
    routes_refs = refs[:homes]
    heads_refs = refs[homes : homes + halves]
    out_ref = refs[-1]
    exp_index = lax.axis_index("exp")
    order = reversed_bits(homes)
    width = heads_refs[0].shape[1]
    flight = homes
    lines = flight * homes * CAP
    line = lax.broadcasted_iota(jnp.int32, (lines, 1), 0)
    line_home = line // CAP % homes
    line_slot = (line % CAP).astype(jnp.float32)
    line_place = line // (CAP * homes)
    line_expert = jnp.zeros((lines, 1), jnp.int32)
    for position in range(flight):
        line_expert = jnp.where(line_place == position, order[position] ^ exp_index, line_expert)
    col = lax.broadcasted_iota(jnp.int32, (lines, flight), 1)
    onehot = (col == line_expert).astype(jnp.bfloat16)
    routed = jnp.zeros((lines, width), jnp.float32)
    for position in range(homes):
        mask = order[position]
        named, ranks = slot_ranks(routes_refs[mask][...], flight)
        named_l = jnp.dot(onehot, named.astype(jnp.bfloat16), preferred_element_type=jnp.float32)
        ranks_l = jnp.dot(onehot, ranks.astype(jnp.bfloat16), preferred_element_type=jnp.float32)
        hit = (named_l > 0.5) & (ranks_l == line_slot) & (line_home == (mask ^ exp_index))
        picks = jnp.where(hit, 1.0, 0.0)
        for half in range(halves):
            routed = routed + jnp.dot(
                picks[:, half * sub : (half + 1) * sub].astype(jnp.bfloat16),
                heads_refs[half][position * sub : (position + 1) * sub, :],
                preferred_element_type=jnp.float32,
            )
    out_ref[:lines, :] = routed.astype(jnp.bfloat16)
    slots = flight * CAP
    named, ranks = slot_ranks(routes_refs[0][...], flight)
    slot = lax.broadcasted_iota(jnp.int32, (slots, 1), 0)
    named_s = spread(named, slots, lambda i: i // CAP)
    ranks_s = spread(ranks, slots, lambda i: i // CAP)
    hit = (named_s > 0.5) & (ranks_s == (slot % CAP).astype(jnp.float32))
    rows = jnp.dot(
        jnp.where(hit, 1.0, 0.0).astype(jnp.bfloat16),
        residual_ref[...],
        preferred_element_type=jnp.float32,
    )
    parts = residual_ref.shape[1] // width
    rows = jnp.concatenate([rows[:, i * width : (i + 1) * width] for i in range(parts)], axis=0)
    out_ref[lines:, :] = rows.astype(jnp.bfloat16)


def pick(residual, routes_all, heads_out, sub):
    homes = len(routes_all)
    width = heads_out[0].shape[1]
    rows = homes * homes * CAP + homes * CAP * (residual.shape[1] // width)
    return pl.pallas_call(
        functools.partial(pick_kernel, homes=homes, halves=len(heads_out), sub=sub),
        out_shape=jax.ShapeDtypeStruct((rows, width), jnp.bfloat16),
        in_specs=whole_vmem(1 + homes + len(heads_out)),
        out_specs=pl.BlockSpec(memory_space=pltpu.VMEM),
        compiler_params=vmem(16),
        cost_estimate=FREE,
        name="pick",
    )(residual, *routes_all, *heads_out)


def routed_kernel(*refs, count, homes, after):
    piece_refs = refs[:count]
    weight_ref = refs[count]
    keep_ref, send_ref = refs[count + 1 + after :]
    ctx_index = lax.axis_index("ctx")
    exp_index = lax.axis_index("exp")
    order = reversed_bits(homes)
    cols = weight_ref.shape[1]
    depth = weight_ref.shape[0]
    flight = homes
    slots = flight * CAP
    lines = flight * homes * CAP
    half = lines // 2
    line = lax.broadcasted_iota(jnp.int32, (lines, slots), 0)
    line_place = line // (CAP * homes)
    expert = jnp.zeros((lines, slots), jnp.int32)
    for position in range(flight):
        expert = jnp.where(line_place == position, order[position] ^ exp_index, expert)
    source = jnp.where(line // CAP % homes == exp_index, expert * CAP + line % CAP, -1)
    onehot = (source == lax.broadcasted_iota(jnp.int32, (lines, slots), 1)).astype(jnp.bfloat16)
    heads = jnp.concatenate([ref[:lines, :] for ref in piece_refs], axis=0)
    product = jnp.dot(heads, weight_ref[...], preferred_element_type=jnp.float32)
    first_col = ctx_index * cols
    column = pl.multiple_of(first_col % depth, HD)
    row = pl.multiple_of(lines + first_col // depth * slots, slots)
    for place in range(count):
        extra = jnp.dot(
            onehot,
            piece_refs[place][pl.ds(row, slots), pl.ds(column, cols)],
            preferred_element_type=jnp.float32,
        )
        total = product[place * lines : (place + 1) * lines] + extra
        keep_ref[ctx_index ^ place] = total[:half].astype(jnp.bfloat16)
        send_ref[ctx_index ^ place] = total[half:].astype(jnp.bfloat16)


def routed_product(pieces, out_weight, homes, after=()):
    count = len(pieces)
    cols = out_weight.shape[1]
    shape = jax.ShapeDtypeStruct((count, homes * homes * CAP // 2, cols), jnp.bfloat16)
    return pl.pallas_call(
        functools.partial(routed_kernel, count=count, homes=homes, after=len(after)),
        out_shape=(shape, shape),
        in_specs=whole_vmem(count + 1) + anywhere(len(after)),
        out_specs=tuple(whole_vmem(2)),
        compiler_params=vmem(32),
        cost_estimate=FREE,
        name="routed_product",
    )(*pieces, out_weight, *after)


def add_middle_kernel(keep_ref, arrived_ref, *refs, last):
    total = keep_ref[...].astype(jnp.float32) + arrived_ref[...].astype(jnp.float32)
    count, rows, cols = total.shape
    if last:
        refs[0][...] = total.reshape(count * rows, cols).astype(refs[0].dtype)
    else:
        refs[0][...] = total[:, : rows // 2].astype(refs[0].dtype)
        refs[1][...] = total[:, rows // 2 :].astype(refs[1].dtype)


def add_middle(keep, arrived, last):
    count, rows, cols = keep.shape
    if last:
        out = jax.ShapeDtypeStruct((count * rows, cols), jnp.bfloat16)
    else:
        out = (
            jax.ShapeDtypeStruct((count, rows // 2, cols), jnp.float32),
            jax.ShapeDtypeStruct((count, rows // 2, cols), jnp.bfloat16),
        )
    return pl.pallas_call(
        functools.partial(add_middle_kernel, last=last),
        out_shape=out,
        in_specs=whole_vmem(2),
        out_specs=whole_vmem(1)[0] if last else tuple(whole_vmem(2)),
        compiler_params=vmem(16),
        cost_estimate=FREE,
        name="routed_sum",
    )(keep, arrived)


def project_kernel(*refs, count, homes, sub, upper, after):
    piece_refs = refs[:count]
    weight_ref = refs[count]
    out_ref = refs[-1]
    half = homes // 2
    begin = half * sub if upper else 0
    weight = weight_ref[...]
    for i in range(0, count, 2):
        pair = piece_refs[i : i + 2]
        rows = jnp.concatenate([ref[begin : begin + half * sub, :] for ref in pair], axis=0)
        product = jnp.dot(rows, weight, preferred_element_type=jnp.float32).astype(jnp.bfloat16)
        for k in range(len(pair)):
            for place in range(half):
                at = (place * count + i + k) * sub
                source = (k * half + place) * sub
                out_ref[at : at + sub, :] = product[source : source + sub]


def project(pieces, out_weight, homes, sub, upper, after=()):
    count = len(pieces)
    return pl.pallas_call(
        functools.partial(
            project_kernel, count=count, homes=homes, sub=sub, upper=upper, after=len(after)
        ),
        out_shape=jax.ShapeDtypeStruct(
            (homes // 2 * count * sub, out_weight.shape[1]), jnp.bfloat16
        ),
        in_specs=whole_vmem(count + 1) + anywhere(len(after)),
        out_specs=pl.BlockSpec(memory_space=pltpu.VMEM),
        compiler_params=vmem(32),
        cost_estimate=FREE,
        name="project_leave" if upper else "project_stay",
    )(*pieces, out_weight, *after)


def add_kernel(keep_ref, arrived_ref, *refs):
    rows = keep_ref.shape[0] // len(refs)
    for i, ref in enumerate(refs):
        part = slice(i * rows, (i + 1) * rows)
        total = keep_ref[part, :].astype(jnp.float32) + arrived_ref[part, :].astype(jnp.float32)
        ref[...] = total.astype(ref.dtype)


def add(keep, arrived, dtypes):
    rows, cols = keep.shape
    count = len(dtypes)
    out = tuple(jax.ShapeDtypeStruct((rows // count, cols), dtype) for dtype in dtypes)
    return pl.pallas_call(
        add_kernel,
        out_shape=out,
        in_specs=whole_vmem(2),
        out_specs=tuple(whole_vmem(count)),
        compiler_params=vmem(16),
        cost_estimate=FREE,
        name="add",
    )(keep, arrived)


def hidden_kernel(*refs, count):
    row_refs = refs[:count]
    gain_ref, gate_ref, up_ref = refs[count : count + 3]
    out_ref = refs[-1]
    ctx_index = lax.axis_index("ctx")
    cols = row_refs[0].shape[1]
    rows = [ref[...].astype(jnp.float32) for ref in row_refs]
    square = sum(jnp.sum(row * row, axis=1, keepdims=True) for row in rows)
    inverse = lax.rsqrt(square / (cols * count) + 1e-06)
    gate = None
    up = None
    for place in range(count):
        at = pl.multiple_of((ctx_index ^ place) * cols, cols)
        normed = (rows[place] * inverse * gain_ref[:, pl.ds(at, cols)]).astype(jnp.bfloat16)
        gate_part = jnp.dot(normed, gate_ref[0, pl.ds(at, cols), :], preferred_element_type=jnp.float32)
        up_part = jnp.dot(normed, up_ref[0, pl.ds(at, cols), :], preferred_element_type=jnp.float32)
        gate = gate_part if gate is None else gate + gate_part
        up = up_part if up is None else up + up_part
    out_ref[...] = (gate / (1.0 + jnp.exp(-gate)) * up).astype(jnp.bfloat16)


def hidden_units(pieces, gain, gate_weight, up_weight, after=()):
    count = len(pieces)
    rows = pieces[0].shape[0]
    units = gate_weight.shape[2]
    return pl.pallas_call(
        functools.partial(hidden_kernel, count=count),
        out_shape=jax.ShapeDtypeStruct((rows, units), jnp.bfloat16),
        in_specs=whole_vmem(count + 3) + anywhere(len(after)),
        out_specs=pl.BlockSpec(memory_space=pltpu.VMEM),
        compiler_params=vmem(20),
        cost_estimate=FREE,
        name="hidden_units",
    )(*pieces, gain, gate_weight, up_weight, *after)


def down_kernel(*refs, count):
    piece_refs = refs[:count]
    down_ref = refs[count]
    out_ref = refs[-1]
    ctx_index = lax.axis_index("ctx")
    units = piece_refs[0].shape[1]
    total = None
    for place in range(count):
        at = pl.multiple_of((ctx_index ^ place) * units, units)
        part = jnp.dot(
            piece_refs[place][...], down_ref[0, pl.ds(at, units), :], preferred_element_type=jnp.float32
        )
        total = part if total is None else total + part
    out_ref[...] = total.astype(jnp.bfloat16)


def down_product(pieces, down_weight, after=()):
    count = len(pieces)
    rows = pieces[0].shape[0]
    return pl.pallas_call(
        functools.partial(down_kernel, count=count),
        out_shape=jax.ShapeDtypeStruct((rows, down_weight.shape[2]), jnp.bfloat16),
        in_specs=whole_vmem(count + 1) + anywhere(len(after)),
        out_specs=pl.BlockSpec(memory_space=pltpu.VMEM),
        compiler_params=vmem(20),
        cost_estimate=FREE,
        name="down_product",
    )(*pieces, down_weight, *after)


def attended_kernel(*refs, places):
    residual_ref = refs[len(places)]
    out_ref = refs[-1]
    ctx_index = lax.axis_index("ctx")
    for (place, row0), ref in zip(places, refs):
        rows, cols = ref.shape
        at = pl.multiple_of((ctx_index ^ place) * cols, cols)
        total = residual_ref[row0 : row0 + rows, pl.ds(at, cols)].astype(jnp.float32)
        total = total + ref[...].astype(jnp.float32)
        out_ref[row0 : row0 + rows, pl.ds(at, cols)] = total.astype(jnp.bfloat16)


def attended_rows(pieces, places, residual):
    return pl.pallas_call(
        functools.partial(attended_kernel, places=places),
        out_shape=jax.ShapeDtypeStruct(residual.shape, jnp.bfloat16),
        in_specs=whole_vmem(len(pieces) + 1),
        out_specs=pl.BlockSpec(memory_space=pltpu.VMEM),
        compiler_params=vmem(20),
        cost_estimate=FREE,
        name="attended_rows",
    )(*pieces, residual)


def combine_kernel(routes_ref, weights_ref, *refs, flight, count):
    back_refs = refs[:count]
    out_ref = refs[-1]
    routes_t = routes_ref[...]
    scores = weights_ref[...]
    shares = scores / jnp.sum(scores, axis=0, keepdims=True)
    named, ranks = slot_ranks(routes_t, flight)
    lines = []
    for j in range(flight):
        share = jnp.sum(jnp.where(routes_t == j, shares, 0.0), axis=0, keepdims=True)
        for r in range(CAP):
            lines.append(jnp.where(ranks[j : j + 1] == r, share, 0.0))
    lines = jnp.concatenate(lines, axis=0)
    cols = back_refs[0].shape[1]
    for place, ref in enumerate(back_refs):
        out_ref[:, place * cols : (place + 1) * cols] = lax.dot_general(
            lines,
            ref[...].astype(jnp.float32),
            (((0,), (0,)), ((), ())),
            precision=lax.Precision.HIGHEST,
            preferred_element_type=jnp.float32,
        ).astype(jnp.bfloat16)


def gather_pieces(x, axis):
    count = lax.axis_size(axis)
    found = {0: x}
    step = count // 2
    while step >= 1:
        keys = sorted(found)
        if len(keys) == 1:
            moved = [swap(found[0], axis, step)]
        else:
            packed = swap(jnp.stack([found[k] for k in keys]), axis, step)
            moved = [packed[i] for i in range(len(keys))]
        for k, piece in zip(keys, moved):
            found[k ^ step] = piece
        step //= 2
    return [found[k] for k in range(count)]


def gather_direct(x, axis):
    return [x] + [swap(x, axis, k) for k in range(1, lax.axis_size(axis))]


def after(x, *others):
    return lax.optimization_barrier((x,) + others)[0]


class Sequence:
    def __init__(self):
        self.last = None

    def tie(self, *xs):
        if self.last is None:
            return xs
        return lax.optimization_barrier(xs + (self.last,))[:-1]

    def run(self, step, xs, *rest):
        out = step(*self.tie(*xs), *rest)
        self.last = out[-1] if isinstance(out, (tuple, list)) else out
        return out


class Gather:
    def __init__(self, sequence, x):
        self.sequence = sequence
        self.found = {0: x}
        self.step = lax.axis_size("ctx") // 2

    def hop(self):
        names = sorted(self.found)
        pieces = self.sequence.tie(*[self.found[k] for k in names])
        for k, piece in zip(names, pieces):
            self.found[k ^ self.step] = swap(piece, "ctx", self.step)
        self.step //= 2

    def hops_to(self, step):
        while self.step >= step:
            self.hop()

    def pieces(self, names):
        return tuple(self.found[k] for k in names)


class Halving:
    def __init__(self, sequence, send, add_step):
        self.sequence = sequence
        self.keep = None
        self.result = None
        self.step = 1
        self.add_step = add_step
        self.count = lax.axis_size("exp")
        self.arrived = swap(send, "exp", 1)

    def advance(self, hold=False):
        self.step *= 2
        last = self.step >= self.count
        out = self.sequence.run(lambda k, a: self.add_step(k, a, last), (self.keep, self.arrived))
        if last:
            self.result = out
        else:
            self.keep, self.send = out
            if not hold:
                self.release()

    def release(self):
        (send,) = self.sequence.tie(self.send)
        self.arrived = swap(send, "exp", self.step)

    def finish(self):
        while self.step < self.count:
            self.advance()
        return self.result


def shards(
    queries,
    keys,
    values,
    doc_lengths,
    residual_in,
    out_weight,
    norm_gain,
    routes,
    route_weights,
    gate_weight,
    up_weight,
    down_weight,
):
    tokens = queries.shape[0]
    local_heads = queries.shape[1] // HD
    n_ctx = lax.axis_size("ctx")
    homes = lax.axis_size("exp")
    flight = gate_weight.shape[0] * homes
    ctx_index = lax.axis_index("ctx")
    exp_index = lax.axis_index("exp")
    block_tokens = residual_in.shape[0]
    width = residual_in.shape[1]
    cols = out_weight.shape[1]
    halves = 2 if block_tokens % 32 == 0 else 1
    sub = block_tokens // halves
    sequence = Sequence()

    def plain_add(kinds):
        def step(keep, arrived, last):
            return add(keep, arrived, kinds if last else (jnp.float32, jnp.bfloat16))

        return step

    kv_head = exp_index * local_heads // (QH // KVH)
    kv_own = jnp.stack(
        [
            lax.dynamic_slice_in_dim(keys, kv_head * HD, HD, 1),
            lax.dynamic_slice_in_dim(values, kv_head * HD, HD, 1),
        ]
    )
    kv_near = shift(kv_own, "ctx", 1)
    kv_far = shift(kv_own, "ctx", 2)
    q_ready, bias = ready(doc_lengths, after(queries, kv_own))

    routes_all = gather_direct(after(routes.T, kv_own), "exp")
    heads_out = []
    near = []
    far = []
    for half in range(halves):
        if half == halves - 1:
            routes_all = list(sequence.tie(*routes_all))
            (q_ready,) = lax.optimization_barrier((q_ready,) + tuple(routes_all))[:1]
        rows = sequence.run(
            lambda q: attention(q, bias, kv_far, kv_near, kv_own, homes, half, sub), (q_ready,)
        )
        heads_out.append(rows)
        near.append(swap(rows, "ctx", 1))
        far.append(Gather(sequence, rows))

    def leaving(blocks):
        return sequence.run(lambda *xs: project(xs, out_weight, homes, sub, True), blocks)

    def staying(blocks):
        return sequence.run(lambda *xs: project(xs, out_weight, homes, sub, False), blocks)

    names = [k for k in range(n_ctx) if k > 1]
    one = (jnp.bfloat16,)
    mine = tuple(heads_out)
    near = tuple(near)
    own = Halving(sequence, leaving(mine), plain_add(one))
    routed = sequence.run(lambda r: pick(r, routes_all, heads_out, sub), (residual_in,))
    routed_all = Gather(sequence, routed)
    routed_all.hops_to(2)
    beside = Halving(sequence, leaving(near), plain_add(one))
    own.keep = staying(mine)
    beside.keep = staying(near)
    own.advance()
    routed_all.hop()
    for gather in far:
        gather.found[0] = after(gather.found[0], routed_all.found[n_ctx // 2])
        gather.hops_to(2)
    keep, send = sequence.run(
        lambda *xs: routed_product(xs, out_weight, homes), routed_all.pieces(range(n_ctx))
    )
    routed_sum = Halving(sequence, send, add_middle)
    routed_sum.keep = keep
    beside.advance()
    (own_sum,) = own.finish()
    routed_sum.advance()
    far[0].hop()
    first = far[0].pieces(names)
    sums = [Halving(sequence, leaving(first), plain_add(one * len(names)))]
    sums[0].keep = staying(first)
    (near_sum,) = beside.finish()
    routed_sum.finish()
    stream_rows = gather_direct(routed_sum.result, "ctx")
    sums[0].advance()
    if halves > 1:
        far[1].hop()
        second = far[1].pieces(names)
        sums.append(Halving(sequence, leaving(second), plain_add(one * len(names))))
        sums[1].keep = staying(second)
    hidden = sequence.run(
        lambda *xs: hidden_units(xs, norm_gain[None, :], gate_weight, up_weight), tuple(stream_rows)
    )
    hidden_pieces = gather_direct(hidden, "ctx")
    sums[0].finish()
    if halves > 1:
        sums[1].advance()
    produced = sequence.run(lambda *xs: down_product(xs, down_weight), tuple(hidden_pieces))
    back = lax.all_to_all(
        produced.reshape(n_ctx * homes, CAP, cols),
        ("ctx", "exp"),
        split_axis=0,
        concat_axis=0,
        tiled=True,
    ).reshape(n_ctx, flight * CAP, cols)
    for total in sums:
        total.finish()
    parts = [own_sum, swap(near_sum, "ctx", 1)]
    places = [(0, 0), (1, 0)]

    def combine(*back):
        return pl.pallas_call(
            functools.partial(combine_kernel, flight=flight, count=n_ctx),
            out_shape=jax.ShapeDtypeStruct((block_tokens, width), jnp.bfloat16),
            in_specs=whole_vmem(2 + n_ctx),
            out_specs=pl.BlockSpec(memory_space=pltpu.VMEM),
            compiler_params=vmem(20),
            cost_estimate=FREE,
            name="combine",
        )(routes.T, route_weights.T, *back)

    combined = sequence.run(combine, tuple(back[i] for i in range(n_ctx)))
    for half in range(halves):
        for k, piece in zip(names, sums[half].result):
            parts.append(swap(piece, "ctx", k))
            places.append((k, half * sub))
    attended = sequence.run(lambda *xs: attended_rows(xs, places, residual_in), tuple(parts))
    return (attended, combined)


def solution(mesh):
    placed = (
        P(("grp", "ctx"), "exp"),
        P(("grp", "ctx"), None),
        P(("grp", "ctx"), None),
        P("grp"),
        P(("grp", "ctx", "exp"), None),
        P("exp", "ctx"),
        P(),
        P(("grp", "ctx", "exp"), None),
        P(("grp", "ctx", "exp"), None),
        P("exp", None, "ctx"),
        P("exp", None, "ctx"),
        P("exp", None, "ctx"),
    )
    return jax.shard_map(
        shards,
        mesh=mesh,
        in_specs=placed,
        out_specs=(P(("grp", "ctx", "exp"), None), P(("grp", "ctx", "exp"), None)),
        check_vma=False,
    )
```

```python
import functools

import jax
import jax.numpy as jnp
from jax import lax
from jax.experimental import pallas as pl
from jax.experimental.pallas import tpu as pltpu
from jax.sharding import PartitionSpec as P

QH = 64
KVH = 4
HD = 128
CAP = 2
DOCMAX = 512
KEY_TILE = 128
MIB = 1024 * 1024
LOG2E = 1.4426950408889634


def swap(x, axis, mask):
    count = lax.axis_size(axis)
    return lax.ppermute(x, axis, [(i, i ^ mask) for i in range(count)])


def shift(x, axis, by):
    count = lax.axis_size(axis)
    return lax.ppermute(x, axis, [(i, (i + by) % count) for i in range(count)])


def reversed_bits(count):
    order = [0]
    step = 1
    while step < count:
        order = [2 * i for i in order]
        order = order + [i + 1 for i in order]
        step *= 2
    return order


def vmem(limit_mib):
    return pltpu.CompilerParams(vmem_limit_bytes=limit_mib * MIB)


def whole_vmem(count):
    return [pl.BlockSpec(memory_space=pltpu.VMEM)] * count


def anywhere(count):
    return [pl.BlockSpec(memory_space=pl.ANY)] * count


FREE = pl.CostEstimate(flops=0, bytes_accessed=0, transcendentals=0)


class Step:
    def __init__(self, body, operands, results):
        self.body = body
        self.operands = tuple(operands)
        self.results = tuple(results)


def together(name, steps, *operands):
    counts = [(len(step.operands), len(step.results)) for step in steps]
    total = sum(ins for ins, _ in counts)

    def kernel(*refs):
        at, out_at = 0, total
        for step, (ins, outs) in zip(steps, counts):
            step.body(*refs[at : at + ins], *refs[out_at : out_at + outs])
            at += ins
            out_at += outs

    shapes = tuple(shape for step in steps for shape in step.results)
    flat = pl.pallas_call(
        kernel,
        out_shape=shapes,
        in_specs=whole_vmem(total),
        out_specs=tuple(whole_vmem(len(shapes))),
        compiler_params=vmem(40),
        cost_estimate=FREE,
        name=name,
    )(*operands)
    results = []
    for _, outs in counts:
        results.append(tuple(flat[:outs]))
        flat = flat[outs:]
    return results


def slot_ranks(routes_t, flight):
    tokens = routes_t.shape[1]
    rows = [jnp.max((routes_t == j).astype(jnp.float32), axis=0, keepdims=True) for j in range(flight)]
    named = jnp.concatenate(rows, axis=0)
    before = lax.broadcasted_iota(jnp.int32, (tokens, tokens), 0) < lax.broadcasted_iota(
        jnp.int32, (tokens, tokens), 1
    )
    ranks = jnp.dot(
        named.astype(jnp.bfloat16), before.astype(jnp.bfloat16), preferred_element_type=jnp.float32
    )
    return named, ranks


def spread(rows, count, source_of):
    have = rows.shape[0]
    out_row = lax.broadcasted_iota(jnp.int32, (count, have), 0)
    col = lax.broadcasted_iota(jnp.int32, (count, have), 1)
    onehot = (col == source_of(out_row)).astype(jnp.bfloat16)
    return jnp.dot(onehot, rows.astype(jnp.bfloat16), preferred_element_type=jnp.float32)


def ready_kernel(
    lengths_hbm, q_hbm, q_ref, bias_ref, lengths_ref, q_sem, lengths_sem
):
    q_copy = pltpu.make_async_copy(q_hbm, q_ref, q_sem)
    lengths_copy = pltpu.make_async_copy(lengths_hbm, lengths_ref, lengths_sem)
    lengths_copy.start()
    q_copy.start()
    tokens = q_ref.shape[0]
    window = DOCMAX + KEY_TILE
    lengths_copy.wait()
    first = lax.axis_index("ctx") * tokens
    bounds = [jnp.int32(0)]
    for i in range(lengths_ref.shape[0] - 1):
        bounds.append(bounds[-1] + lengths_ref[i])
    for row0 in range(0, tokens, KEY_TILE):
        query_pos = first + row0 + lax.broadcasted_iota(jnp.int32, (KEY_TILE, 1), 0)
        starts = jnp.zeros((KEY_TILE, 1), jnp.int32)
        for bound in bounds:
            starts = jnp.where(query_pos >= bound, bound, starts)
        key_pos = first + row0 - DOCMAX + lax.broadcasted_iota(jnp.int32, (KEY_TILE, window), 1)
        allowed = (key_pos <= query_pos) & (key_pos >= starts)
        bias_ref[row0 : row0 + KEY_TILE, :] = jnp.where(allowed, 0.0, -1e30)
    q_copy.wait()


def ready(lengths, queries):
    tokens = queries.shape[0]
    return pl.pallas_call(
        ready_kernel,
        out_shape=(
            jax.ShapeDtypeStruct(queries.shape, queries.dtype),
            jax.ShapeDtypeStruct((tokens, DOCMAX + KEY_TILE), jnp.float32),
        ),
        in_specs=[pl.BlockSpec(memory_space=pltpu.HBM)] * 2,
        out_specs=tuple(whole_vmem(2)),
        scratch_shapes=[
            pltpu.SMEM(lengths.shape, jnp.int32),
            pltpu.SemaphoreType.DMA,
            pltpu.SemaphoreType.DMA,
        ],
        compiler_params=vmem(16),
        cost_estimate=FREE,
        name="ready",
    )(lengths, queries)


def attention_kernel(
    q_ref, bias_ref, kv_far_ref, kv_near_ref, kv_own_ref, out_ref, k_all, v_all, *, heads, homes, half, sub
):
    tokens = q_ref.shape[0]
    block_tokens = tokens // homes
    exp_index = lax.axis_index("exp")
    for place, ref in enumerate((kv_far_ref, kv_near_ref, kv_own_ref)):
        k_all[place * tokens : (place + 1) * tokens, :] = ref[0]
        v_all[place * tokens : (place + 1) * tokens, :] = ref[1]
    order = reversed_bits(homes)
    window = DOCMAX + KEY_TILE
    scale = LOG2E / HD**0.5
    for home in range(homes):
        row0 = home * block_tokens + half * sub
        key0 = row0 // KEY_TILE * KEY_TILE
        k = k_all[key0 : key0 + window, :]
        v = v_all[key0 : key0 + window, :]
        other = home ^ exp_index
        place = jnp.int32(0)
        for position in range(homes):
            place = jnp.where(other == order[position], position, place)
        at = pl.multiple_of(place * sub, sub)
        queries = jnp.concatenate(
            [q_ref[row0 : row0 + sub, h * HD : (h + 1) * HD] for h in range(heads)], axis=0
        )
        scores = lax.dot_general(
            queries, k, (((1,), (1,)), ((), ())), preferred_element_type=jnp.float32
        )
        scores = scores.reshape(heads, sub, window) * scale + bias_ref[row0 : row0 + sub, :][None]
        best = jnp.max(scores, axis=2, keepdims=True)
        probs = jnp.exp2(scores - best)
        total = jnp.sum(probs, axis=2, keepdims=True)
        mixed = jnp.dot(
            probs.reshape(heads * sub, window).astype(jnp.bfloat16),
            v,
            preferred_element_type=jnp.float32,
        )
        result = (mixed / total.reshape(heads * sub, 1)).astype(jnp.bfloat16)
        for h in range(heads):
            out_ref[pl.ds(at, sub), h * HD : (h + 1) * HD] = result[h * sub : (h + 1) * sub]


def attention(queries, bias, kv_far, kv_near, kv_own, homes, half, sub):
    tokens, width = queries.shape
    return pl.pallas_call(
        functools.partial(
            attention_kernel, heads=width // HD, homes=homes, half=half, sub=sub
        ),
        out_shape=jax.ShapeDtypeStruct((homes * sub, width), jnp.bfloat16),
        in_specs=whole_vmem(5),
        out_specs=pl.BlockSpec(memory_space=pltpu.VMEM),
        scratch_shapes=[pltpu.VMEM((3 * tokens, HD), jnp.bfloat16)] * 2,
        compiler_params=vmem(24),
        cost_estimate=FREE,
        name="attention_" + str(half),
    )(queries, bias, kv_far, kv_near, kv_own)


def pick_kernel(residual_ref, *refs, homes, halves, sub):
    routes_refs = refs[:homes]
    heads_refs = refs[homes : homes + halves]
    out_ref = refs[-1]
    exp_index = lax.axis_index("exp")
    order = reversed_bits(homes)
    width = heads_refs[0].shape[1]
    flight = homes
    lines = flight * homes * CAP
    line = lax.broadcasted_iota(jnp.int32, (lines, 1), 0)
    line_home = line // CAP % homes
    line_slot = (line % CAP).astype(jnp.float32)
    line_place = line // (CAP * homes)
    line_expert = line_place ^ exp_index
    col = lax.broadcasted_iota(jnp.int32, (lines, flight), 1)
    onehot = (col == line_expert).astype(jnp.bfloat16)
    routed = jnp.zeros((lines, width), jnp.float32)
    for position in range(homes):
        mask = order[position]
        named, ranks = slot_ranks(routes_refs[mask][...], flight)
        named_l = jnp.dot(onehot, named.astype(jnp.bfloat16), preferred_element_type=jnp.float32)
        ranks_l = jnp.dot(onehot, ranks.astype(jnp.bfloat16), preferred_element_type=jnp.float32)
        hit = (named_l > 0.5) & (ranks_l == line_slot) & (line_home == (mask ^ exp_index))
        picks = jnp.where(hit, 1.0, 0.0)
        for half in range(halves):
            routed = routed + jnp.dot(
                picks[:, half * sub : (half + 1) * sub].astype(jnp.bfloat16),
                heads_refs[half][position * sub : (position + 1) * sub, :],
                preferred_element_type=jnp.float32,
            )
    out_ref[:lines, :] = routed.astype(jnp.bfloat16)
    slots = flight * CAP
    named, ranks = slot_ranks(routes_refs[0][...], flight)
    slot = lax.broadcasted_iota(jnp.int32, (slots, 1), 0)
    named_s = spread(named, slots, lambda i: i // CAP)
    ranks_s = spread(ranks, slots, lambda i: i // CAP)
    hit = (named_s > 0.5) & (ranks_s == (slot % CAP).astype(jnp.float32))
    rows = jnp.dot(
        jnp.where(hit, 1.0, 0.0).astype(jnp.bfloat16),
        residual_ref[...],
        preferred_element_type=jnp.float32,
    )
    parts = residual_ref.shape[1] // width
    rows = jnp.concatenate([rows[:, i * width : (i + 1) * width] for i in range(parts)], axis=0)
    out_ref[lines:, :] = rows.astype(jnp.bfloat16)


def pick(residual, routes_all, heads_out, sub):
    homes = len(routes_all)
    width = heads_out[0].shape[1]
    rows = homes * homes * CAP + homes * CAP * (residual.shape[1] // width)
    return Step(
        functools.partial(pick_kernel, homes=homes, halves=len(heads_out), sub=sub),
        (residual, *routes_all, *heads_out),
        (jax.ShapeDtypeStruct((rows, width), jnp.bfloat16),),
    )


def routed_kernel(*refs, count, homes):
    piece_refs = refs[:count]
    weight_ref = refs[count]
    out_refs = refs[count + 1 :]
    ctx_index = lax.axis_index("ctx")
    exp_index = lax.axis_index("exp")
    cols = weight_ref.shape[1]
    depth = weight_ref.shape[0]
    flight = homes
    slots = flight * CAP
    block = homes * CAP
    lines = flight * block
    line = lax.broadcasted_iota(jnp.int32, (lines, slots), 0)
    expert = line // block ^ exp_index
    source = jnp.where(line // CAP % homes == exp_index, expert * CAP + line % CAP, -1)
    onehot = (source == lax.broadcasted_iota(jnp.int32, (lines, slots), 1)).astype(jnp.bfloat16)
    heads = jnp.concatenate([ref[:lines, :] for ref in piece_refs], axis=0)
    product = jnp.dot(heads, weight_ref[...], preferred_element_type=jnp.float32)
    first_col = ctx_index * cols
    column = pl.multiple_of(first_col % depth, HD)
    row = pl.multiple_of(lines + first_col // depth * slots, slots)
    for place in range(count):
        extra = jnp.dot(
            onehot,
            piece_refs[place][pl.ds(row, slots), pl.ds(column, cols)],
            preferred_element_type=jnp.float32,
        )
        total = product[place * lines : (place + 1) * lines] + extra
        for k in range(flight):
            out_refs[k][ctx_index ^ place] = total[k * block : (k + 1) * block].astype(jnp.bfloat16)


def routed_product(pieces, out_weight, homes):
    count = len(pieces)
    shape = jax.ShapeDtypeStruct((count, homes * CAP, out_weight.shape[1]), jnp.bfloat16)
    return Step(
        functools.partial(routed_kernel, count=count, homes=homes),
        (*pieces, out_weight),
        (shape,) * homes,
    )


def routed_sum_kernel(*refs):
    total = refs[0][...].astype(jnp.float32)
    for ref in refs[1:-1]:
        total = total + ref[...].astype(jnp.float32)
    count, rows, cols = total.shape
    refs[-1][...] = total.reshape(count * rows, cols).astype(jnp.bfloat16)


def routed_sum(*blocks):
    count, rows, cols = blocks[0].shape
    return pl.pallas_call(
        routed_sum_kernel,
        out_shape=jax.ShapeDtypeStruct((count * rows, cols), jnp.bfloat16),
        in_specs=whole_vmem(len(blocks)),
        out_specs=pl.BlockSpec(memory_space=pltpu.VMEM),
        compiler_params=vmem(24),
        cost_estimate=FREE,
        name="routed_sum",
    )(*blocks)


def project_kernel(*refs, count, homes, sub, upper):
    piece_refs = refs[:count]
    weight_ref = refs[count]
    out_ref = refs[-1]
    half = homes // 2
    begin = half * sub if upper else 0
    weight = weight_ref[...]
    for i in range(0, count, 2):
        pair = piece_refs[i : i + 2]
        rows = jnp.concatenate([ref[begin : begin + half * sub, :] for ref in pair], axis=0)
        product = jnp.dot(rows, weight, preferred_element_type=jnp.float32).astype(jnp.bfloat16)
        for k in range(len(pair)):
            for place in range(half):
                at = (place * count + i + k) * sub
                source = (k * half + place) * sub
                out_ref[at : at + sub, :] = product[source : source + sub]


def project(pieces, out_weight, homes, sub, upper):
    count = len(pieces)
    return Step(
        functools.partial(project_kernel, count=count, homes=homes, sub=sub, upper=upper),
        (*pieces, out_weight),
        (
            jax.ShapeDtypeStruct(
                (homes // 2 * count * sub, out_weight.shape[1]), jnp.bfloat16
            ),
        ),
    )


def add_kernel(keep_ref, arrived_ref, *refs):
    rows = keep_ref.shape[0] // len(refs)
    for i, ref in enumerate(refs):
        part = slice(i * rows, (i + 1) * rows)
        total = keep_ref[part, :].astype(jnp.float32) + arrived_ref[part, :].astype(jnp.float32)
        ref[...] = total.astype(ref.dtype)


def add(keep, arrived, dtypes):
    rows, cols = keep.shape
    count = len(dtypes)
    out = tuple(jax.ShapeDtypeStruct((rows // count, cols), dtype) for dtype in dtypes)
    return pl.pallas_call(
        add_kernel,
        out_shape=out,
        in_specs=whole_vmem(2),
        out_specs=tuple(whole_vmem(count)),
        compiler_params=vmem(16),
        cost_estimate=FREE,
        name="add",
    )(keep, arrived)


def hidden_kernel(*refs, count):
    row_refs = refs[:count]
    gain_ref, gate_ref, up_ref = refs[count : count + 3]
    out_ref = refs[-1]
    ctx_index = lax.axis_index("ctx")
    cols = row_refs[0].shape[1]
    rows = [ref[...].astype(jnp.float32) for ref in row_refs]
    square = sum(jnp.sum(row * row, axis=1, keepdims=True) for row in rows)
    inverse = lax.rsqrt(square / (cols * count) + 1e-06)
    gate = None
    up = None
    for place in range(count):
        at = pl.multiple_of((ctx_index ^ place) * cols, cols)
        normed = (rows[place] * inverse * gain_ref[:, pl.ds(at, cols)]).astype(jnp.bfloat16)
        gate_part = jnp.dot(normed, gate_ref[0, pl.ds(at, cols), :], preferred_element_type=jnp.float32)
        up_part = jnp.dot(normed, up_ref[0, pl.ds(at, cols), :], preferred_element_type=jnp.float32)
        gate = gate_part if gate is None else gate + gate_part
        up = up_part if up is None else up + up_part
    out_ref[...] = (gate / (1.0 + jnp.exp(-gate)) * up).astype(jnp.bfloat16)


def hidden_units(pieces, gain, gate_weight, up_weight, after=()):
    count = len(pieces)
    rows = pieces[0].shape[0]
    units = gate_weight.shape[2]
    return pl.pallas_call(
        functools.partial(hidden_kernel, count=count),
        out_shape=jax.ShapeDtypeStruct((rows, units), jnp.bfloat16),
        in_specs=whole_vmem(count + 3) + anywhere(len(after)),
        out_specs=pl.BlockSpec(memory_space=pltpu.VMEM),
        compiler_params=vmem(20),
        cost_estimate=FREE,
        name="hidden_units",
    )(*pieces, gain, gate_weight, up_weight, *after)


def down_kernel(*refs, count):
    piece_refs = refs[:count]
    down_ref = refs[count]
    out_ref = refs[-1]
    ctx_index = lax.axis_index("ctx")
    units = piece_refs[0].shape[1]
    total = None
    for place in range(count):
        at = pl.multiple_of((ctx_index ^ place) * units, units)
        part = jnp.dot(
            piece_refs[place][...], down_ref[0, pl.ds(at, units), :], preferred_element_type=jnp.float32
        )
        total = part if total is None else total + part
    for home in range(out_ref.shape[0]):
        out_ref[home] = total[home * CAP : (home + 1) * CAP].astype(jnp.bfloat16)


def down_product(pieces, down_weight):
    count = len(pieces)
    rows = pieces[0].shape[0]
    return pl.pallas_call(
        functools.partial(down_kernel, count=count),
        out_shape=jax.ShapeDtypeStruct((rows // CAP, CAP, down_weight.shape[2]), jnp.bfloat16),
        in_specs=whole_vmem(count + 1),
        out_specs=pl.BlockSpec(memory_space=pltpu.VMEM),
        compiler_params=vmem(20),
        cost_estimate=FREE,
        name="down_product",
    )(*pieces, down_weight)


def attended_kernel(*refs, places):
    residual_ref = refs[len(places)]
    out_ref = refs[-1]
    ctx_index = lax.axis_index("ctx")
    for (place, row0), ref in zip(places, refs):
        rows, cols = ref.shape
        at = pl.multiple_of((ctx_index ^ place) * cols, cols)
        total = residual_ref[row0 : row0 + rows, pl.ds(at, cols)].astype(jnp.float32)
        total = total + ref[...].astype(jnp.float32)
        out_ref[row0 : row0 + rows, pl.ds(at, cols)] = total.astype(jnp.bfloat16)


def attended_rows(pieces, places, residual):
    return pl.pallas_call(
        functools.partial(attended_kernel, places=places),
        out_shape=jax.ShapeDtypeStruct(residual.shape, jnp.bfloat16),
        in_specs=whole_vmem(len(pieces) + 1),
        out_specs=pl.BlockSpec(memory_space=pltpu.VMEM),
        compiler_params=vmem(20),
        cost_estimate=FREE,
        name="attended_rows",
    )(*pieces, residual)


def combine_kernel(routes_ref, weights_ref, back_ref, out_ref, *, flight, count):
    routes_t = routes_ref[...]
    scores = weights_ref[...]
    shares = scores / jnp.sum(scores, axis=0, keepdims=True)
    named, ranks = slot_ranks(routes_t, flight)
    lines = []
    for j in range(flight):
        share = jnp.sum(jnp.where(routes_t == j, shares, 0.0), axis=0, keepdims=True)
        for r in range(CAP):
            lines.append(jnp.where(ranks[j : j + 1] == r, share, 0.0))
    lines = jnp.concatenate(lines, axis=0)
    pieces = []
    rest = lines
    for _ in range(3):
        piece = rest.astype(jnp.bfloat16)
        pieces.append(piece.astype(jnp.float32))
        rest = rest - pieces[-1]
    pieces = jnp.concatenate(pieces, axis=0).T.astype(jnp.bfloat16)
    cols = back_ref.shape[2]
    for place in range(count):
        rows = [back_ref[place * flight + j].astype(jnp.float32) for j in range(flight)]
        rows = jnp.concatenate(rows * 3, axis=0).astype(jnp.bfloat16)
        out_ref[:, place * cols : (place + 1) * cols] = jnp.dot(
            pieces, rows, preferred_element_type=jnp.float32
        ).astype(jnp.bfloat16)


def gather_pieces(x, axis):
    count = lax.axis_size(axis)
    found = {0: x}
    step = count // 2
    while step >= 1:
        keys = sorted(found)
        if len(keys) == 1:
            moved = [swap(found[0], axis, step)]
        else:
            packed = swap(jnp.stack([found[k] for k in keys]), axis, step)
            moved = [packed[i] for i in range(len(keys))]
        for k, piece in zip(keys, moved):
            found[k ^ step] = piece
        step //= 2
    return [found[k] for k in range(count)]


def gather_direct(x, axis):
    return [x] + [swap(x, axis, k) for k in range(1, lax.axis_size(axis))]


def after(x, *others):
    return lax.optimization_barrier((x,) + others)[0]


class Sequence:
    def __init__(self):
        self.last = None

    def tie(self, *xs):
        if self.last is None:
            return xs
        return lax.optimization_barrier(xs + (self.last,))[:-1]

    def run(self, step, xs, *rest):
        out = step(*self.tie(*xs), *rest)
        self.last = out[-1] if isinstance(out, (tuple, list)) else out
        return out


    def steps(self, name, *steps):
        operands = self.tie(*[x for step in steps for x in step.operands])
        results = together(name, steps, *operands)
        self.last = results[-1][-1]
        return results


class Gather:
    def __init__(self, sequence, x):
        self.sequence = sequence
        self.found = {0: x}
        self.step = lax.axis_size("ctx") // 2

    def hop(self):
        names = sorted(self.found)
        pieces = self.sequence.tie(*[self.found[k] for k in names])
        for k, piece in zip(names, pieces):
            self.found[k ^ self.step] = swap(piece, "ctx", self.step)
        self.step //= 2

    def wait(self, *others):
        for k in self.found:
            self.found[k] = after(self.found[k], *others)

    def hops_to(self, step):
        while self.step >= step:
            self.hop()

    def pieces(self, names):
        return tuple(self.found[k] for k in names)


class Halving:
    def __init__(self, sequence, keep, send, add_step, step=1):
        self.sequence = sequence
        self.keep = keep
        self.result = None
        self.step = step
        self.add_step = add_step
        self.count = lax.axis_size("exp")
        self.arrived = swap(send, "exp", step)

    def advance(self, hold=False):
        self.step *= 2
        last = self.step >= self.count
        out = self.sequence.run(lambda k, a: self.add_step(k, a, last), (self.keep, self.arrived))
        if last:
            self.result = out
        else:
            self.keep, self.send = out
            if not hold:
                self.release()

    def wait(self, *others):
        self.arrived = after(self.arrived, *others)

    def release(self):
        (send,) = self.sequence.tie(self.send)
        self.arrived = swap(send, "exp", self.step)

    def finish(self):
        while self.step < self.count:
            self.advance()
        return self.result


def shards(
    queries,
    keys,
    values,
    doc_lengths,
    residual_in,
    out_weight,
    norm_gain,
    routes,
    route_weights,
    gate_weight,
    up_weight,
    down_weight,
):
    tokens = queries.shape[0]
    local_heads = queries.shape[1] // HD
    n_ctx = lax.axis_size("ctx")
    homes = lax.axis_size("exp")
    flight = gate_weight.shape[0] * homes
    ctx_index = lax.axis_index("ctx")
    exp_index = lax.axis_index("exp")
    block_tokens = residual_in.shape[0]
    width = residual_in.shape[1]
    cols = out_weight.shape[1]
    halves = 2 if block_tokens % 32 == 0 else 1
    sub = block_tokens // halves
    sequence = Sequence()

    def plain_add(kinds):
        def step(keep, arrived, last):
            return add(keep, arrived, kinds if last else (jnp.float32, jnp.bfloat16))

        return step

    kv_head = exp_index * local_heads // (QH // KVH)
    kv_own = jnp.stack(
        [
            lax.dynamic_slice_in_dim(keys, kv_head * HD, HD, 1),
            lax.dynamic_slice_in_dim(values, kv_head * HD, HD, 1),
        ]
    )
    kv_near = shift(kv_own, "ctx", 1)
    kv_far = shift(kv_own, "ctx", 2)
    q_ready, bias = ready(doc_lengths, after(queries, kv_own))

    routes_all = gather_direct(after(routes.T, kv_own), "exp")
    heads_out = []
    near = []
    far = []
    for half in range(halves):
        if half == halves - 1:
            routes_all = list(sequence.tie(*routes_all))
            (q_ready,) = lax.optimization_barrier((q_ready,) + tuple(routes_all))[:1]
        rows = sequence.run(
            lambda q: attention(q, bias, kv_far, kv_near, kv_own, homes, half, sub), (q_ready,)
        )
        heads_out.append(rows)
        near.append(swap(rows, "ctx", 1))
        far.append(Gather(sequence, rows))

    def leaving(blocks):
        return project(blocks, out_weight, homes, sub, True)

    def staying(blocks):
        return project(blocks, out_weight, homes, sub, False)

    names = [k for k in range(n_ctx) if k > 1]
    one = (jnp.bfloat16,)
    mine = tuple(heads_out)
    near = tuple(near)
    far[0].hops_to(2)
    (own_send,), (routed,) = sequence.steps(
        "leave_and_pick", leaving(mine), pick(residual_in, routes_all, heads_out, sub)
    )
    routed_all = Gather(sequence, routed)
    (near_send,), (own_keep,), (near_keep,) = sequence.steps(
        "leave_and_stay", leaving(near), staying(mine), staying(near)
    )
    own = Halving(sequence, own_keep, own_send, plain_add(one))
    beside = Halving(sequence, near_keep, near_send, plain_add(one))
    own.advance()
    routed_all.hops_to(2)
    beside.advance()
    routed_all.hop()
    far[0].wait(routed_all.found[n_ctx // 2])
    far[0].hop()
    (own_sum,) = own.finish()
    if halves > 1:
        far[1].wait(routed_all.found[n_ctx // 2])
        far[1].hops_to(2)
    (blocks,) = sequence.steps(
        "routed_product", routed_product(routed_all.pieces(range(n_ctx)), out_weight, homes)
    )
    blocks = [blocks[0]] + [swap(blocks[k], "exp", k) for k in range(1, homes)]
    first = far[0].pieces(names)
    (send,), (keep,) = sequence.steps("far", leaving(first), staying(first))
    sums = [Halving(sequence, keep, send, plain_add(one * len(names)))]
    (near_sum,) = beside.finish()
    stream = sequence.run(routed_sum, tuple(blocks))
    stream_rows = gather_direct(stream, "ctx")
    if halves > 1:
        far[1].hop()
        second = far[1].pieces(names)
        (send,), (keep,) = sequence.steps("far", leaving(second), staying(second))
        sums.append(Halving(sequence, keep, send, plain_add(one * len(names))))
    hidden = sequence.run(
        lambda *xs: hidden_units(xs, norm_gain[None, :], gate_weight, up_weight), tuple(stream_rows)
    )
    hidden_pieces = gather_direct(hidden, "ctx")
    sums[0].advance()
    if halves > 1:
        sums[1].wait(*hidden_pieces)
        sums[1].advance()
    produced = sequence.run(lambda *xs: down_product(xs, down_weight), tuple(hidden_pieces))
    back = lax.all_to_all(
        produced,
        ("ctx", "exp"),
        split_axis=0,
        concat_axis=0,
        tiled=True,
    )
    for total in sums:
        total.finish()
    parts = [own_sum, swap(near_sum, "ctx", 1)]
    places = [(0, 0), (1, 0)]

    def combine(back):
        return pl.pallas_call(
            functools.partial(combine_kernel, flight=flight, count=n_ctx),
            out_shape=jax.ShapeDtypeStruct((block_tokens, width), jnp.bfloat16),
            in_specs=whole_vmem(3),
            out_specs=pl.BlockSpec(memory_space=pltpu.VMEM),
            compiler_params=vmem(20),
            cost_estimate=FREE,
            name="combine",
        )(routes.T, route_weights.T, back)

    combined = sequence.run(combine, (back,))
    for half in range(halves):
        for k, piece in zip(names, sums[half].result):
            parts.append(swap(piece, "ctx", k))
            places.append((k, half * sub))
    attended = sequence.run(lambda *xs: attended_rows(xs, places, residual_in), tuple(parts))
    return (attended, combined)


def solution(mesh):
    placed = (
        P(("grp", "ctx"), "exp"),
        P(("grp", "ctx"), None),
        P(("grp", "ctx"), None),
        P("grp"),
        P(("grp", "ctx", "exp"), None),
        P("exp", "ctx"),
        P(),
        P(("grp", "ctx", "exp"), None),
        P(("grp", "ctx", "exp"), None),
        P("exp", None, "ctx"),
        P("exp", None, "ctx"),
        P("exp", None, "ctx"),
    )
    return jax.shard_map(
        shards,
        mesh=mesh,
        in_specs=placed,
        out_specs=(P(("grp", "ctx", "exp"), None), P(("grp", "ctx", "exp"), None)),
        check_vma=False,
    )
```

```python
import functools

import jax
import jax.numpy as jnp
from jax import lax
from jax.experimental import pallas as pl
from jax.experimental.pallas import tpu as pltpu
from jax.sharding import PartitionSpec as P

QH = 64
KVH = 4
HD = 128
CAP = 2
DOCMAX = 512
KEY_TILE = 128
MIB = 1024 * 1024
LOG2E = 1.4426950408889634


def swap(x, axis, mask):
    count = lax.axis_size(axis)
    return lax.ppermute(x, axis, [(i, i ^ mask) for i in range(count)])


def shift(x, axis, by):
    count = lax.axis_size(axis)
    return lax.ppermute(x, axis, [(i, (i + by) % count) for i in range(count)])


def reversed_bits(count):
    order = [0]
    step = 1
    while step < count:
        order = [2 * i for i in order]
        order = order + [i + 1 for i in order]
        step *= 2
    return order


def vmem(limit_mib):
    return pltpu.CompilerParams(vmem_limit_bytes=limit_mib * MIB)


def whole_vmem(count):
    return [pl.BlockSpec(memory_space=pltpu.VMEM)] * count


def anywhere(count):
    return [pl.BlockSpec(memory_space=pl.ANY)] * count


FREE = pl.CostEstimate(flops=0, bytes_accessed=0, transcendentals=0)


class Step:
    def __init__(self, body, operands, results):
        self.body = body
        self.operands = tuple(operands)
        self.results = tuple(results)


def together(name, steps, *operands):
    counts = [(len(step.operands), len(step.results)) for step in steps]
    total = sum(ins for ins, _ in counts)

    def kernel(*refs):
        at, out_at = 0, total
        for step, (ins, outs) in zip(steps, counts):
            step.body(*refs[at : at + ins], *refs[out_at : out_at + outs])
            at += ins
            out_at += outs

    shapes = tuple(shape for step in steps for shape in step.results)
    flat = pl.pallas_call(
        kernel,
        out_shape=shapes,
        in_specs=whole_vmem(total),
        out_specs=tuple(whole_vmem(len(shapes))),
        compiler_params=vmem(40),
        cost_estimate=FREE,
        name=name,
    )(*operands)
    results = []
    for _, outs in counts:
        results.append(tuple(flat[:outs]))
        flat = flat[outs:]
    return results


def slot_ranks(routes_t, flight):
    tokens = routes_t.shape[1]
    rows = [jnp.max((routes_t == j).astype(jnp.float32), axis=0, keepdims=True) for j in range(flight)]
    named = jnp.concatenate(rows, axis=0)
    before = lax.broadcasted_iota(jnp.int32, (tokens, tokens), 0) < lax.broadcasted_iota(
        jnp.int32, (tokens, tokens), 1
    )
    ranks = jnp.dot(
        named.astype(jnp.bfloat16), before.astype(jnp.bfloat16), preferred_element_type=jnp.float32
    )
    return named, ranks


def spread(rows, count, source_of):
    have = rows.shape[0]
    out_row = lax.broadcasted_iota(jnp.int32, (count, have), 0)
    col = lax.broadcasted_iota(jnp.int32, (count, have), 1)
    onehot = (col == source_of(out_row)).astype(jnp.bfloat16)
    return jnp.dot(onehot, rows.astype(jnp.bfloat16), preferred_element_type=jnp.float32)


def ready_kernel(
    lengths_hbm, q_hbm, q_ref, bias_ref, lengths_ref, q_sem, lengths_sem
):
    q_copy = pltpu.make_async_copy(q_hbm, q_ref, q_sem)
    lengths_copy = pltpu.make_async_copy(lengths_hbm, lengths_ref, lengths_sem)
    lengths_copy.start()
    q_copy.start()
    tokens = q_ref.shape[0]
    window = DOCMAX + KEY_TILE
    lengths_copy.wait()
    first = lax.axis_index("ctx") * tokens
    bounds = [jnp.int32(0)]
    for i in range(lengths_ref.shape[0] - 1):
        bounds.append(bounds[-1] + lengths_ref[i])
    for row0 in range(0, tokens, KEY_TILE):
        query_pos = first + row0 + lax.broadcasted_iota(jnp.int32, (KEY_TILE, 1), 0)
        starts = jnp.zeros((KEY_TILE, 1), jnp.int32)
        for bound in bounds:
            starts = jnp.where(query_pos >= bound, bound, starts)
        key_pos = first + row0 - DOCMAX + lax.broadcasted_iota(jnp.int32, (KEY_TILE, window), 1)
        allowed = (key_pos <= query_pos) & (key_pos >= starts)
        bias_ref[row0 : row0 + KEY_TILE, :] = jnp.where(allowed, 0.0, -1e30)
    q_copy.wait()


def ready(lengths, queries):
    tokens = queries.shape[0]
    return pl.pallas_call(
        ready_kernel,
        out_shape=(
            jax.ShapeDtypeStruct(queries.shape, queries.dtype),
            jax.ShapeDtypeStruct((tokens, DOCMAX + KEY_TILE), jnp.float32),
        ),
        in_specs=[pl.BlockSpec(memory_space=pltpu.HBM)] * 2,
        out_specs=tuple(whole_vmem(2)),
        scratch_shapes=[
            pltpu.SMEM(lengths.shape, jnp.int32),
            pltpu.SemaphoreType.DMA,
            pltpu.SemaphoreType.DMA,
        ],
        compiler_params=vmem(16),
        cost_estimate=FREE,
        name="ready",
    )(lengths, queries)


def attention_kernel(
    q_ref, bias_ref, kv_far_ref, kv_near_ref, kv_own_ref, out_ref, k_all, v_all, *, heads, homes, half, sub
):
    tokens = q_ref.shape[0]
    block_tokens = tokens // homes
    exp_index = lax.axis_index("exp")
    for place, ref in enumerate((kv_far_ref, kv_near_ref, kv_own_ref)):
        k_all[place * tokens : (place + 1) * tokens, :] = ref[0]
        v_all[place * tokens : (place + 1) * tokens, :] = ref[1]
    order = reversed_bits(homes)
    window = DOCMAX + KEY_TILE
    scale = LOG2E / HD**0.5
    for home in range(homes):
        row0 = home * block_tokens + half * sub
        key0 = row0 // KEY_TILE * KEY_TILE
        k = k_all[key0 : key0 + window, :]
        v = v_all[key0 : key0 + window, :]
        other = home ^ exp_index
        place = jnp.int32(0)
        for position in range(homes):
            place = jnp.where(other == order[position], position, place)
        at = pl.multiple_of(place * sub, sub)
        queries = jnp.concatenate(
            [q_ref[row0 : row0 + sub, h * HD : (h + 1) * HD] for h in range(heads)], axis=0
        )
        scores = lax.dot_general(
            queries, k, (((1,), (1,)), ((), ())), preferred_element_type=jnp.float32
        )
        scores = scores.reshape(heads, sub, window) * scale + bias_ref[row0 : row0 + sub, :][None]
        best = jnp.max(scores, axis=2, keepdims=True)
        probs = jnp.exp2(scores - best)
        total = jnp.sum(probs, axis=2, keepdims=True)
        mixed = jnp.dot(
            probs.reshape(heads * sub, window).astype(jnp.bfloat16),
            v,
            preferred_element_type=jnp.float32,
        )
        result = (mixed / total.reshape(heads * sub, 1)).astype(jnp.bfloat16)
        for h in range(heads):
            out_ref[pl.ds(at, sub), h * HD : (h + 1) * HD] = result[h * sub : (h + 1) * sub]


def attention(queries, bias, kv_far, kv_near, kv_own, homes, half, sub):
    tokens, width = queries.shape
    return pl.pallas_call(
        functools.partial(
            attention_kernel, heads=width // HD, homes=homes, half=half, sub=sub
        ),
        out_shape=jax.ShapeDtypeStruct((homes * sub, width), jnp.bfloat16),
        in_specs=whole_vmem(5),
        out_specs=pl.BlockSpec(memory_space=pltpu.VMEM),
        scratch_shapes=[pltpu.VMEM((3 * tokens, HD), jnp.bfloat16)] * 2,
        compiler_params=vmem(24),
        cost_estimate=FREE,
        name="attention_" + str(half),
    )(queries, bias, kv_far, kv_near, kv_own)


def pick_kernel(residual_ref, *refs, homes, halves, sub):
    routes_refs = refs[:homes]
    heads_refs = refs[homes : homes + halves]
    out_ref = refs[-1]
    exp_index = lax.axis_index("exp")
    order = reversed_bits(homes)
    width = heads_refs[0].shape[1]
    flight = homes
    lines = flight * homes * CAP
    line = lax.broadcasted_iota(jnp.int32, (lines, 1), 0)
    line_home = line // CAP % homes
    line_slot = (line % CAP).astype(jnp.float32)
    line_place = line // (CAP * homes)
    line_expert = line_place ^ exp_index
    col = lax.broadcasted_iota(jnp.int32, (lines, flight), 1)
    onehot = (col == line_expert).astype(jnp.bfloat16)
    routed = jnp.zeros((lines, width), jnp.float32)
    for position in range(homes):
        mask = order[position]
        named, ranks = slot_ranks(routes_refs[mask][...], flight)
        named_l = jnp.dot(onehot, named.astype(jnp.bfloat16), preferred_element_type=jnp.float32)
        ranks_l = jnp.dot(onehot, ranks.astype(jnp.bfloat16), preferred_element_type=jnp.float32)
        hit = (named_l > 0.5) & (ranks_l == line_slot) & (line_home == (mask ^ exp_index))
        picks = jnp.where(hit, 1.0, 0.0)
        for half in range(halves):
            routed = routed + jnp.dot(
                picks[:, half * sub : (half + 1) * sub].astype(jnp.bfloat16),
                heads_refs[half][position * sub : (position + 1) * sub, :],
                preferred_element_type=jnp.float32,
            )
    out_ref[:lines, :] = routed.astype(jnp.bfloat16)
    slots = flight * CAP
    named, ranks = slot_ranks(routes_refs[0][...], flight)
    slot = lax.broadcasted_iota(jnp.int32, (slots, 1), 0)
    named_s = spread(named, slots, lambda i: i // CAP)
    ranks_s = spread(ranks, slots, lambda i: i // CAP)
    hit = (named_s > 0.5) & (ranks_s == (slot % CAP).astype(jnp.float32))
    rows = jnp.dot(
        jnp.where(hit, 1.0, 0.0).astype(jnp.bfloat16),
        residual_ref[...],
        preferred_element_type=jnp.float32,
    )
    parts = residual_ref.shape[1] // width
    rows = jnp.concatenate([rows[:, i * width : (i + 1) * width] for i in range(parts)], axis=0)
    out_ref[lines:, :] = rows.astype(jnp.bfloat16)


def pick(residual, routes_all, heads_out, sub):
    homes = len(routes_all)
    width = heads_out[0].shape[1]
    rows = homes * homes * CAP + homes * CAP * (residual.shape[1] // width)
    return Step(
        functools.partial(pick_kernel, homes=homes, halves=len(heads_out), sub=sub),
        (residual, *routes_all, *heads_out),
        (jax.ShapeDtypeStruct((rows, width), jnp.bfloat16),),
    )


def routed_kernel(*refs, count, homes):
    piece_refs = refs[:count]
    weight_ref = refs[count]
    out_refs = refs[count + 1 :]
    ctx_index = lax.axis_index("ctx")
    exp_index = lax.axis_index("exp")
    cols = weight_ref.shape[1]
    depth = weight_ref.shape[0]
    flight = homes
    slots = flight * CAP
    block = homes * CAP
    lines = flight * block
    line = lax.broadcasted_iota(jnp.int32, (lines, slots), 0)
    expert = line // block ^ exp_index
    source = jnp.where(line // CAP % homes == exp_index, expert * CAP + line % CAP, -1)
    onehot = (source == lax.broadcasted_iota(jnp.int32, (lines, slots), 1)).astype(jnp.bfloat16)
    heads = jnp.concatenate([ref[:lines, :] for ref in piece_refs], axis=0)
    product = jnp.dot(heads, weight_ref[...], preferred_element_type=jnp.float32)
    first_col = ctx_index * cols
    column = pl.multiple_of(first_col % depth, HD)
    row = pl.multiple_of(lines + first_col // depth * slots, slots)
    for place in range(count):
        extra = jnp.dot(
            onehot,
            piece_refs[place][pl.ds(row, slots), pl.ds(column, cols)],
            preferred_element_type=jnp.float32,
        )
        total = product[place * lines : (place + 1) * lines] + extra
        for k in range(flight):
            out_refs[k][ctx_index ^ place] = total[k * block : (k + 1) * block].astype(jnp.bfloat16)


def routed_product(pieces, out_weight, homes):
    count = len(pieces)
    shape = jax.ShapeDtypeStruct((count, homes * CAP, out_weight.shape[1]), jnp.bfloat16)
    return Step(
        functools.partial(routed_kernel, count=count, homes=homes),
        (*pieces, out_weight),
        (shape,) * homes,
    )


def routed_sum_kernel(*refs):
    total = refs[0][...].astype(jnp.float32)
    for ref in refs[1:-1]:
        total = total + ref[...].astype(jnp.float32)
    count, rows, cols = total.shape
    refs[-1][...] = total.reshape(count * rows, cols).astype(jnp.bfloat16)


def routed_sum(*blocks):
    count, rows, cols = blocks[0].shape
    return pl.pallas_call(
        routed_sum_kernel,
        out_shape=jax.ShapeDtypeStruct((count * rows, cols), jnp.bfloat16),
        in_specs=whole_vmem(len(blocks)),
        out_specs=pl.BlockSpec(memory_space=pltpu.VMEM),
        compiler_params=vmem(24),
        cost_estimate=FREE,
        name="routed_sum",
    )(*blocks)


def project_kernel(*refs, count, homes, sub, upper):
    piece_refs = refs[:count]
    weight_ref = refs[count]
    out_ref = refs[-1]
    half = homes // 2
    begin = half * sub if upper else 0
    weight = weight_ref[...]
    for i in range(0, count, 2):
        pair = piece_refs[i : i + 2]
        rows = jnp.concatenate([ref[begin : begin + half * sub, :] for ref in pair], axis=0)
        product = jnp.dot(rows, weight, preferred_element_type=jnp.float32).astype(jnp.bfloat16)
        for k in range(len(pair)):
            for place in range(half):
                at = (place * count + i + k) * sub
                source = (k * half + place) * sub
                out_ref[at : at + sub, :] = product[source : source + sub]


def project(pieces, out_weight, homes, sub, upper):
    count = len(pieces)
    return Step(
        functools.partial(project_kernel, count=count, homes=homes, sub=sub, upper=upper),
        (*pieces, out_weight),
        (
            jax.ShapeDtypeStruct(
                (homes // 2 * count * sub, out_weight.shape[1]), jnp.bfloat16
            ),
        ),
    )


def add_kernel(keep_ref, arrived_ref, *refs):
    rows = keep_ref.shape[0] // len(refs)
    for i, ref in enumerate(refs):
        part = slice(i * rows, (i + 1) * rows)
        total = keep_ref[part, :].astype(jnp.float32) + arrived_ref[part, :].astype(jnp.float32)
        ref[...] = total.astype(ref.dtype)


def add(keep, arrived, dtypes):
    rows, cols = keep.shape
    count = len(dtypes)
    out = tuple(jax.ShapeDtypeStruct((rows // count, cols), dtype) for dtype in dtypes)
    return pl.pallas_call(
        add_kernel,
        out_shape=out,
        in_specs=whole_vmem(2),
        out_specs=tuple(whole_vmem(count)),
        compiler_params=vmem(16),
        cost_estimate=FREE,
        name="add",
    )(keep, arrived)


def hidden_kernel(*refs, count):
    row_refs = refs[:count]
    gain_ref, gate_ref, up_ref = refs[count : count + 3]
    out_ref = refs[-1]
    ctx_index = lax.axis_index("ctx")
    cols = row_refs[0].shape[1]
    rows = [ref[...].astype(jnp.float32) for ref in row_refs]
    square = sum(jnp.sum(row * row, axis=1, keepdims=True) for row in rows)
    inverse = lax.rsqrt(square / (cols * count) + 1e-06)
    gate = None
    up = None
    for place in range(count):
        at = pl.multiple_of((ctx_index ^ place) * cols, cols)
        normed = (rows[place] * inverse * gain_ref[:, pl.ds(at, cols)]).astype(jnp.bfloat16)
        gate_part = jnp.dot(normed, gate_ref[0, pl.ds(at, cols), :], preferred_element_type=jnp.float32)
        up_part = jnp.dot(normed, up_ref[0, pl.ds(at, cols), :], preferred_element_type=jnp.float32)
        gate = gate_part if gate is None else gate + gate_part
        up = up_part if up is None else up + up_part
    out_ref[...] = (gate / (1.0 + jnp.exp(-gate)) * up).astype(jnp.bfloat16)


def hidden_units(pieces, gain, gate_weight, up_weight, after=()):
    count = len(pieces)
    rows = pieces[0].shape[0]
    units = gate_weight.shape[2]
    return pl.pallas_call(
        functools.partial(hidden_kernel, count=count),
        out_shape=jax.ShapeDtypeStruct((rows, units), jnp.bfloat16),
        in_specs=whole_vmem(count + 3) + anywhere(len(after)),
        out_specs=pl.BlockSpec(memory_space=pltpu.VMEM),
        compiler_params=vmem(20),
        cost_estimate=FREE,
        name="hidden_units",
    )(*pieces, gain, gate_weight, up_weight, *after)


def down_kernel(*refs, count):
    piece_refs = refs[:count]
    down_ref = refs[count]
    out_ref = refs[-1]
    ctx_index = lax.axis_index("ctx")
    units = piece_refs[0].shape[1]
    total = None
    for place in range(count):
        at = pl.multiple_of((ctx_index ^ place) * units, units)
        part = jnp.dot(
            piece_refs[place][...], down_ref[0, pl.ds(at, units), :], preferred_element_type=jnp.float32
        )
        total = part if total is None else total + part
    for home in range(out_ref.shape[0]):
        out_ref[home] = total[home * CAP : (home + 1) * CAP].astype(jnp.bfloat16)


def down_product(pieces, down_weight):
    count = len(pieces)
    rows = pieces[0].shape[0]
    return pl.pallas_call(
        functools.partial(down_kernel, count=count),
        out_shape=jax.ShapeDtypeStruct((rows // CAP, CAP, down_weight.shape[2]), jnp.bfloat16),
        in_specs=whole_vmem(count + 1),
        out_specs=pl.BlockSpec(memory_space=pltpu.VMEM),
        compiler_params=vmem(20),
        cost_estimate=FREE,
        name="down_product",
    )(*pieces, down_weight)


def attended_kernel(*refs, places):
    residual_ref = refs[len(places)]
    out_ref = refs[-1]
    ctx_index = lax.axis_index("ctx")
    for (place, row0), ref in zip(places, refs):
        rows, cols = ref.shape
        at = pl.multiple_of((ctx_index ^ place) * cols, cols)
        total = residual_ref[row0 : row0 + rows, pl.ds(at, cols)].astype(jnp.float32)
        total = total + ref[...].astype(jnp.float32)
        out_ref[row0 : row0 + rows, pl.ds(at, cols)] = total.astype(jnp.bfloat16)


def attended_rows(pieces, places, residual):
    return pl.pallas_call(
        functools.partial(attended_kernel, places=places),
        out_shape=jax.ShapeDtypeStruct(residual.shape, jnp.bfloat16),
        in_specs=whole_vmem(len(pieces) + 1),
        out_specs=pl.BlockSpec(memory_space=pltpu.VMEM),
        compiler_params=vmem(20),
        cost_estimate=FREE,
        name="attended_rows",
    )(*pieces, residual)


def combine_kernel(routes_ref, weights_ref, back_ref, out_ref, *, flight, count):
    routes_t = routes_ref[...]
    scores = weights_ref[...]
    shares = scores / jnp.sum(scores, axis=0, keepdims=True)
    named, ranks = slot_ranks(routes_t, flight)
    lines = []
    for j in range(flight):
        share = jnp.sum(jnp.where(routes_t == j, shares, 0.0), axis=0, keepdims=True)
        for r in range(CAP):
            lines.append(jnp.where(ranks[j : j + 1] == r, share, 0.0))
    lines = jnp.concatenate(lines, axis=0)
    pieces = []
    rest = lines
    for _ in range(3):
        piece = rest.astype(jnp.bfloat16)
        pieces.append(piece.astype(jnp.float32))
        rest = rest - pieces[-1]
    pieces = jnp.concatenate(pieces, axis=0).T.astype(jnp.bfloat16)
    cols = back_ref.shape[2]
    for place in range(count):
        rows = [back_ref[place * flight + j].astype(jnp.float32) for j in range(flight)]
        rows = jnp.concatenate(rows * 3, axis=0).astype(jnp.bfloat16)
        out_ref[:, place * cols : (place + 1) * cols] = jnp.dot(
            pieces, rows, preferred_element_type=jnp.float32
        ).astype(jnp.bfloat16)


def gather_pieces(x, axis):
    count = lax.axis_size(axis)
    found = {0: x}
    step = count // 2
    while step >= 1:
        keys = sorted(found)
        if len(keys) == 1:
            moved = [swap(found[0], axis, step)]
        else:
            packed = swap(jnp.stack([found[k] for k in keys]), axis, step)
            moved = [packed[i] for i in range(len(keys))]
        for k, piece in zip(keys, moved):
            found[k ^ step] = piece
        step //= 2
    return [found[k] for k in range(count)]


def gather_direct(x, axis):
    return [x] + [swap(x, axis, k) for k in range(1, lax.axis_size(axis))]


def after(x, *others):
    return lax.optimization_barrier((x,) + others)[0]


class Sequence:
    def __init__(self):
        self.last = None

    def tie(self, *xs):
        if self.last is None:
            return xs
        return lax.optimization_barrier(xs + (self.last,))[:-1]

    def run(self, step, xs, *rest):
        out = step(*self.tie(*xs), *rest)
        self.last = out[-1] if isinstance(out, (tuple, list)) else out
        return out


    def steps(self, name, *steps):
        operands = self.tie(*[x for step in steps for x in step.operands])
        results = together(name, steps, *operands)
        self.last = results[-1][-1]
        return results


class Gather:
    def __init__(self, sequence, x):
        self.sequence = sequence
        self.found = {0: x}
        self.step = lax.axis_size("ctx") // 2

    def hop(self):
        names = sorted(self.found)
        pieces = self.sequence.tie(*[self.found[k] for k in names])
        for k, piece in zip(names, pieces):
            self.found[k ^ self.step] = swap(piece, "ctx", self.step)
        self.step //= 2

    def wait(self, *others):
        for k in self.found:
            self.found[k] = after(self.found[k], *others)

    def hops_to(self, step):
        while self.step >= step:
            self.hop()

    def pieces(self, names):
        return tuple(self.found[k] for k in names)


class Halving:
    def __init__(self, sequence, keep, send, add_step, step=1):
        self.sequence = sequence
        self.keep = keep
        self.result = None
        self.step = step
        self.add_step = add_step
        self.count = lax.axis_size("exp")
        self.arrived = swap(send, "exp", step)

    def advance(self, hold=False):
        self.step *= 2
        last = self.step >= self.count
        out = self.sequence.run(lambda k, a: self.add_step(k, a, last), (self.keep, self.arrived))
        if last:
            self.result = out
        else:
            self.keep, self.send = out
            if not hold:
                self.release()

    def wait(self, *others):
        self.arrived = after(self.arrived, *others)

    def release(self):
        (send,) = self.sequence.tie(self.send)
        self.arrived = swap(send, "exp", self.step)

    def finish(self):
        while self.step < self.count:
            self.advance()
        return self.result


def shards(
    queries,
    keys,
    values,
    doc_lengths,
    residual_in,
    out_weight,
    norm_gain,
    routes,
    route_weights,
    gate_weight,
    up_weight,
    down_weight,
):
    tokens = queries.shape[0]
    local_heads = queries.shape[1] // HD
    n_ctx = lax.axis_size("ctx")
    homes = lax.axis_size("exp")
    flight = gate_weight.shape[0] * homes
    ctx_index = lax.axis_index("ctx")
    exp_index = lax.axis_index("exp")
    block_tokens = residual_in.shape[0]
    width = residual_in.shape[1]
    cols = out_weight.shape[1]
    halves = 2 if block_tokens % 32 == 0 else 1
    sub = block_tokens // halves
    sequence = Sequence()

    def plain_add(kinds):
        def step(keep, arrived, last):
            return add(keep, arrived, kinds if last else (jnp.float32, jnp.bfloat16))

        return step

    kv_head = exp_index * local_heads // (QH // KVH)
    kv_own = jnp.stack(
        [
            lax.dynamic_slice_in_dim(keys, kv_head * HD, HD, 1),
            lax.dynamic_slice_in_dim(values, kv_head * HD, HD, 1),
        ]
    )
    kv_near = shift(kv_own, "ctx", 1)
    kv_far = shift(kv_own, "ctx", 2)
    q_ready, bias = ready(doc_lengths, after(queries, kv_own))

    routes_all = gather_direct(after(routes.T, kv_own), "exp")
    heads_out = []
    near = []
    far = []
    for half in range(halves):
        if half == halves - 1:
            routes_all = list(sequence.tie(*routes_all))
            (q_ready,) = lax.optimization_barrier((q_ready,) + tuple(routes_all))[:1]
        rows = sequence.run(
            lambda q: attention(q, bias, kv_far, kv_near, kv_own, homes, half, sub), (q_ready,)
        )
        heads_out.append(rows)
        near.append(swap(rows, "ctx", 1))
        far.append(Gather(sequence, rows))

    def leaving(blocks):
        return project(blocks, out_weight, homes, sub, True)

    def staying(blocks):
        return project(blocks, out_weight, homes, sub, False)

    names = [k for k in range(n_ctx) if k > 1]
    one = (jnp.bfloat16,)
    mine = tuple(heads_out)
    near = tuple(near)
    far[0].hops_to(2)
    (own_send,), (routed,) = sequence.steps(
        "leave_and_pick", leaving(mine), pick(residual_in, routes_all, heads_out, sub)
    )
    routed_all = Gather(sequence, routed)
    (near_send,), (own_keep,), (near_keep,) = sequence.steps(
        "leave_and_stay", leaving(near), staying(mine), staying(near)
    )
    own = Halving(sequence, own_keep, own_send, plain_add(one))
    beside = Halving(sequence, near_keep, near_send, plain_add(one))
    own.advance()
    routed_all.hops_to(2)
    beside.advance()
    routed_all.hop()
    far[0].wait(routed_all.found[n_ctx // 2])
    far[0].hop()
    (own_sum,) = own.finish()
    if halves > 1:
        far[1].wait(routed_all.found[n_ctx // 2])
        far[1].hops_to(2)
    (blocks,) = sequence.steps(
        "routed_product", routed_product(routed_all.pieces(range(n_ctx)), out_weight, homes)
    )
    blocks = [blocks[0]] + [swap(blocks[k], "exp", k) for k in range(1, homes)]
    first = far[0].pieces(names)
    (send,), (keep,) = sequence.steps("far", leaving(first), staying(first))
    sums = [Halving(sequence, keep, send, plain_add(one * len(names)))]
    (near_sum,) = beside.finish()
    stream = sequence.run(routed_sum, tuple(blocks))
    stream_rows = gather_direct(stream, "ctx")
    if halves > 1:
        far[1].hop()
        second = far[1].pieces(names)
        second = lax.optimization_barrier(second + tuple(stream_rows))[: len(second)]
        (send,), (keep,) = sequence.steps("far", leaving(second), staying(second))
        sums.append(Halving(sequence, keep, send, plain_add(one * len(names))))
    hidden = sequence.run(
        lambda *xs: hidden_units(xs, norm_gain[None, :], gate_weight, up_weight), tuple(stream_rows)
    )
    hidden_pieces = gather_direct(hidden, "ctx")
    sums[0].advance()
    produced = sequence.run(lambda *xs: down_product(xs, down_weight), tuple(hidden_pieces))
    if halves > 1:
        sums[1].advance()
    (produced,) = sequence.tie(produced)
    back = lax.all_to_all(
        produced,
        ("ctx", "exp"),
        split_axis=0,
        concat_axis=0,
        tiled=True,
    )
    for total in sums:
        total.finish()
    parts = [own_sum, swap(near_sum, "ctx", 1)]
    places = [(0, 0), (1, 0)]

    def combine(back):
        return pl.pallas_call(
            functools.partial(combine_kernel, flight=flight, count=n_ctx),
            out_shape=jax.ShapeDtypeStruct((block_tokens, width), jnp.bfloat16),
            in_specs=whole_vmem(3),
            out_specs=pl.BlockSpec(memory_space=pltpu.VMEM),
            compiler_params=vmem(20),
            cost_estimate=FREE,
            name="combine",
        )(routes.T, route_weights.T, back)

    combined = sequence.run(combine, (back,))
    for half in range(halves):
        for k, piece in zip(names, sums[half].result):
            parts.append(swap(piece, "ctx", k))
            places.append((k, half * sub))
    attended = sequence.run(lambda *xs: attended_rows(xs, places, residual_in), tuple(parts))
    return (attended, combined)


def solution(mesh):
    placed = (
        P(("grp", "ctx"), "exp"),
        P(("grp", "ctx"), None),
        P(("grp", "ctx"), None),
        P("grp"),
        P(("grp", "ctx", "exp"), None),
        P("exp", "ctx"),
        P(),
        P(("grp", "ctx", "exp"), None),
        P(("grp", "ctx", "exp"), None),
        P("exp", None, "ctx"),
        P("exp", None, "ctx"),
        P("exp", None, "ctx"),
    )
    return jax.shard_map(
        shards,
        mesh=mesh,
        in_specs=placed,
        out_specs=(P(("grp", "ctx", "exp"), None), P(("grp", "ctx", "exp"), None)),
        check_vma=False,
    )
```

```python
import functools

import jax
import jax.numpy as jnp
from jax import lax
from jax.experimental import pallas as pl
from jax.experimental.pallas import tpu as pltpu
from jax.sharding import PartitionSpec as P

QH = 64
KVH = 4
HD = 128
CAP = 2
DOCMAX = 512
KEY_TILE = 128
MIB = 1024 * 1024
LOG2E = 1.4426950408889634


def swap(x, axis, mask):
    count = lax.axis_size(axis)
    return lax.ppermute(x, axis, [(i, i ^ mask) for i in range(count)])


def shift(x, axis, by):
    count = lax.axis_size(axis)
    return lax.ppermute(x, axis, [(i, (i + by) % count) for i in range(count)])


def reversed_bits(count):
    order = [0]
    step = 1
    while step < count:
        order = [2 * i for i in order]
        order = order + [i + 1 for i in order]
        step *= 2
    return order


def vmem(limit_mib):
    return pltpu.CompilerParams(vmem_limit_bytes=limit_mib * MIB)


def whole_vmem(count):
    return [pl.BlockSpec(memory_space=pltpu.VMEM)] * count


def anywhere(count):
    return [pl.BlockSpec(memory_space=pl.ANY)] * count


FREE = pl.CostEstimate(flops=0, bytes_accessed=0, transcendentals=0)


class Step:
    def __init__(self, body, operands, results):
        self.body = body
        self.operands = tuple(operands)
        self.results = tuple(results)


def together(name, steps, *operands):
    counts = [(len(step.operands), len(step.results)) for step in steps]
    total = sum(ins for ins, _ in counts)

    def kernel(*refs):
        at, out_at = 0, total
        for step, (ins, outs) in zip(steps, counts):
            step.body(*refs[at : at + ins], *refs[out_at : out_at + outs])
            at += ins
            out_at += outs

    shapes = tuple(shape for step in steps for shape in step.results)
    flat = pl.pallas_call(
        kernel,
        out_shape=shapes,
        in_specs=whole_vmem(total),
        out_specs=tuple(whole_vmem(len(shapes))),
        compiler_params=vmem(40),
        cost_estimate=FREE,
        name=name,
    )(*operands)
    results = []
    for _, outs in counts:
        results.append(tuple(flat[:outs]))
        flat = flat[outs:]
    return results


def slot_ranks(routes_t, flight):
    tokens = routes_t.shape[1]
    rows = [jnp.max((routes_t == j).astype(jnp.float32), axis=0, keepdims=True) for j in range(flight)]
    named = jnp.concatenate(rows, axis=0)
    before = lax.broadcasted_iota(jnp.int32, (tokens, tokens), 0) < lax.broadcasted_iota(
        jnp.int32, (tokens, tokens), 1
    )
    ranks = jnp.dot(
        named.astype(jnp.bfloat16), before.astype(jnp.bfloat16), preferred_element_type=jnp.float32
    )
    return named, ranks


def spread(rows, count, source_of):
    have = rows.shape[0]
    out_row = lax.broadcasted_iota(jnp.int32, (count, have), 0)
    col = lax.broadcasted_iota(jnp.int32, (count, have), 1)
    onehot = (col == source_of(out_row)).astype(jnp.bfloat16)
    return jnp.dot(onehot, rows.astype(jnp.bfloat16), preferred_element_type=jnp.float32)


def ready_kernel(
    lengths_hbm, q_hbm, q_ref, bias_ref, lengths_ref, q_sem, lengths_sem
):
    q_copy = pltpu.make_async_copy(q_hbm, q_ref, q_sem)
    lengths_copy = pltpu.make_async_copy(lengths_hbm, lengths_ref, lengths_sem)
    lengths_copy.start()
    q_copy.start()
    tokens = q_ref.shape[0]
    window = DOCMAX + KEY_TILE
    lengths_copy.wait()
    first = lax.axis_index("ctx") * tokens
    bounds = [jnp.int32(0)]
    for i in range(lengths_ref.shape[0] - 1):
        bounds.append(bounds[-1] + lengths_ref[i])
    for row0 in range(0, tokens, KEY_TILE):
        query_pos = first + row0 + lax.broadcasted_iota(jnp.int32, (KEY_TILE, 1), 0)
        starts = jnp.zeros((KEY_TILE, 1), jnp.int32)
        for bound in bounds:
            starts = jnp.where(query_pos >= bound, bound, starts)
        key_pos = first + row0 - DOCMAX + lax.broadcasted_iota(jnp.int32, (KEY_TILE, window), 1)
        allowed = (key_pos <= query_pos) & (key_pos >= starts)
        bias_ref[row0 : row0 + KEY_TILE, :] = jnp.where(allowed, 0.0, -1e30)
    q_copy.wait()


def ready(lengths, queries):
    tokens = queries.shape[0]
    return pl.pallas_call(
        ready_kernel,
        out_shape=(
            jax.ShapeDtypeStruct(queries.shape, queries.dtype),
            jax.ShapeDtypeStruct((tokens, DOCMAX + KEY_TILE), jnp.float32),
        ),
        in_specs=[pl.BlockSpec(memory_space=pltpu.HBM)] * 2,
        out_specs=tuple(whole_vmem(2)),
        scratch_shapes=[
            pltpu.SMEM(lengths.shape, jnp.int32),
            pltpu.SemaphoreType.DMA,
            pltpu.SemaphoreType.DMA,
        ],
        compiler_params=vmem(16),
        cost_estimate=FREE,
        name="ready",
    )(lengths, queries)


def attention_kernel(
    q_ref, bias_ref, kv_far_ref, kv_near_ref, kv_own_ref, out_ref, k_all, v_all, *, heads, homes, half, sub
):
    tokens = q_ref.shape[0]
    block_tokens = tokens // homes
    exp_index = lax.axis_index("exp")
    for place, ref in enumerate((kv_far_ref, kv_near_ref, kv_own_ref)):
        k_all[place * tokens : (place + 1) * tokens, :] = ref[0]
        v_all[place * tokens : (place + 1) * tokens, :] = ref[1]
    order = reversed_bits(homes)
    window = DOCMAX + KEY_TILE
    scale = LOG2E / HD**0.5
    for home in range(homes):
        row0 = home * block_tokens + half * sub
        key0 = row0 // KEY_TILE * KEY_TILE
        k = k_all[key0 : key0 + window, :]
        v = v_all[key0 : key0 + window, :]
        other = home ^ exp_index
        place = jnp.int32(0)
        for position in range(homes):
            place = jnp.where(other == order[position], position, place)
        at = pl.multiple_of(place * sub, sub)
        queries = jnp.concatenate(
            [q_ref[row0 : row0 + sub, h * HD : (h + 1) * HD] for h in range(heads)], axis=0
        )
        scores = lax.dot_general(
            queries, k, (((1,), (1,)), ((), ())), preferred_element_type=jnp.float32
        )
        scores = scores.reshape(heads, sub, window) * scale + bias_ref[row0 : row0 + sub, :][None]
        best = jnp.max(scores, axis=2, keepdims=True)
        probs = jnp.exp2(scores - best)
        total = jnp.sum(probs, axis=2, keepdims=True)
        mixed = jnp.dot(
            probs.reshape(heads * sub, window).astype(jnp.bfloat16),
            v,
            preferred_element_type=jnp.float32,
        )
        result = (mixed / total.reshape(heads * sub, 1)).astype(jnp.bfloat16)
        for h in range(heads):
            out_ref[pl.ds(at, sub), h * HD : (h + 1) * HD] = result[h * sub : (h + 1) * sub]


def attention(queries, bias, kv_far, kv_near, kv_own, homes, half, sub):
    tokens, width = queries.shape
    return pl.pallas_call(
        functools.partial(
            attention_kernel, heads=width // HD, homes=homes, half=half, sub=sub
        ),
        out_shape=jax.ShapeDtypeStruct((homes * sub, width), jnp.bfloat16),
        in_specs=whole_vmem(5),
        out_specs=pl.BlockSpec(memory_space=pltpu.VMEM),
        scratch_shapes=[pltpu.VMEM((3 * tokens, HD), jnp.bfloat16)] * 2,
        compiler_params=vmem(24),
        cost_estimate=FREE,
        name="attention_" + str(half),
    )(queries, bias, kv_far, kv_near, kv_own)


def pick_kernel(residual_ref, *refs, homes, halves, sub):
    routes_refs = refs[:homes]
    heads_refs = refs[homes : homes + halves]
    out_ref = refs[-1]
    exp_index = lax.axis_index("exp")
    order = reversed_bits(homes)
    width = heads_refs[0].shape[1]
    flight = homes
    lines = flight * homes * CAP
    line = lax.broadcasted_iota(jnp.int32, (lines, 1), 0)
    line_home = line // CAP % homes
    line_slot = (line % CAP).astype(jnp.float32)
    line_place = line // (CAP * homes)
    line_expert = line_place ^ exp_index
    col = lax.broadcasted_iota(jnp.int32, (lines, flight), 1)
    onehot = (col == line_expert).astype(jnp.bfloat16)
    routed = jnp.zeros((lines, width), jnp.float32)
    for position in range(homes):
        mask = order[position]
        named, ranks = slot_ranks(routes_refs[mask][...], flight)
        named_l = jnp.dot(onehot, named.astype(jnp.bfloat16), preferred_element_type=jnp.float32)
        ranks_l = jnp.dot(onehot, ranks.astype(jnp.bfloat16), preferred_element_type=jnp.float32)
        hit = (named_l > 0.5) & (ranks_l == line_slot) & (line_home == (mask ^ exp_index))
        picks = jnp.where(hit, 1.0, 0.0)
        for half in range(halves):
            routed = routed + jnp.dot(
                picks[:, half * sub : (half + 1) * sub].astype(jnp.bfloat16),
                heads_refs[half][position * sub : (position + 1) * sub, :],
                preferred_element_type=jnp.float32,
            )
    out_ref[:lines, :] = routed.astype(jnp.bfloat16)
    slots = flight * CAP
    named, ranks = slot_ranks(routes_refs[0][...], flight)
    slot = lax.broadcasted_iota(jnp.int32, (slots, 1), 0)
    named_s = spread(named, slots, lambda i: i // CAP)
    ranks_s = spread(ranks, slots, lambda i: i // CAP)
    hit = (named_s > 0.5) & (ranks_s == (slot % CAP).astype(jnp.float32))
    rows = jnp.dot(
        jnp.where(hit, 1.0, 0.0).astype(jnp.bfloat16),
        residual_ref[...],
        preferred_element_type=jnp.float32,
    )
    parts = residual_ref.shape[1] // width
    rows = jnp.concatenate([rows[:, i * width : (i + 1) * width] for i in range(parts)], axis=0)
    out_ref[lines:, :] = rows.astype(jnp.bfloat16)


def pick(residual, routes_all, heads_out, sub):
    homes = len(routes_all)
    width = heads_out[0].shape[1]
    rows = homes * homes * CAP + homes * CAP * (residual.shape[1] // width)
    return Step(
        functools.partial(pick_kernel, homes=homes, halves=len(heads_out), sub=sub),
        (residual, *routes_all, *heads_out),
        (jax.ShapeDtypeStruct((rows, width), jnp.bfloat16),),
    )


def routed_kernel(*refs, count, homes):
    piece_refs = refs[:count]
    weight_ref = refs[count]
    out_refs = refs[count + 1 :]
    ctx_index = lax.axis_index("ctx")
    exp_index = lax.axis_index("exp")
    cols = weight_ref.shape[1]
    depth = weight_ref.shape[0]
    flight = homes
    slots = flight * CAP
    block = homes * CAP
    lines = flight * block
    line = lax.broadcasted_iota(jnp.int32, (lines, slots), 0)
    expert = line // block ^ exp_index
    source = jnp.where(line // CAP % homes == exp_index, expert * CAP + line % CAP, -1)
    onehot = (source == lax.broadcasted_iota(jnp.int32, (lines, slots), 1)).astype(jnp.bfloat16)
    heads = jnp.concatenate([ref[:lines, :] for ref in piece_refs], axis=0)
    product = jnp.dot(heads, weight_ref[...], preferred_element_type=jnp.float32)
    first_col = ctx_index * cols
    column = pl.multiple_of(first_col % depth, HD)
    row = pl.multiple_of(lines + first_col // depth * slots, slots)
    for place in range(count):
        extra = jnp.dot(
            onehot,
            piece_refs[place][pl.ds(row, slots), pl.ds(column, cols)],
            preferred_element_type=jnp.float32,
        )
        total = product[place * lines : (place + 1) * lines] + extra
        for k in range(flight):
            out_refs[k][ctx_index ^ place] = total[k * block : (k + 1) * block].astype(jnp.bfloat16)


def routed_product(pieces, out_weight, homes):
    count = len(pieces)
    shape = jax.ShapeDtypeStruct((count, homes * CAP, out_weight.shape[1]), jnp.bfloat16)
    return Step(
        functools.partial(routed_kernel, count=count, homes=homes),
        (*pieces, out_weight),
        (shape,) * homes,
    )


def routed_sum_kernel(*refs):
    total = refs[0][...].astype(jnp.float32)
    for ref in refs[1:-1]:
        total = total + ref[...].astype(jnp.float32)
    count, rows, cols = total.shape
    refs[-1][...] = total.reshape(count * rows, cols).astype(jnp.bfloat16)


def routed_sum(*blocks):
    count, rows, cols = blocks[0].shape
    return pl.pallas_call(
        routed_sum_kernel,
        out_shape=jax.ShapeDtypeStruct((count * rows, cols), jnp.bfloat16),
        in_specs=whole_vmem(len(blocks)),
        out_specs=pl.BlockSpec(memory_space=pltpu.VMEM),
        compiler_params=vmem(24),
        cost_estimate=FREE,
        name="routed_sum",
    )(*blocks)


def project_kernel(*refs, count, homes, sub, upper):
    piece_refs = refs[:count]
    weight_ref = refs[count]
    out_ref = refs[-1]
    half = homes // 2
    begin = half * sub if upper else 0
    weight = weight_ref[...]
    for i in range(0, count, 2):
        pair = piece_refs[i : i + 2]
        rows = jnp.concatenate([ref[begin : begin + half * sub, :] for ref in pair], axis=0)
        product = jnp.dot(rows, weight, preferred_element_type=jnp.float32).astype(jnp.bfloat16)
        for k in range(len(pair)):
            for place in range(half):
                at = (place * count + i + k) * sub
                source = (k * half + place) * sub
                out_ref[at : at + sub, :] = product[source : source + sub]


def project(pieces, out_weight, homes, sub, upper):
    count = len(pieces)
    return Step(
        functools.partial(project_kernel, count=count, homes=homes, sub=sub, upper=upper),
        (*pieces, out_weight),
        (
            jax.ShapeDtypeStruct(
                (homes // 2 * count * sub, out_weight.shape[1]), jnp.bfloat16
            ),
        ),
    )


def add_kernel(keep_ref, arrived_ref, *refs):
    rows = keep_ref.shape[0] // len(refs)
    for i, ref in enumerate(refs):
        part = slice(i * rows, (i + 1) * rows)
        total = keep_ref[part, :].astype(jnp.float32) + arrived_ref[part, :].astype(jnp.float32)
        ref[...] = total.astype(ref.dtype)


def add(keep, arrived, dtypes):
    rows, cols = keep.shape
    count = len(dtypes)
    out = tuple(jax.ShapeDtypeStruct((rows // count, cols), dtype) for dtype in dtypes)
    return pl.pallas_call(
        add_kernel,
        out_shape=out,
        in_specs=whole_vmem(2),
        out_specs=tuple(whole_vmem(count)),
        compiler_params=vmem(16),
        cost_estimate=FREE,
        name="add",
    )(keep, arrived)


def hidden_kernel(*refs, count):
    row_refs = refs[:count]
    gain_ref, gate_ref, up_ref = refs[count : count + 3]
    out_ref = refs[-1]
    ctx_index = lax.axis_index("ctx")
    cols = row_refs[0].shape[1]
    rows = [ref[...].astype(jnp.float32) for ref in row_refs]
    square = sum(jnp.sum(row * row, axis=1, keepdims=True) for row in rows)
    inverse = lax.rsqrt(square / (cols * count) + 1e-06)
    gate = None
    up = None
    for place in range(count):
        at = pl.multiple_of((ctx_index ^ place) * cols, cols)
        normed = (rows[place] * inverse * gain_ref[:, pl.ds(at, cols)]).astype(jnp.bfloat16)
        gate_part = jnp.dot(normed, gate_ref[0, pl.ds(at, cols), :], preferred_element_type=jnp.float32)
        up_part = jnp.dot(normed, up_ref[0, pl.ds(at, cols), :], preferred_element_type=jnp.float32)
        gate = gate_part if gate is None else gate + gate_part
        up = up_part if up is None else up + up_part
    out_ref[...] = (gate / (1.0 + jnp.exp(-gate)) * up).astype(jnp.bfloat16)


def hidden_units(pieces, gain, gate_weight, up_weight, after=()):
    count = len(pieces)
    rows = pieces[0].shape[0]
    units = gate_weight.shape[2]
    return pl.pallas_call(
        functools.partial(hidden_kernel, count=count),
        out_shape=jax.ShapeDtypeStruct((rows, units), jnp.bfloat16),
        in_specs=whole_vmem(count + 3) + anywhere(len(after)),
        out_specs=pl.BlockSpec(memory_space=pltpu.VMEM),
        compiler_params=vmem(20),
        cost_estimate=FREE,
        name="hidden_units",
    )(*pieces, gain, gate_weight, up_weight, *after)


def down_kernel(*refs, count):
    piece_refs = refs[:count]
    down_ref = refs[count]
    out_ref = refs[-1]
    ctx_index = lax.axis_index("ctx")
    units = piece_refs[0].shape[1]
    total = None
    for place in range(count):
        at = pl.multiple_of((ctx_index ^ place) * units, units)
        part = jnp.dot(
            piece_refs[place][...], down_ref[0, pl.ds(at, units), :], preferred_element_type=jnp.float32
        )
        total = part if total is None else total + part
    for home in range(out_ref.shape[0]):
        out_ref[home] = total[home * CAP : (home + 1) * CAP].astype(jnp.bfloat16)


def down_product(pieces, down_weight):
    count = len(pieces)
    rows = pieces[0].shape[0]
    return pl.pallas_call(
        functools.partial(down_kernel, count=count),
        out_shape=jax.ShapeDtypeStruct((rows // CAP, CAP, down_weight.shape[2]), jnp.bfloat16),
        in_specs=whole_vmem(count + 1),
        out_specs=pl.BlockSpec(memory_space=pltpu.VMEM),
        compiler_params=vmem(20),
        cost_estimate=FREE,
        name="down_product",
    )(*pieces, down_weight)


def attended_kernel(*refs, places):
    residual_ref = refs[len(places)]
    out_ref = refs[-1]
    ctx_index = lax.axis_index("ctx")
    for (place, row0), ref in zip(places, refs):
        rows, cols = ref.shape
        at = pl.multiple_of((ctx_index ^ place) * cols, cols)
        total = residual_ref[row0 : row0 + rows, pl.ds(at, cols)].astype(jnp.float32)
        total = total + ref[...].astype(jnp.float32)
        out_ref[row0 : row0 + rows, pl.ds(at, cols)] = total.astype(jnp.bfloat16)


def attended_rows(pieces, places, residual):
    return pl.pallas_call(
        functools.partial(attended_kernel, places=places),
        out_shape=jax.ShapeDtypeStruct(residual.shape, jnp.bfloat16),
        in_specs=whole_vmem(len(pieces) + 1),
        out_specs=pl.BlockSpec(memory_space=pltpu.VMEM),
        compiler_params=vmem(20),
        cost_estimate=FREE,
        name="attended_rows",
    )(*pieces, residual)


def combine_kernel(routes_ref, weights_ref, back_ref, out_ref, *, flight, count):
    routes_t = routes_ref[...]
    scores = weights_ref[...]
    shares = scores / jnp.sum(scores, axis=0, keepdims=True)
    named, ranks = slot_ranks(routes_t, flight)
    lines = []
    for j in range(flight):
        share = jnp.sum(jnp.where(routes_t == j, shares, 0.0), axis=0, keepdims=True)
        for r in range(CAP):
            lines.append(jnp.where(ranks[j : j + 1] == r, share, 0.0))
    lines = jnp.concatenate(lines, axis=0)
    pieces = []
    rest = lines
    for _ in range(3):
        piece = rest.astype(jnp.bfloat16)
        pieces.append(piece.astype(jnp.float32))
        rest = rest - pieces[-1]
    pieces = jnp.concatenate(pieces, axis=0).T.astype(jnp.bfloat16)
    cols = back_ref.shape[2]
    for place in range(count):
        rows = [back_ref[place * flight + j].astype(jnp.float32) for j in range(flight)]
        rows = jnp.concatenate(rows * 3, axis=0).astype(jnp.bfloat16)
        out_ref[:, place * cols : (place + 1) * cols] = jnp.dot(
            pieces, rows, preferred_element_type=jnp.float32
        ).astype(jnp.bfloat16)


def gather_pieces(x, axis):
    count = lax.axis_size(axis)
    found = {0: x}
    step = count // 2
    while step >= 1:
        keys = sorted(found)
        if len(keys) == 1:
            moved = [swap(found[0], axis, step)]
        else:
            packed = swap(jnp.stack([found[k] for k in keys]), axis, step)
            moved = [packed[i] for i in range(len(keys))]
        for k, piece in zip(keys, moved):
            found[k ^ step] = piece
        step //= 2
    return [found[k] for k in range(count)]


def gather_direct(x, axis):
    return [x] + [swap(x, axis, k) for k in range(1, lax.axis_size(axis))]


def after(x, *others):
    return lax.optimization_barrier((x,) + others)[0]


class Sequence:
    def __init__(self):
        self.last = None

    def tie(self, *xs):
        if self.last is None:
            return xs
        return lax.optimization_barrier(xs + (self.last,))[:-1]

    def run(self, step, xs, *rest):
        out = step(*self.tie(*xs), *rest)
        self.last = out[-1] if isinstance(out, (tuple, list)) else out
        return out


    def steps(self, name, *steps):
        operands = self.tie(*[x for step in steps for x in step.operands])
        results = together(name, steps, *operands)
        self.last = results[-1][-1]
        return results


class Gather:
    def __init__(self, sequence, x):
        self.sequence = sequence
        self.found = {0: x}
        self.step = lax.axis_size("ctx") // 2

    def hop(self):
        names = sorted(self.found)
        pieces = self.sequence.tie(*[self.found[k] for k in names])
        for k, piece in zip(names, pieces):
            self.found[k ^ self.step] = swap(piece, "ctx", self.step)
        self.step //= 2

    def wait(self, *others):
        for k in self.found:
            self.found[k] = after(self.found[k], *others)

    def hops_to(self, step):
        while self.step >= step:
            self.hop()

    def pieces(self, names):
        return tuple(self.found[k] for k in names)


class Halving:
    def __init__(self, sequence, keep, send, add_step, step=1):
        self.sequence = sequence
        self.keep = keep
        self.result = None
        self.step = step
        self.add_step = add_step
        self.count = lax.axis_size("exp")
        self.arrived = swap(send, "exp", step)

    def advance(self, hold=False):
        self.step *= 2
        last = self.step >= self.count
        out = self.sequence.run(lambda k, a: self.add_step(k, a, last), (self.keep, self.arrived))
        if last:
            self.result = out
        else:
            self.keep, self.send = out
            if not hold:
                self.release()

    def wait(self, *others):
        self.arrived = after(self.arrived, *others)

    def release(self):
        (send,) = self.sequence.tie(self.send)
        self.arrived = swap(send, "exp", self.step)

    def finish(self):
        while self.step < self.count:
            self.advance()
        return self.result


def shards(
    queries,
    keys,
    values,
    doc_lengths,
    residual_in,
    out_weight,
    norm_gain,
    routes,
    route_weights,
    gate_weight,
    up_weight,
    down_weight,
):
    tokens = queries.shape[0]
    local_heads = queries.shape[1] // HD
    n_ctx = lax.axis_size("ctx")
    homes = lax.axis_size("exp")
    flight = gate_weight.shape[0] * homes
    ctx_index = lax.axis_index("ctx")
    exp_index = lax.axis_index("exp")
    block_tokens = residual_in.shape[0]
    width = residual_in.shape[1]
    cols = out_weight.shape[1]
    halves = 2 if block_tokens % 32 == 0 else 1
    sub = block_tokens // halves
    sequence = Sequence()

    def plain_add(kinds):
        def step(keep, arrived, last):
            return add(keep, arrived, kinds if last else (jnp.float32, jnp.bfloat16))

        return step

    kv_head = exp_index * local_heads // (QH // KVH)
    kv_own = jnp.stack(
        [
            lax.dynamic_slice_in_dim(keys, kv_head * HD, HD, 1),
            lax.dynamic_slice_in_dim(values, kv_head * HD, HD, 1),
        ]
    )
    kv_near = shift(kv_own, "ctx", 1)
    kv_far = shift(kv_own, "ctx", 2)
    q_ready, bias = ready(doc_lengths, after(queries, kv_own))

    routes_all = gather_direct(after(routes.T, kv_own), "exp")
    heads_out = []
    near = []
    far = []
    for half in range(halves):
        if half == halves - 1:
            routes_all = list(sequence.tie(*routes_all))
            (q_ready,) = lax.optimization_barrier((q_ready,) + tuple(routes_all))[:1]
        rows = sequence.run(
            lambda q: attention(q, bias, kv_far, kv_near, kv_own, homes, half, sub), (q_ready,)
        )
        heads_out.append(rows)
        near.append(swap(rows, "ctx", 1))
        far.append(Gather(sequence, rows))

    def leaving(blocks):
        return project(blocks, out_weight, homes, sub, True)

    def staying(blocks):
        return project(blocks, out_weight, homes, sub, False)

    names = [k for k in range(n_ctx) if k > 1]
    one = (jnp.bfloat16,)
    mine = tuple(heads_out)
    near = tuple(near)
    far[0].hops_to(2)
    ((own_send,),) = sequence.steps("leave", leaving(mine))
    ((routed,),) = sequence.steps("pick", pick(residual_in, routes_all, heads_out, sub))
    routed_all = Gather(sequence, routed)
    (near_send,), (own_keep,), (near_keep,) = sequence.steps(
        "leave_and_stay", leaving(near), staying(mine), staying(near)
    )
    own = Halving(sequence, own_keep, own_send, plain_add(one))
    beside = Halving(sequence, near_keep, near_send, plain_add(one))
    own.advance()
    routed_all.hops_to(2)
    beside.advance()
    routed_all.hop()
    far[0].wait(routed_all.found[n_ctx // 2])
    far[0].hop()
    (own_sum,) = own.finish()
    if halves > 1:
        far[1].wait(routed_all.found[n_ctx // 2])
        far[1].hops_to(2)
    (blocks,) = sequence.steps(
        "routed_product", routed_product(routed_all.pieces(range(n_ctx)), out_weight, homes)
    )
    blocks = [blocks[0]] + [swap(blocks[k], "exp", k) for k in range(1, homes)]
    first = far[0].pieces(names)
    (send,), (keep,) = sequence.steps("far", leaving(first), staying(first))
    sums = [Halving(sequence, keep, send, plain_add(one * len(names)))]
    (near_sum,) = beside.finish()
    stream = sequence.run(routed_sum, tuple(blocks))
    stream_rows = gather_direct(stream, "ctx")
    if halves > 1:
        far[1].hop()
        second = far[1].pieces(names)
        second = lax.optimization_barrier(second + tuple(stream_rows))[: len(second)]
        (send,), (keep,) = sequence.steps("far", leaving(second), staying(second))
        sums.append(Halving(sequence, keep, send, plain_add(one * len(names))))
    hidden = sequence.run(
        lambda *xs: hidden_units(xs, norm_gain[None, :], gate_weight, up_weight), tuple(stream_rows)
    )
    hidden_pieces = gather_direct(hidden, "ctx")
    sums[0].advance()
    produced = sequence.run(lambda *xs: down_product(xs, down_weight), tuple(hidden_pieces))
    if halves > 1:
        sums[1].advance()
    (produced,) = sequence.tie(produced)
    back = lax.all_to_all(
        produced,
        ("ctx", "exp"),
        split_axis=0,
        concat_axis=0,
        tiled=True,
    )
    for total in sums:
        total.finish()
    parts = [own_sum, swap(near_sum, "ctx", 1)]
    places = [(0, 0), (1, 0)]

    def combine(back):
        return pl.pallas_call(
            functools.partial(combine_kernel, flight=flight, count=n_ctx),
            out_shape=jax.ShapeDtypeStruct((block_tokens, width), jnp.bfloat16),
            in_specs=whole_vmem(3),
            out_specs=pl.BlockSpec(memory_space=pltpu.VMEM),
            compiler_params=vmem(20),
            cost_estimate=FREE,
            name="combine",
        )(routes.T, route_weights.T, back)

    combined = sequence.run(combine, (back,))
    for half in range(halves):
        for k, piece in zip(names, sums[half].result):
            parts.append(swap(piece, "ctx", k))
            places.append((k, half * sub))
    attended = sequence.run(lambda *xs: attended_rows(xs, places, residual_in), tuple(parts))
    return (attended, combined)


def solution(mesh):
    placed = (
        P(("grp", "ctx"), "exp"),
        P(("grp", "ctx"), None),
        P(("grp", "ctx"), None),
        P("grp"),
        P(("grp", "ctx", "exp"), None),
        P("exp", "ctx"),
        P(),
        P(("grp", "ctx", "exp"), None),
        P(("grp", "ctx", "exp"), None),
        P("exp", None, "ctx"),
        P("exp", None, "ctx"),
        P("exp", None, "ctx"),
    )
    return jax.shard_map(
        shards,
        mesh=mesh,
        in_specs=placed,
        out_specs=(P(("grp", "ctx", "exp"), None), P(("grp", "ctx", "exp"), None)),
        check_vma=False,
    )
```

```python
import functools

import jax
import jax.numpy as jnp
from jax import lax
from jax.experimental import pallas as pl
from jax.experimental.pallas import tpu as pltpu
from jax.sharding import PartitionSpec as P

QH = 64
KVH = 4
HD = 128
CAP = 2
DOCMAX = 512
KEY_TILE = 128
MIB = 1024 * 1024
LOG2E = 1.4426950408889634


def swap(x, axis, mask):
    count = lax.axis_size(axis)
    return lax.ppermute(x, axis, [(i, i ^ mask) for i in range(count)])


def shift(x, axis, by):
    count = lax.axis_size(axis)
    return lax.ppermute(x, axis, [(i, (i + by) % count) for i in range(count)])


def reversed_bits(count):
    order = [0]
    step = 1
    while step < count:
        order = [2 * i for i in order]
        order = order + [i + 1 for i in order]
        step *= 2
    return order


def vmem(limit_mib):
    return pltpu.CompilerParams(vmem_limit_bytes=limit_mib * MIB)


def whole_vmem(count):
    return [pl.BlockSpec(memory_space=pltpu.VMEM)] * count


def anywhere(count):
    return [pl.BlockSpec(memory_space=pl.ANY)] * count


FREE = pl.CostEstimate(flops=0, bytes_accessed=0, transcendentals=0)


class Step:
    def __init__(self, body, operands, results):
        self.body = body
        self.operands = tuple(operands)
        self.results = tuple(results)


def together(name, steps, *operands):
    counts = [(len(step.operands), len(step.results)) for step in steps]
    total = sum(ins for ins, _ in counts)

    def kernel(*refs):
        at, out_at = 0, total
        for step, (ins, outs) in zip(steps, counts):
            step.body(*refs[at : at + ins], *refs[out_at : out_at + outs])
            at += ins
            out_at += outs

    shapes = tuple(shape for step in steps for shape in step.results)
    flat = pl.pallas_call(
        kernel,
        out_shape=shapes,
        in_specs=whole_vmem(total),
        out_specs=tuple(whole_vmem(len(shapes))),
        compiler_params=vmem(40),
        cost_estimate=FREE,
        name=name,
    )(*operands)
    results = []
    for _, outs in counts:
        results.append(tuple(flat[:outs]))
        flat = flat[outs:]
    return results


def slot_ranks(routes_t, flight):
    tokens = routes_t.shape[1]
    rows = [jnp.max((routes_t == j).astype(jnp.float32), axis=0, keepdims=True) for j in range(flight)]
    named = jnp.concatenate(rows, axis=0)
    before = lax.broadcasted_iota(jnp.int32, (tokens, tokens), 0) < lax.broadcasted_iota(
        jnp.int32, (tokens, tokens), 1
    )
    ranks = jnp.dot(
        named.astype(jnp.bfloat16), before.astype(jnp.bfloat16), preferred_element_type=jnp.float32
    )
    return named, ranks


def spread(rows, count, source_of):
    have = rows.shape[0]
    out_row = lax.broadcasted_iota(jnp.int32, (count, have), 0)
    col = lax.broadcasted_iota(jnp.int32, (count, have), 1)
    onehot = (col == source_of(out_row)).astype(jnp.bfloat16)
    return jnp.dot(onehot, rows.astype(jnp.bfloat16), preferred_element_type=jnp.float32)


def ready_kernel(
    lengths_hbm, q_hbm, q_ref, bias_ref, lengths_ref, q_sem, lengths_sem
):
    q_copy = pltpu.make_async_copy(q_hbm, q_ref, q_sem)
    lengths_copy = pltpu.make_async_copy(lengths_hbm, lengths_ref, lengths_sem)
    lengths_copy.start()
    q_copy.start()
    tokens = q_ref.shape[0]
    window = DOCMAX + KEY_TILE
    lengths_copy.wait()
    first = lax.axis_index("ctx") * tokens
    bounds = [jnp.int32(0)]
    for i in range(lengths_ref.shape[0] - 1):
        bounds.append(bounds[-1] + lengths_ref[i])
    for row0 in range(0, tokens, KEY_TILE):
        query_pos = first + row0 + lax.broadcasted_iota(jnp.int32, (KEY_TILE, 1), 0)
        starts = jnp.zeros((KEY_TILE, 1), jnp.int32)
        for bound in bounds:
            starts = jnp.where(query_pos >= bound, bound, starts)
        key_pos = first + row0 - DOCMAX + lax.broadcasted_iota(jnp.int32, (KEY_TILE, window), 1)
        allowed = (key_pos <= query_pos) & (key_pos >= starts)
        bias_ref[row0 : row0 + KEY_TILE, :] = jnp.where(allowed, 0.0, -1e30)
    q_copy.wait()


def ready(lengths, queries):
    tokens = queries.shape[0]
    return pl.pallas_call(
        ready_kernel,
        out_shape=(
            jax.ShapeDtypeStruct(queries.shape, queries.dtype),
            jax.ShapeDtypeStruct((tokens, DOCMAX + KEY_TILE), jnp.float32),
        ),
        in_specs=[pl.BlockSpec(memory_space=pltpu.HBM)] * 2,
        out_specs=tuple(whole_vmem(2)),
        scratch_shapes=[
            pltpu.SMEM(lengths.shape, jnp.int32),
            pltpu.SemaphoreType.DMA,
            pltpu.SemaphoreType.DMA,
        ],
        compiler_params=vmem(16),
        cost_estimate=FREE,
        name="ready",
    )(lengths, queries)


def attention_kernel(
    q_ref, bias_ref, kv_far_ref, kv_near_ref, kv_own_ref, out_ref, k_all, v_all, *, heads, homes, half, sub
):
    tokens = q_ref.shape[0]
    block_tokens = tokens // homes
    exp_index = lax.axis_index("exp")
    for place, ref in enumerate((kv_far_ref, kv_near_ref, kv_own_ref)):
        k_all[place * tokens : (place + 1) * tokens, :] = ref[0]
        v_all[place * tokens : (place + 1) * tokens, :] = ref[1]
    order = reversed_bits(homes)
    window = DOCMAX + KEY_TILE
    scale = LOG2E / HD**0.5
    for home in range(homes):
        row0 = home * block_tokens + half * sub
        key0 = row0 // KEY_TILE * KEY_TILE
        k = k_all[key0 : key0 + window, :]
        v = v_all[key0 : key0 + window, :]
        other = home ^ exp_index
        place = jnp.int32(0)
        for position in range(homes):
            place = jnp.where(other == order[position], position, place)
        at = pl.multiple_of(place * sub, sub)
        queries = jnp.concatenate(
            [q_ref[row0 : row0 + sub, h * HD : (h + 1) * HD] for h in range(heads)], axis=0
        )
        scores = lax.dot_general(
            queries, k, (((1,), (1,)), ((), ())), preferred_element_type=jnp.float32
        )
        scores = scores.reshape(heads, sub, window) * scale + bias_ref[row0 : row0 + sub, :][None]
        best = jnp.max(scores, axis=2, keepdims=True)
        probs = jnp.exp2(scores - best)
        total = jnp.sum(probs, axis=2, keepdims=True)
        mixed = jnp.dot(
            probs.reshape(heads * sub, window).astype(jnp.bfloat16),
            v,
            preferred_element_type=jnp.float32,
        )
        result = (mixed / total.reshape(heads * sub, 1)).astype(jnp.bfloat16)
        for h in range(heads):
            out_ref[pl.ds(at, sub), h * HD : (h + 1) * HD] = result[h * sub : (h + 1) * sub]


def attention(queries, bias, kv_far, kv_near, kv_own, homes, half, sub):
    tokens, width = queries.shape
    return pl.pallas_call(
        functools.partial(
            attention_kernel, heads=width // HD, homes=homes, half=half, sub=sub
        ),
        out_shape=jax.ShapeDtypeStruct((homes * sub, width), jnp.bfloat16),
        in_specs=whole_vmem(5),
        out_specs=pl.BlockSpec(memory_space=pltpu.VMEM),
        scratch_shapes=[pltpu.VMEM((3 * tokens, HD), jnp.bfloat16)] * 2,
        compiler_params=vmem(24),
        cost_estimate=FREE,
        name="attention_" + str(half),
    )(queries, bias, kv_far, kv_near, kv_own)


def pick_kernel(residual_ref, *refs, homes, halves, sub):
    routes_refs = refs[:homes]
    heads_refs = refs[homes : homes + halves]
    out_ref = refs[-1]
    exp_index = lax.axis_index("exp")
    order = reversed_bits(homes)
    width = heads_refs[0].shape[1]
    flight = homes
    lines = flight * homes * CAP
    line = lax.broadcasted_iota(jnp.int32, (lines, 1), 0)
    line_home = line // CAP % homes
    line_slot = (line % CAP).astype(jnp.float32)
    line_place = line // (CAP * homes)
    line_expert = line_place ^ exp_index
    col = lax.broadcasted_iota(jnp.int32, (lines, flight), 1)
    onehot = (col == line_expert).astype(jnp.bfloat16)
    routed = jnp.zeros((lines, width), jnp.float32)
    for position in range(homes):
        mask = order[position]
        named, ranks = slot_ranks(routes_refs[mask][...], flight)
        named_l = jnp.dot(onehot, named.astype(jnp.bfloat16), preferred_element_type=jnp.float32)
        ranks_l = jnp.dot(onehot, ranks.astype(jnp.bfloat16), preferred_element_type=jnp.float32)
        hit = (named_l > 0.5) & (ranks_l == line_slot) & (line_home == (mask ^ exp_index))
        picks = jnp.where(hit, 1.0, 0.0)
        for half in range(halves):
            routed = routed + jnp.dot(
                picks[:, half * sub : (half + 1) * sub].astype(jnp.bfloat16),
                heads_refs[half][position * sub : (position + 1) * sub, :],
                preferred_element_type=jnp.float32,
            )
    out_ref[:lines, :] = routed.astype(jnp.bfloat16)
    slots = flight * CAP
    named, ranks = slot_ranks(routes_refs[0][...], flight)
    slot = lax.broadcasted_iota(jnp.int32, (slots, 1), 0)
    named_s = spread(named, slots, lambda i: i // CAP)
    ranks_s = spread(ranks, slots, lambda i: i // CAP)
    hit = (named_s > 0.5) & (ranks_s == (slot % CAP).astype(jnp.float32))
    rows = jnp.dot(
        jnp.where(hit, 1.0, 0.0).astype(jnp.bfloat16),
        residual_ref[...],
        preferred_element_type=jnp.float32,
    )
    parts = residual_ref.shape[1] // width
    rows = jnp.concatenate([rows[:, i * width : (i + 1) * width] for i in range(parts)], axis=0)
    out_ref[lines:, :] = rows.astype(jnp.bfloat16)


def pick(residual, routes_all, heads_out, sub):
    homes = len(routes_all)
    width = heads_out[0].shape[1]
    rows = homes * homes * CAP + homes * CAP * (residual.shape[1] // width)
    return Step(
        functools.partial(pick_kernel, homes=homes, halves=len(heads_out), sub=sub),
        (residual, *routes_all, *heads_out),
        (jax.ShapeDtypeStruct((rows, width), jnp.bfloat16),),
    )


def routed_kernel(*refs, count, homes):
    piece_refs = refs[:count]
    weight_ref = refs[count]
    out_refs = refs[count + 1 :]
    ctx_index = lax.axis_index("ctx")
    exp_index = lax.axis_index("exp")
    cols = weight_ref.shape[1]
    depth = weight_ref.shape[0]
    flight = homes
    slots = flight * CAP
    block = homes * CAP
    lines = flight * block
    first_col = ctx_index * cols
    column = pl.multiple_of(first_col % depth, HD)
    held = piece_refs[0].shape[0] - lines
    line = lax.broadcasted_iota(jnp.int32, (lines, held), 0)
    expert = line // block ^ exp_index
    row = first_col // depth * slots + expert * CAP + line % CAP
    source = jnp.where(line // CAP % homes == exp_index, row, -1)
    onehot = (source == lax.broadcasted_iota(jnp.int32, (lines, held), 1)).astype(jnp.bfloat16)
    heads = jnp.concatenate([ref[:lines, :] for ref in piece_refs], axis=0)
    product = jnp.dot(heads, weight_ref[...], preferred_element_type=jnp.float32)
    for place in range(count):
        extra = jnp.dot(
            onehot,
            piece_refs[place][lines:, pl.ds(column, cols)],
            preferred_element_type=jnp.float32,
        )
        total = product[place * lines : (place + 1) * lines] + extra
        for k in range(flight):
            out_refs[k][ctx_index ^ place] = total[k * block : (k + 1) * block].astype(jnp.bfloat16)


def routed_product(pieces, out_weight, homes):
    count = len(pieces)
    shape = jax.ShapeDtypeStruct((count, homes * CAP, out_weight.shape[1]), jnp.bfloat16)
    return Step(
        functools.partial(routed_kernel, count=count, homes=homes),
        (*pieces, out_weight),
        (shape,) * homes,
    )


def routed_sum_kernel(*refs):
    total = refs[0][...].astype(jnp.float32)
    for ref in refs[1:-1]:
        total = total + ref[...].astype(jnp.float32)
    count, rows, cols = total.shape
    refs[-1][...] = total.reshape(count * rows, cols).astype(jnp.bfloat16)


def routed_sum(*blocks):
    count, rows, cols = blocks[0].shape
    return pl.pallas_call(
        routed_sum_kernel,
        out_shape=jax.ShapeDtypeStruct((count * rows, cols), jnp.bfloat16),
        in_specs=whole_vmem(len(blocks)),
        out_specs=pl.BlockSpec(memory_space=pltpu.VMEM),
        compiler_params=vmem(24),
        cost_estimate=FREE,
        name="routed_sum",
    )(*blocks)


def project_kernel(*refs, count, homes, sub, upper):
    piece_refs = refs[:count]
    weight_ref = refs[count]
    out_ref = refs[-1]
    half = homes // 2
    begin = half * sub if upper else 0
    weight = weight_ref[...]
    for i in range(0, count, 2):
        pair = piece_refs[i : i + 2]
        rows = jnp.concatenate([ref[begin : begin + half * sub, :] for ref in pair], axis=0)
        product = jnp.dot(rows, weight, preferred_element_type=jnp.float32).astype(jnp.bfloat16)
        for k in range(len(pair)):
            for place in range(half):
                at = (place * count + i + k) * sub
                source = (k * half + place) * sub
                out_ref[at : at + sub, :] = product[source : source + sub]


def project(pieces, out_weight, homes, sub, upper):
    count = len(pieces)
    return Step(
        functools.partial(project_kernel, count=count, homes=homes, sub=sub, upper=upper),
        (*pieces, out_weight),
        (
            jax.ShapeDtypeStruct(
                (homes // 2 * count * sub, out_weight.shape[1]), jnp.bfloat16
            ),
        ),
    )


def add_kernel(keep_ref, arrived_ref, *refs):
    rows = keep_ref.shape[0] // len(refs)
    for i, ref in enumerate(refs):
        part = slice(i * rows, (i + 1) * rows)
        total = keep_ref[part, :].astype(jnp.float32) + arrived_ref[part, :].astype(jnp.float32)
        ref[...] = total.astype(ref.dtype)


def add(keep, arrived, dtypes):
    rows, cols = keep.shape
    count = len(dtypes)
    out = tuple(jax.ShapeDtypeStruct((rows // count, cols), dtype) for dtype in dtypes)
    return pl.pallas_call(
        add_kernel,
        out_shape=out,
        in_specs=whole_vmem(2),
        out_specs=tuple(whole_vmem(count)),
        compiler_params=vmem(16),
        cost_estimate=FREE,
        name="add",
    )(keep, arrived)


def hidden_kernel(*refs, count):
    row_refs = refs[:count]
    gain_ref, gate_ref, up_ref = refs[count : count + 3]
    out_ref = refs[-1]
    ctx_index = lax.axis_index("ctx")
    cols = row_refs[0].shape[1]
    rows = [ref[...].astype(jnp.float32) for ref in row_refs]
    square = sum(jnp.sum(row * row, axis=1, keepdims=True) for row in rows)
    inverse = lax.rsqrt(square / (cols * count) + 1e-06)
    gate = None
    up = None
    for place in range(count):
        at = pl.multiple_of((ctx_index ^ place) * cols, cols)
        normed = (rows[place] * inverse * gain_ref[:, pl.ds(at, cols)]).astype(jnp.bfloat16)
        gate_part = jnp.dot(normed, gate_ref[0, pl.ds(at, cols), :], preferred_element_type=jnp.float32)
        up_part = jnp.dot(normed, up_ref[0, pl.ds(at, cols), :], preferred_element_type=jnp.float32)
        gate = gate_part if gate is None else gate + gate_part
        up = up_part if up is None else up + up_part
    out_ref[...] = (gate / (1.0 + jnp.exp(-gate)) * up).astype(jnp.bfloat16)


def hidden_units(pieces, gain, gate_weight, up_weight, after=()):
    count = len(pieces)
    rows = pieces[0].shape[0]
    units = gate_weight.shape[2]
    return pl.pallas_call(
        functools.partial(hidden_kernel, count=count),
        out_shape=jax.ShapeDtypeStruct((rows, units), jnp.bfloat16),
        in_specs=whole_vmem(count + 3) + anywhere(len(after)),
        out_specs=pl.BlockSpec(memory_space=pltpu.VMEM),
        compiler_params=vmem(20),
        cost_estimate=FREE,
        name="hidden_units",
    )(*pieces, gain, gate_weight, up_weight, *after)


def down_kernel(*refs, count):
    piece_refs = refs[:count]
    down_ref = refs[count]
    out_ref = refs[-1]
    ctx_index = lax.axis_index("ctx")
    units = piece_refs[0].shape[1]
    total = None
    for place in range(count):
        at = pl.multiple_of((ctx_index ^ place) * units, units)
        part = jnp.dot(
            piece_refs[place][...], down_ref[0, pl.ds(at, units), :], preferred_element_type=jnp.float32
        )
        total = part if total is None else total + part
    for home in range(out_ref.shape[0]):
        out_ref[home] = total[home * CAP : (home + 1) * CAP].astype(jnp.bfloat16)


def down_product(pieces, down_weight):
    count = len(pieces)
    rows = pieces[0].shape[0]
    return pl.pallas_call(
        functools.partial(down_kernel, count=count),
        out_shape=jax.ShapeDtypeStruct((rows // CAP, CAP, down_weight.shape[2]), jnp.bfloat16),
        in_specs=whole_vmem(count + 1),
        out_specs=pl.BlockSpec(memory_space=pltpu.VMEM),
        compiler_params=vmem(20),
        cost_estimate=FREE,
        name="down_product",
    )(*pieces, down_weight)


def attended_kernel(*refs, places):
    residual_ref = refs[len(places)]
    out_ref = refs[-1]
    ctx_index = lax.axis_index("ctx")
    for (place, row0), ref in zip(places, refs):
        rows, cols = ref.shape
        at = pl.multiple_of((ctx_index ^ place) * cols, cols)
        total = residual_ref[row0 : row0 + rows, pl.ds(at, cols)].astype(jnp.float32)
        total = total + ref[...].astype(jnp.float32)
        out_ref[row0 : row0 + rows, pl.ds(at, cols)] = total.astype(jnp.bfloat16)


def attended_rows(pieces, places, residual):
    return pl.pallas_call(
        functools.partial(attended_kernel, places=places),
        out_shape=jax.ShapeDtypeStruct(residual.shape, jnp.bfloat16),
        in_specs=whole_vmem(len(pieces) + 1),
        out_specs=pl.BlockSpec(memory_space=pltpu.VMEM),
        compiler_params=vmem(20),
        cost_estimate=FREE,
        name="attended_rows",
    )(*pieces, residual)


def combine_kernel(routes_ref, weights_ref, back_ref, out_ref, *, flight, count):
    routes_t = routes_ref[...]
    scores = weights_ref[...]
    shares = scores / jnp.sum(scores, axis=0, keepdims=True)
    named, ranks = slot_ranks(routes_t, flight)
    lines = []
    for j in range(flight):
        share = jnp.sum(jnp.where(routes_t == j, shares, 0.0), axis=0, keepdims=True)
        for r in range(CAP):
            lines.append(jnp.where(ranks[j : j + 1] == r, share, 0.0))
    lines = jnp.concatenate(lines, axis=0)
    pieces = []
    rest = lines
    for _ in range(3):
        piece = rest.astype(jnp.bfloat16)
        pieces.append(piece.astype(jnp.float32))
        rest = rest - pieces[-1]
    pieces = jnp.concatenate(pieces, axis=0).T.astype(jnp.bfloat16)
    cols = back_ref.shape[2]
    for place in range(count):
        rows = [back_ref[place * flight + j].astype(jnp.float32) for j in range(flight)]
        rows = jnp.concatenate(rows * 3, axis=0).astype(jnp.bfloat16)
        out_ref[:, place * cols : (place + 1) * cols] = jnp.dot(
            pieces, rows, preferred_element_type=jnp.float32
        ).astype(jnp.bfloat16)


def gather_pieces(x, axis):
    count = lax.axis_size(axis)
    found = {0: x}
    step = count // 2
    while step >= 1:
        keys = sorted(found)
        if len(keys) == 1:
            moved = [swap(found[0], axis, step)]
        else:
            packed = swap(jnp.stack([found[k] for k in keys]), axis, step)
            moved = [packed[i] for i in range(len(keys))]
        for k, piece in zip(keys, moved):
            found[k ^ step] = piece
        step //= 2
    return [found[k] for k in range(count)]


def gather_direct(x, axis):
    return [x] + [swap(x, axis, k) for k in range(1, lax.axis_size(axis))]


def after(x, *others):
    return lax.optimization_barrier((x,) + others)[0]


class Sequence:
    def __init__(self):
        self.last = None

    def tie(self, *xs):
        if self.last is None:
            return xs
        return lax.optimization_barrier(xs + (self.last,))[:-1]

    def run(self, step, xs, *rest):
        out = step(*self.tie(*xs), *rest)
        self.last = out[-1] if isinstance(out, (tuple, list)) else out
        return out


    def steps(self, name, *steps):
        operands = self.tie(*[x for step in steps for x in step.operands])
        results = together(name, steps, *operands)
        self.last = results[-1][-1]
        return results


class Gather:
    def __init__(self, sequence, x):
        self.sequence = sequence
        self.found = {0: x}
        self.step = lax.axis_size("ctx") // 2

    def hop(self):
        names = sorted(self.found)
        pieces = self.sequence.tie(*[self.found[k] for k in names])
        for k, piece in zip(names, pieces):
            self.found[k ^ self.step] = swap(piece, "ctx", self.step)
        self.step //= 2

    def wait(self, *others):
        for k in self.found:
            self.found[k] = after(self.found[k], *others)

    def hops_to(self, step):
        while self.step >= step:
            self.hop()

    def pieces(self, names):
        return tuple(self.found[k] for k in names)


class Halving:
    def __init__(self, sequence, keep, send, add_step, step=1):
        self.sequence = sequence
        self.keep = keep
        self.result = None
        self.step = step
        self.add_step = add_step
        self.count = lax.axis_size("exp")
        self.arrived = swap(send, "exp", step)

    def advance(self, hold=False):
        self.step *= 2
        last = self.step >= self.count
        out = self.sequence.run(lambda k, a: self.add_step(k, a, last), (self.keep, self.arrived))
        if last:
            self.result = out
        else:
            self.keep, self.send = out
            if not hold:
                self.release()

    def wait(self, *others):
        self.arrived = after(self.arrived, *others)

    def release(self):
        (send,) = self.sequence.tie(self.send)
        self.arrived = swap(send, "exp", self.step)

    def finish(self):
        while self.step < self.count:
            self.advance()
        return self.result


def shards(
    queries,
    keys,
    values,
    doc_lengths,
    residual_in,
    out_weight,
    norm_gain,
    routes,
    route_weights,
    gate_weight,
    up_weight,
    down_weight,
):
    tokens = queries.shape[0]
    local_heads = queries.shape[1] // HD
    n_ctx = lax.axis_size("ctx")
    homes = lax.axis_size("exp")
    flight = gate_weight.shape[0] * homes
    ctx_index = lax.axis_index("ctx")
    exp_index = lax.axis_index("exp")
    block_tokens = residual_in.shape[0]
    width = residual_in.shape[1]
    cols = out_weight.shape[1]
    halves = 2 if block_tokens % 32 == 0 else 1
    sub = block_tokens // halves
    sequence = Sequence()

    def plain_add(kinds):
        def step(keep, arrived, last):
            return add(keep, arrived, kinds if last else (jnp.float32, jnp.bfloat16))

        return step

    kv_head = exp_index * local_heads // (QH // KVH)
    kv_own = jnp.stack(
        [
            lax.dynamic_slice_in_dim(keys, kv_head * HD, HD, 1),
            lax.dynamic_slice_in_dim(values, kv_head * HD, HD, 1),
        ]
    )
    kv_near = shift(kv_own, "ctx", 1)
    kv_far = shift(kv_own, "ctx", 2)
    q_ready, bias = ready(doc_lengths, after(queries, kv_own))

    routes_all = gather_direct(after(routes.T, kv_own), "exp")
    heads_out = []
    near = []
    far = []
    for half in range(halves):
        if half == halves - 1:
            routes_all = list(sequence.tie(*routes_all))
            (q_ready,) = lax.optimization_barrier((q_ready,) + tuple(routes_all))[:1]
        rows = sequence.run(
            lambda q: attention(q, bias, kv_far, kv_near, kv_own, homes, half, sub), (q_ready,)
        )
        heads_out.append(rows)
        near.append(swap(rows, "ctx", 1))
        far.append(Gather(sequence, rows))

    def leaving(blocks):
        return project(blocks, out_weight, homes, sub, True)

    def staying(blocks):
        return project(blocks, out_weight, homes, sub, False)

    names = [k for k in range(n_ctx) if k > 1]
    one = (jnp.bfloat16,)
    mine = tuple(heads_out)
    near = tuple(near)
    far[0].hops_to(2)
    ((own_send,),) = sequence.steps("leave", leaving(mine))
    ((routed,),) = sequence.steps("pick", pick(residual_in, routes_all, heads_out, sub))
    routed_all = Gather(sequence, routed)
    (near_send,), (own_keep,), (near_keep,) = sequence.steps(
        "leave_and_stay", leaving(near), staying(mine), staying(near)
    )
    own = Halving(sequence, own_keep, own_send, plain_add(one))
    beside = Halving(sequence, near_keep, near_send, plain_add(one))
    own.advance()
    routed_all.hops_to(2)
    beside.advance()
    routed_all.hop()
    far[0].wait(routed_all.found[n_ctx // 2])
    far[0].hop()
    (own_sum,) = own.finish()
    if halves > 1:
        far[1].wait(routed_all.found[n_ctx // 2])
        far[1].hops_to(2)
    (blocks,) = sequence.steps(
        "routed_product", routed_product(routed_all.pieces(range(n_ctx)), out_weight, homes)
    )
    blocks = [blocks[0]] + [swap(blocks[k], "exp", k) for k in range(1, homes)]
    first = far[0].pieces(names)
    (send,), (keep,) = sequence.steps("far", leaving(first), staying(first))
    sums = [Halving(sequence, keep, send, plain_add(one * len(names)))]
    (near_sum,) = beside.finish()
    stream = sequence.run(routed_sum, tuple(blocks))
    stream_rows = gather_direct(stream, "ctx")
    if halves > 1:
        far[1].hop()
        second = far[1].pieces(names)
        second = lax.optimization_barrier(second + tuple(stream_rows))[: len(second)]
        (send,), (keep,) = sequence.steps("far", leaving(second), staying(second))
        sums.append(Halving(sequence, keep, send, plain_add(one * len(names))))
    hidden = sequence.run(
        lambda *xs: hidden_units(xs, norm_gain[None, :], gate_weight, up_weight), tuple(stream_rows)
    )
    hidden_pieces = gather_direct(hidden, "ctx")
    sums[0].advance()
    produced = sequence.run(lambda *xs: down_product(xs, down_weight), tuple(hidden_pieces))
    if halves > 1:
        sums[1].advance()
    (produced,) = sequence.tie(produced)
    back = lax.all_to_all(
        produced,
        ("ctx", "exp"),
        split_axis=0,
        concat_axis=0,
        tiled=True,
    )
    for total in sums:
        total.finish()
    parts = [own_sum, swap(near_sum, "ctx", 1)]
    places = [(0, 0), (1, 0)]

    def combine(back):
        return pl.pallas_call(
            functools.partial(combine_kernel, flight=flight, count=n_ctx),
            out_shape=jax.ShapeDtypeStruct((block_tokens, width), jnp.bfloat16),
            in_specs=whole_vmem(3),
            out_specs=pl.BlockSpec(memory_space=pltpu.VMEM),
            compiler_params=vmem(20),
            cost_estimate=FREE,
            name="combine",
        )(routes.T, route_weights.T, back)

    combined = sequence.run(combine, (back,))
    for half in range(halves):
        for k, piece in zip(names, sums[half].result):
            parts.append(swap(piece, "ctx", k))
            places.append((k, half * sub))
    attended = sequence.run(lambda *xs: attended_rows(xs, places, residual_in), tuple(parts))
    return (attended, combined)


def solution(mesh):
    placed = (
        P(("grp", "ctx"), "exp"),
        P(("grp", "ctx"), None),
        P(("grp", "ctx"), None),
        P("grp"),
        P(("grp", "ctx", "exp"), None),
        P("exp", "ctx"),
        P(),
        P(("grp", "ctx", "exp"), None),
        P(("grp", "ctx", "exp"), None),
        P("exp", None, "ctx"),
        P("exp", None, "ctx"),
        P("exp", None, "ctx"),
    )
    return jax.shard_map(
        shards,
        mesh=mesh,
        in_specs=placed,
        out_specs=(P(("grp", "ctx", "exp"), None), P(("grp", "ctx", "exp"), None)),
        check_vma=False,
    )
```
